128 devices in a mesh: blk: 64 (over y, x_lo, z, core), tower: 2 (over x_hi).
Axes of the slice: x: 4 (x_hi: 2, x_lo: 2; x = x_hi * 2 + x_lo), y: 4, z: 4, core: 2. Of those that a mesh axis runs over, the one named last changes fastest.
Arguments:
- features: bfloat16 [2, 8192, 9216], P('tower', 'blk'), may hold values from -6 to 6
- group: int32 [8192], P('blk'), may hold values from 0 to 1
- pad_mask: int32 [9216], replicated, may hold values from 0 to 1, as said below
- weights: bfloat16 [2, 4096, 9216], P('tower', 'blk'), may hold values from -0.0625 to 0.0625
- bias: float32 [2, 4096], P('tower'), may hold values from -3 to 3
- stitch: float32 [2, 2, 4096], replicated, may hold values from 0.05 to 1.2
- momentum: float32 [2, 4096, 9216], P('tower', 'blk'), may hold values from -96 to 96
- cotangent: bfloat16 [2, 8192, 4096], P('tower', 'blk'), may hold values from -6 to 6
Outputs:
- mixed: bfloat16 [2, 8192, 4096], P('tower', 'blk')
- feat_grad: bfloat16 [2, 8192, 9216], P('tower', 'blk')
- weight_grad: float32 [2, 4096, 9216], P('tower', 'blk')
- bias_grad: float32 [2, 4096], P('tower')
- stitch_grad: float32 [2, 2, 4096], replicated
- new_momentum: float32 [2, 4096, 9216], P('tower', 'blk')
- new_weights: float32 [2, 4096, 9216], P('tower', 'blk')
The draws below stay inside these ranges and needn't reach their ends.
Inputs may be any that keep to these rules, and one draw needn't show every extreme that they name: `pad_mask`: exactly 6400 entries are 1, the rest 0.
All inputs are finite; a program needn't handle non-finite values.
Results may differ from the reference program's by a relative error of at most 0.0055.
Values may be sent and summed in bfloat16 or wider, within the bound.
A program may use at most 448 MiB of HBM per device.

```python
import jax
import jax.numpy as jnp
from jax import lax

FEAT = 9216
OUT = 4096
KEPT = 6400
IMAGES = 8192


def draw_pad_mask(key, part):
    key = jax.random.fold_in(key, 11)
    order = jax.random.permutation(key, FEAT)
    return (order < KEPT).astype(jnp.int32)


def draw_stitch(key, part):
    key = jax.random.fold_in(key, 12)
    first, second = jax.random.split(key)
    diagonal = jax.random.uniform(first, (2, OUT), jnp.float32, 0.6, 1.2)
    across = jax.random.uniform(second, (2, OUT), jnp.float32, 0.05, 0.45)
    return jnp.stack([jnp.stack([diagonal[0], across[0]]), jnp.stack([across[1], diagonal[1]])])


def draw_cotangent(key, part):
    key = jax.random.fold_in(key, 13)
    rows = jnp.arange(IMAGES, dtype=jnp.float32) / IMAGES
    base = jnp.clip(jax.random.normal(key, (2, IMAGES, OUT), jnp.float32), -3.3, 3.3)
    factor = 0.6 * 3.0 ** rows
    return (base * factor[None, :, None]).astype(jnp.bfloat16)


def place_ends(drawn, stream_key, smallest, top_value):
    dims = drawn.shape
    index_at = [jax.random.randint(jax.random.fold_in(stream_key, axis), (), 0, dims[axis]) for axis in range(len(dims))]
    drawn = drawn.at[tuple(index_at)].set(smallest)
    longest = dims.index(max(dims))
    index_at[longest] = (index_at[longest] + 1) % dims[longest]
    return drawn.at[tuple(index_at)].set(top_value)


def block_levels(own_key, extent, shards, least, top_value):
    factor_of = 1.0
    for position, parts in shards:
        heights = jax.random.uniform(jax.random.fold_in(jax.random.fold_in(own_key, 6), position), (parts,), jnp.float32, least / len(shards), top_value / len(shards))
        factor_of = factor_of * jnp.repeat(jnp.exp(heights), extent[position] // parts).reshape((-1,) + (1,) * (len(extent) - 1 - position))
    return factor_of


def noise(key, shape, deviation, reach, pieces=(), kind=jnp.bfloat16):
    loudness = block_levels(key, shape, pieces, -0.22, 0.18) if pieces else 1.0
    values = jax.random.normal(key, shape, jnp.float32) * deviation * loudness
    return jnp.minimum(jnp.maximum(values, -reach), reach).astype(kind)


def setup_inputs(seed: int = 0) -> dict:
    key_list = jax.random.split(jax.random.key(seed), 9)
    features = noise(key_list[0], (2, IMAGES, FEAT), 1.0, 6.0, ((0, 2), (1, 64)))
    group = place_ends(jax.random.randint(key_list[1], (IMAGES,), 0, 2), jax.random.fold_in(key_list[1], 1), 0, 1).astype(jnp.int32)
    pad_mask = draw_pad_mask(jax.random.fold_in(key_list[8], 71), 0)
    weights = noise(key_list[3], (2, OUT, FEAT), FEAT ** -0.5, 0.0625, ((0, 2), (1, 64)))
    bias = noise(key_list[4], (2, OUT), 0.5, 3.0, ((0, 2),), jnp.float32)
    stitch = draw_stitch(jax.random.fold_in(key_list[8], 71), 0)
    momentum = noise(key_list[6], (2, OUT, FEAT), 16.0, 96.0, ((0, 2), (1, 64)), jnp.float32)
    cotangent = draw_cotangent(jax.random.fold_in(key_list[8], 71), 0)
    return dict(features=features, group=group, pad_mask=pad_mask, weights=weights, bias=bias, stitch=stitch, momentum=momentum, cotangent=cotangent)


momentum_rate = 0.9
learn_rate = 0.0001

@jax.custom_vjp
def low(v):
    return lax.optimization_barrier(v.astype(jnp.bfloat16)).astype(jnp.float32)

@jax.custom_vjp
def low_back(v):
    return v

def low_keep(v):
    return (low(v), None)

def low_pass(kept, grad):
    return (grad,)

def back_keep(v):
    return (v, None)

def back_low(kept, grad):
    return (low(grad),)
low.defvjp(low_keep, low_pass)
low_back.defvjp(back_keep, back_low)

def forward(feats, weight_rows, bias, stitch, row_keep):
    masked = feats * row_keep[None]
    pre = jnp.einsum('tbf,tof->tbo', masked, weight_rows, precision=lax.Precision.HIGHEST) + bias[:, None, :]
    pre = low_back(pre)
    hidden = low(jax.nn.silu(pre))
    return stitch[:, 0, None, :] * hidden[0][None] + stitch[:, 1, None, :] * hidden[1][None]

def reference(features, group, pad_mask, weights, bias, stitch, momentum, cotangent):
    row_keep = jnp.where(group[:, None] == 1, pad_mask[None, :], 1).astype(jnp.float32)

    def apply_layer(feats, weight_rows, bias_row, stitch_val):
        return forward(feats, weight_rows, bias_row, stitch_val, row_keep)
    mixed, pullback = jax.vjp(apply_layer, features.astype(jnp.float32), weights.astype(jnp.float32), bias, stitch)
    feat_grad, weight_grad, bias_grad, stitch_grad = pullback(cotangent.astype(jnp.float32))
    new_momentum = momentum_rate * momentum + weight_grad
    new_weights = weights.astype(jnp.float32) - learn_rate * new_momentum
    return (mixed.astype(jnp.bfloat16), feat_grad.astype(jnp.bfloat16), weight_grad, bias_grad, stitch_grad, new_momentum, new_weights)
```

```python
import jax
import jax.numpy as jnp
from jax import lax
from jax.experimental import pallas as pl
from jax.experimental.pallas import tpu as pltpu
from jax.sharding import PartitionSpec as P

momentum_rate = 0.9
learn_rate = 0.0001

FEAT = 9216
OUT = 4096
HALF = FEAT // 2
OWN = 128
ROWS = 64
SPAN = 1024
CUT = 512
CUTS = HALF // CUT
STRIP = 32

KINDS = (
    "x_sib", "w_sib", "cot", "w_x", "own_yp", "own_ym", "own_zp", "own_zm", "fwd_yp", "fwd_ym", "fwd_zp",
    "fwd_zm", "hg", "pre", "pg", "hid", "tow", "opp_yp", "opp_ym", "opp_zp", "opp_zm", "sum_yp", "sum_ym",
    "sum_zp", "sum_zm", "g_x", "d_sib", "g_sib", "v_c", "v_x", "v_z", "v_y", "v_t",
)
KIND = {name: row for row, name in enumerate(KINDS)}
LOCALS = ("x", "w", "cot", "d", "g", "mix", "vec")
LOCAL = {name: row for row, name in enumerate(LOCALS)}


def body(
    masked, weights, cotangent, coef,
    mixed_out, feat_out, grad_out, vec_out,
    xb, wb, pre, pre_in, pg, pgt, cot, cot_in, hg_send, hg, hid_send, hid, hid_other, mix,
    relay_yp, relay_ym, part_yp, part_ym, relay_zp, relay_zm, part_zp, part_zm,
    g_keep, g_send, g_in, bias_sum, vec, vec_c, vec_x, vec_xin, vec_z, vec_y, vec_t,
    send_sem, recv_sem, local_sem,
):
    blk, t = lax.axis_index("blk"), lax.axis_index("tower")
    y, x, z, c = blk // 16, (blk // 8) % 2, (blk // 2) % 4, blk % 2
    other = 1 - c

    def place(y, x, z, c):
        return ((y * 2 + x) * 4 + z) * 2 + c

    yp, yo, ym = (y + 1) % 4, (y + 2) % 4, (y + 3) % 4
    zp, zo, zm = (z + 1) % 4, (z + 2) % 4, (z + 3) % 4
    to_yp, to_yo, to_ym = ((place(v, x, z, c), t) for v in (yp, yo, ym))
    to_zp, to_zo, to_zm = ((place(y, x, v, c), t) for v in (zp, zo, zm))
    to_x = (place(y, 1 - x, z, c), t)
    to_sib = (place(y, x, z, other), t)
    to_tower = (blk, 1 - t)
    to_y = (None, to_yp, to_yo, to_ym)
    to_z = (None, to_zp, to_zo, to_zm)

    def remote(kind, k, src, dst, device):
        return pltpu.make_async_remote_copy(
            src_ref=src, dst_ref=dst,
            send_sem=send_sem.at[KIND[kind], k], recv_sem=recv_sem.at[KIND[kind], k],
            device_id=device, device_id_type=pl.DeviceIdType.MESH,
        )

    def arrived(kind, k, dst):
        remote(kind, k, dst, dst, to_sib).wait_recv()

    def sent(kind, k, src):
        remote(kind, k, src, src, to_sib).wait_send()

    def local(kind, k, src, dst):
        return pltpu.make_async_copy(src, dst, local_sem.at[LOCAL[kind], k])

    def columns(side, k):
        return pl.ds(pl.multiple_of(side * HALF + k * CUT, CUT), CUT)

    def loop(count, step):
        lax.fori_loop(0, count, lambda k, carry: (step(k), carry)[1], 0)

    own_rows = pl.ds(pl.multiple_of(c * ROWS, ROWS), ROWS)
    sib_rows = pl.ds(pl.multiple_of(other * ROWS, ROWS), ROWS)

    def load_x(k):
        return local("x", k, masked.at[:, columns(c, k)], xb.at[k, y, c])

    def load_w(k):
        return local("w", k, weights.at[:, columns(c, k)], wb.at[k, x, z, own_rows])

    def load_cot(j):
        return local("cot", j, cotangent.at[:, pl.ds(j * SPAN, SPAN)], cot.at[j])

    def start_loads(k):
        load_x(k).start()
        load_w(k).start()

    loop(CUTS, start_loads)
    for j in range(4):
        load_cot(j).start()

    barrier = pltpu.get_barrier_semaphore()
    partners = (to_yp, to_yo, to_ym, to_zp, to_zo, to_zm, to_x, to_sib, to_tower)
    for device in partners:
        pl.semaphore_signal(barrier, inc=1, device_id=device, device_id_type=pl.DeviceIdType.MESH)
    pl.semaphore_wait(barrier, len(partners))

    def x_sib(k):
        return remote("x_sib", k, masked.at[:, columns(other, k)], xb.at[k, y, c], to_sib)

    def w_sib(k):
        return remote("w_sib", k, weights.at[:, columns(other, k)], wb.at[k, x, z, own_rows], to_sib)

    def to_sibling(k):
        x_sib(k).start()
        w_sib(k).start()

    loop(CUTS, to_sibling)
    for j in range(4):
        remote("cot", j, cotangent.at[:, pl.ds(j * SPAN, SPAN)], cot_in.at[j], to_tower).start()

    def own_out(k):
        load_x(k).wait()
        arrived("x_sib", k, xb.at[k, y, other])
        remote("own_yp", k, xb.at[k, y], xb.at[k, y], to_yp).start()
        remote("own_ym", k, xb.at[k, y], xb.at[k, y], to_ym).start()
        load_w(k).wait()
        arrived("w_sib", k, wb.at[k, x, z, sib_rows])
        remote("w_x", k, wb.at[k, x, z], wb.at[k, x, z], to_x).start()

    loop(CUTS, own_out)

    def pair_out(k):
        arrived("w_x", k, wb.at[k, 1 - x, z])
        remote("own_zp", k, wb.at[k, :, z], wb.at[k, :, z], to_zp).start()
        remote("own_zm", k, wb.at[k, :, z], wb.at[k, :, z], to_zm).start()

    loop(CUTS, pair_out)

    def forward(k):
        arrived("own_yp", k, xb.at[k, ym])
        remote("fwd_yp", k, xb.at[k, ym, 0], xb.at[k, ym, 0], to_yp).start()
        arrived("own_ym", k, xb.at[k, yp])
        remote("fwd_ym", k, xb.at[k, yp, 1], xb.at[k, yp, 1], to_ym).start()
        arrived("own_zp", k, wb.at[k, :, zm])
        remote("fwd_zp", k, wb.at[k, 0, zm], wb.at[k, 0, zm], to_zp).start()
        arrived("own_zm", k, wb.at[k, :, zp])
        remote("fwd_zm", k, wb.at[k, 1, zp], wb.at[k, 1, zp], to_zm).start()

    loop(CUTS, forward)

    for j in range(4):
        load_cot(j).wait()
        arrived("cot", j, cot_in.at[j])
    for d in range(4):
        j = (y + d) % 4

        def combine(i, d=d, j=j):
            rows = pl.ds(pl.multiple_of(i * STRIP, STRIP), STRIP)
            value = (
                coef[j, 0:1, :] * cot[j, rows, :].astype(jnp.float32)
                + coef[j, 1:2, :] * cot_in[j, rows, :].astype(jnp.float32)
            ).astype(jnp.bfloat16)
            if d == 0:
                hg[y, rows, :] = value
            else:
                hg_send[j, rows, :] = value

        loop(OWN // STRIP, combine)
        if d:
            remote("hg", d, hg_send.at[j], hg.at[y], to_y[d]).start()

    def add_product(k):
        arrived("fwd_yp", k, xb.at[k, yo, 0])
        arrived("fwd_ym", k, xb.at[k, yo, 1])
        arrived("fwd_zp", k, wb.at[k, 0, zo])
        arrived("fwd_zm", k, wb.at[k, 1, zo])

        def block(b):
            product = lax.dot_general(
                xb[k, b].reshape(2 * OWN, CUT), wb[k].reshape(SPAN, CUT),
                (((1,), (1,)), ((), ())), preferred_element_type=jnp.float32,
            ).reshape(2, OWN, SPAN)

            @pl.when(k == 0)
            def _():
                pre[b] = product

            @pl.when(k > 0)
            def _():
                pre[b] += product

        loop(4, block)
        sent("x_sib", k, xb.at[k, y, c])
        sent("w_sib", k, wb.at[k, x, z, own_rows])
        sent("own_yp", k, xb.at[k, y])
        sent("own_ym", k, xb.at[k, y])
        sent("w_x", k, wb.at[k, x, z])
        sent("own_zp", k, wb.at[k, :, z])
        sent("own_zm", k, wb.at[k, :, z])
        sent("fwd_yp", k, xb.at[k, ym, 0])
        sent("fwd_ym", k, xb.at[k, yp, 1])
        sent("fwd_zp", k, wb.at[k, 0, zm])
        sent("fwd_zm", k, wb.at[k, 1, zp])

    loop(CUTS, add_product)

    for d in range(4):
        b = (y + d) % 4
        remote("pre", d, pre.at[b, other], pre_in.at[b], to_sib).start()
    bias_sum[...] = jnp.zeros_like(bias_sum)
    for d in range(4):
        b = (y + d) % 4
        arrived("pre", d, pre_in.at[b])
        if d:
            arrived("hg", 4 - d, hg.at[b])

        def act(i, d=d, b=b):
            rows = pl.ds(pl.multiple_of(i * STRIP, STRIP), STRIP)
            value = pre[b, c, rows, :] + pre_in[b, rows, :] + coef[y, 3:4, :]
            gate = jax.nn.sigmoid(value)
            hidden = (value * gate).astype(jnp.bfloat16)
            grad = (hg[b, rows, :].astype(jnp.float32) * gate * (1.0 + value * (1.0 - gate))).astype(jnp.bfloat16)
            pg[b, c, rows, :] = grad
            if d == 0:
                hid[y, rows, :] = hidden
            else:
                hid_send[b, rows, :] = hidden
            bias_sum[...] += jnp.sum(grad.astype(jnp.float32).reshape(STRIP // 8, 8, SPAN), 0)

        loop(OWN // STRIP, act)
        remote("pg", d, pg.at[b, c], pg.at[b, c], to_sib).start()
        if d:
            remote("hid", d, hid_send.at[b], hid.at[y], to_y[d]).start()
    for d in range(4):
        arrived("pg", d, pg.at[(y + d) % 4, other])

    wide = 256
    eye = (
        lax.broadcasted_iota(jnp.int32, (wide, wide), 0) == lax.broadcasted_iota(jnp.int32, (wide, wide), 1)
    ).astype(jnp.bfloat16)
    for o in range(SPAN // wide):
        pgt[o * wide : (o + 1) * wide, :] = lax.dot_general(
            eye, pg[:, :, :, o * wide : (o + 1) * wide].reshape(SPAN, wide),
            (((1,), (1,)), ((), ())), preferred_element_type=jnp.float32,
        ).astype(jnp.bfloat16)

    def slot(k):
        return (k + CUTS) % (CUTS + 1)

    def products(k):
        s = slot(k)

        def block_g(o):
            product = jnp.dot(
                pgt[pl.ds(pl.multiple_of(o * 256, 256), 256), :], xb[k].reshape(SPAN, CUT),
                preferred_element_type=jnp.float32,
            )
            wb[s, o // 2, pl.ds((o % 2) * 2, 2)] = product.astype(jnp.bfloat16).reshape(2, OWN, CUT)

        def block_d(b):
            product = jnp.dot(
                pg[b].reshape(2 * OWN, SPAN), wb[k].reshape(SPAN, CUT), preferred_element_type=jnp.float32
            )
            xb[k, b] = product.astype(jnp.bfloat16).reshape(2, OWN, CUT)

        loop(4, block_g)
        loop(4, block_d)
        remote("opp_yp", k, xb.at[k, yo, 0], relay_yp.at[k], to_yp).start()
        remote("opp_ym", k, xb.at[k, yo, 1], relay_ym.at[k], to_ym).start()
        remote("opp_zp", k, wb.at[s, 0, zo], relay_zp.at[k], to_zp).start()
        remote("opp_zm", k, wb.at[s, 1, zo], relay_zm.at[k], to_zm).start()

    def wide_sum(*terms):
        total = terms[0].astype(jnp.float32)
        for term in terms[1:]:
            total += term.astype(jnp.float32)
        return total

    def relays(k):
        s = slot(k)
        arrived("opp_yp", k, relay_yp.at[k])
        xb[k, yp, 0] = wide_sum(xb[k, yp, 0], relay_yp[k]).astype(jnp.bfloat16)
        remote("sum_yp", k, xb.at[k, yp], part_yp.at[k], to_yp).start()
        arrived("opp_ym", k, relay_ym.at[k])
        xb[k, ym, 1] = wide_sum(xb[k, ym, 1], relay_ym[k]).astype(jnp.bfloat16)
        remote("sum_ym", k, xb.at[k, ym], part_ym.at[k], to_ym).start()
        arrived("opp_zp", k, relay_zp.at[k])
        wb[s, 0, zp] = wide_sum(wb[s, 0, zp], relay_zp[k]).astype(jnp.bfloat16)
        remote("sum_zp", k, wb.at[s, :, zp], part_zp.at[k], to_zp).start()
        arrived("opp_zm", k, relay_zm.at[k])
        wb[s, 1, zm] = wide_sum(wb[s, 1, zm], relay_zm[k]).astype(jnp.bfloat16)
        remote("sum_zm", k, wb.at[s, :, zm], part_zm.at[k], to_zm).start()

    def d_own(k):
        return local("d", k, xb.at[k, y, c], feat_out.at[:, columns(c, k)])

    def d_sib(k):
        return remote("d_sib", k, xb.at[k, y, other], feat_out.at[:, columns(c, k)], to_sib)

    def g_own(k):
        return local("g", k, g_keep.at[k, own_rows], grad_out.at[:, columns(c, k)])

    def g_sib(k):
        return remote("g_sib", k, g_keep.at[k, sib_rows], grad_out.at[:, columns(c, k)], to_sib)

    def sums(k):
        s = slot(k)
        arrived("sum_zp", k, part_zp.at[k])
        arrived("sum_zm", k, part_zm.at[k])
        g_send[k] = wide_sum(wb[s, 1 - x, z], part_zp[k, 1 - x], part_zm[k, 1 - x]).astype(jnp.bfloat16)
        remote("g_x", k, g_send.at[k], g_in.at[k], to_x).start()
        g_keep[k] = wide_sum(wb[s, x, z], part_zp[k, x], part_zm[k, x])
        arrived("sum_yp", k, part_yp.at[k])
        arrived("sum_ym", k, part_ym.at[k])
        xb[k, y] = wide_sum(xb[k, y], part_yp[k], part_ym[k]).astype(jnp.bfloat16)
        d_own(k).start()
        d_sib(k).start()

    def ends(k):
        arrived("g_x", k, g_in.at[k])
        g_keep[k] += g_in[k].astype(jnp.float32)
        g_own(k).start()
        g_sib(k).start()

    def hidden_over():
        for d in range(1, 4):
            arrived("hid", d, hid.at[(y + 4 - d) % 4])
        for j in range(4):
            remote("tow", j, hid.at[j], hid_other.at[j], to_tower).start()

    def mixing():
        for j in range(4):
            arrived("tow", j, hid_other.at[j])

            def strip(i, sums, j=j):
                rows = pl.ds(pl.multiple_of(i * STRIP, STRIP), STRIP)
                here = hid[j, rows, :].astype(jnp.float32)
                there = hid_other[j, rows, :].astype(jnp.float32)
                mix[j, rows, :] = (coef[j, 0:1, :] * here + coef[j, 2:3, :] * there).astype(jnp.bfloat16)
                up = cot[j, rows, :].astype(jnp.float32)
                return (
                    sums[0] + jnp.sum((up * here).reshape(STRIP // 8, 8, SPAN), 0),
                    sums[1] + jnp.sum((up * there).reshape(STRIP // 8, 8, SPAN), 0),
                )

            zero = jnp.zeros((8, SPAN), jnp.float32)
            here, there = lax.fori_loop(0, OWN // STRIP, strip, (zero, zero))
            here, there = jnp.sum(here, 0, keepdims=True), jnp.sum(there, 0, keepdims=True)
            vec[j : j + 1, :] = jnp.where(t == 0, here, there)
            vec[4 + j : 5 + j, :] = jnp.where(t == 0, there, here)
            local("mix", j, mix.at[j], mixed_out.at[:, pl.ds(j * SPAN, SPAN)]).start()
        bias = jnp.sum(bias_sum[...], 0, keepdims=True)
        vec[8:16, :] = jnp.where(lax.broadcasted_iota(jnp.int32, (8, SPAN), 0) == y, bias, 0.0)
        remote("v_c", 0, vec, vec_c, to_sib).start()

    def over_cores():
        arrived("v_c", 0, vec_c)
        vec_x[...] = vec[...] + vec_c[...]
        remote("v_x", 0, vec_x, vec_xin, to_x).start()

    def over_x():
        arrived("v_x", 0, vec_xin)
        vec_z[z] = vec_x[...] + vec_xin[...]
        for d in range(1, 4):
            remote("v_z", d, vec_z.at[z], vec_z.at[z], to_z[d]).start()

    def over_z():
        for d in range(1, 4):
            arrived("v_z", d, vec_z.at[(z + 4 - d) % 4])
        vec_y[y] = (vec_z[0] + vec_z[1]) + (vec_z[2] + vec_z[3])
        for d in range(1, 4):
            remote("v_y", d, vec_y.at[y], vec_y.at[y], to_y[d]).start()

    def over_y():
        for d in range(1, 4):
            arrived("v_y", d, vec_y.at[(y + 4 - d) % 4])
        vec_t[t] = (vec_y[0] + vec_y[1]) + (vec_y[2] + vec_y[3])
        remote("v_t", 0, vec_t.at[t], vec_t.at[t], to_tower).start()

    between = {1: hidden_over, 3: mixing, 4: over_cores, 5: over_x, 6: over_z, 7: over_y}

    def step(s):
        pl.when(s < CUTS)(lambda: products(s))
        pl.when((s >= 1) & (s < CUTS + 1))(lambda: relays(s - 1))
        pl.when((s >= 2) & (s < CUTS + 2))(lambda: sums(s - 2))
        pl.when(s >= 3)(lambda: ends(s - 3))
        for at, task in between.items():
            pl.when(s == at)(task)

    loop(CUTS + 3, step)

    arrived("v_t", 0, vec_t.at[1 - t])
    pltpu.make_async_copy(vec_t, vec_out, local_sem.at[LOCAL["vec"], 0]).start()

    def finish(k):
        s = slot(k)
        sent("opp_yp", k, xb.at[k, yo, 0])
        sent("opp_ym", k, xb.at[k, yo, 1])
        sent("opp_zp", k, wb.at[s, 0, zo])
        sent("opp_zm", k, wb.at[s, 1, zo])
        sent("sum_yp", k, xb.at[k, yp])
        sent("sum_ym", k, xb.at[k, ym])
        sent("sum_zp", k, wb.at[s, :, zp])
        sent("sum_zm", k, wb.at[s, :, zm])
        sent("g_x", k, g_send.at[k])
        d_own(k).wait()
        d_sib(k).wait_send()
        arrived("d_sib", k, feat_out.at[:, columns(other, k)])
        g_own(k).wait()
        g_sib(k).wait_send()
        arrived("g_sib", k, grad_out.at[:, columns(other, k)])

    loop(CUTS, finish)
    for j in range(4):
        sent("cot", j, cot.at[j])
        sent("pre", j, pre.at[j, other])
        sent("pg", j, pg.at[j, c])
        sent("tow", j, hid.at[j])
        local("mix", j, mix.at[j], mixed_out.at[:, pl.ds(j * SPAN, SPAN)]).wait()
    for d in range(1, 4):
        sent("hg", d, hg_send.at[(y + d) % 4])
        sent("hid", d, hid_send.at[(y + d) % 4])
        sent("v_z", d, vec_z.at[z])
        sent("v_y", d, vec_y.at[y])
    sent("v_c", 0, vec)
    sent("v_x", 0, vec_x)
    sent("v_t", 0, vec_t.at[t])
    pltpu.make_async_copy(vec_t, vec_out, local_sem.at[LOCAL["vec"], 0]).wait()


def towers(masked, weights, cotangent, coef):
    low, wide = jnp.bfloat16, jnp.float32
    scratch = [
        ((CUTS, 4, 2, OWN, CUT), low),
        ((CUTS + 1, 2, 4, OWN, CUT), low),
        ((4, 2, OWN, SPAN), wide),
        ((4, OWN, SPAN), wide),
        ((4, 2, OWN, SPAN), low),
        ((SPAN, SPAN), low),
        ((4, OWN, SPAN), low),
        ((4, OWN, SPAN), low),
        ((4, OWN, SPAN), low),
        ((4, OWN, SPAN), low),
        ((4, OWN, SPAN), low),
        ((4, OWN, SPAN), low),
        ((4, OWN, SPAN), low),
        ((4, OWN, SPAN), low),
        ((CUTS, OWN, CUT), low),
        ((CUTS, OWN, CUT), low),
        ((CUTS, 2, OWN, CUT), low),
        ((CUTS, 2, OWN, CUT), low),
        ((CUTS, OWN, CUT), low),
        ((CUTS, OWN, CUT), low),
        ((CUTS, 2, OWN, CUT), low),
        ((CUTS, 2, OWN, CUT), low),
        ((CUTS, OWN, CUT), wide),
        ((CUTS, OWN, CUT), low),
        ((CUTS, OWN, CUT), low),
        ((8, SPAN), wide),
        ((16, SPAN), wide),
        ((16, SPAN), wide),
        ((16, SPAN), wide),
        ((16, SPAN), wide),
        ((4, 16, SPAN), wide),
        ((4, 16, SPAN), wide),
        ((2, 16, SPAN), wide),
    ]
    anywhere = pl.BlockSpec(memory_space=pl.ANY)
    return pl.pallas_call(
        body,
        out_shape=[
            jax.ShapeDtypeStruct((OWN, OUT), low),
            jax.ShapeDtypeStruct((OWN, FEAT), low),
            jax.ShapeDtypeStruct((ROWS, FEAT), wide),
            jax.ShapeDtypeStruct((2, 16, SPAN), wide),
        ],
        in_specs=[anywhere, anywhere, anywhere, pl.BlockSpec(memory_space=pltpu.VMEM)],
        out_specs=[anywhere] * 4,
        scratch_shapes=[pltpu.VMEM(shape, kind) for shape, kind in scratch]
        + [
            pltpu.SemaphoreType.DMA((len(KINDS), CUTS)),
            pltpu.SemaphoreType.DMA((len(KINDS), CUTS)),
            pltpu.SemaphoreType.DMA((len(LOCALS), CUTS)),
        ],
        compiler_params=pltpu.CompilerParams(
            collective_id=0, has_side_effects=True, vmem_limit_bytes=62 * 1024 * 1024
        ),
    )(masked, weights, cotangent, coef)


def shards(features, group, pad_mask, weights, bias, stitch, momentum, cotangent):
    t = lax.axis_index("tower")
    keep_rows = jnp.where(group[:, None] == 1, pad_mask[None, :], 1).astype(jnp.bfloat16)
    masked = features[0] * keep_rows
    own = jnp.where(t == 0, stitch[0, 0], stitch[1, 1])
    below = jnp.where(t == 0, stitch[1, 0], stitch[0, 1])
    beside = jnp.where(t == 0, stitch[0, 1], stitch[1, 0])
    coef = jnp.stack([own, below, beside, bias[0]]).reshape(4, 4, SPAN).transpose(1, 0, 2)
    mixed, feat_sum, weight_grad, vectors = towers(masked, weights[0], cotangent[0], coef)
    feat_grad = feat_sum * keep_rows
    weight_grad = weight_grad[None]
    new_momentum = momentum_rate * momentum + weight_grad
    new_weights = weights.astype(jnp.float32) - learn_rate * new_momentum
    stitch_grad = vectors[:, :8].reshape(2, 2, OUT)
    bias_grad = lax.dynamic_index_in_dim(vectors, t, 0, keepdims=False)[8:12].reshape(1, OUT)
    return (mixed[None], feat_grad[None], weight_grad, bias_grad, stitch_grad, new_momentum, new_weights)


def solution(mesh):
    placed = (
        P("tower", "blk", None),
        P("blk"),
        P(),
        P("tower", "blk", None),
        P("tower", None),
        P(),
        P("tower", "blk", None),
        P("tower", "blk", None),
    )
    return jax.shard_map(
        shards,
        mesh=mesh,
        in_specs=placed,
        out_specs=(
            P("tower", "blk", None),
            P("tower", "blk", None),
            P("tower", "blk", None),
            P("tower", None),
            P(),
            P("tower", "blk", None),
            P("tower", "blk", None),
        ),
        check_vma=False,
    )
```

```python
import jax
import jax.numpy as jnp
from jax import lax
from jax.experimental import pallas as pl
from jax.experimental.pallas import tpu as pltpu
from jax.sharding import PartitionSpec as P

momentum_rate = 0.9
learn_rate = 0.0001

FEAT = 9216
OUT = 4096
HALF = FEAT // 2
OWN = 128
ROWS = 64
SPAN = 1024
CUT = 512
CUTS = HALF // CUT
STRIP = 32
ORDER = (2, 1, 3, 0)

KINDS = (
    "keep", "x_sib", "w_sib", "cot", "w_x", "own_yp", "own_ym", "own_zp", "own_zm", "pair_zp", "pair_zm",
    "fwd_yp", "fwd_ym", "fwd_zp", "fwd_zm", "hg", "pre", "pg", "hid", "tow", "opp_yp", "opp_ym", "opp_zp",
    "opp_zm", "sum_yp", "sum_ym", "sum_zp", "sum_zm", "g_x", "d_sib", "g_sib", "v_c", "v_x", "v_z", "v_y", "v_t",
)
KIND = {name: row for row, name in enumerate(KINDS)}
LOCALS = ("x", "x_other", "w", "cot", "d", "g", "mix")
LOCAL = {name: row for row, name in enumerate(LOCALS)}


def body(
    features, weights, cotangent, group, pad, stitch, bias,
    mixed_out, feat_out, grad_out, stitch_out, bias_out,
    xb, wb, pre, pre_in, pg, pgt, cot, cot_in, hg_send, hg, hid_send, hid, hid_other, d_opp, g_opp,
    relay_yp, relay_ym, part_yp, part_ym, relay_zp, relay_zm, part_zp, part_zm,
    g_send, g_in, grouped, coef, bias_sum, vec, vec_c, vec_x, vec_xin, vec_z, vec_y, vec_t,
    send_sem, recv_sem, local_sem,
):
    blk, t = lax.axis_index("blk"), lax.axis_index("tower")
    y, x, z, c = blk // 16, (blk // 8) % 2, (blk // 2) % 4, blk % 2
    other = 1 - c

    def place(y, x, z, c):
        return ((y * 2 + x) * 4 + z) * 2 + c

    yp, yo, ym = (y + 1) % 4, (y + 2) % 4, (y + 3) % 4
    zp, zo, zm = (z + 1) % 4, (z + 2) % 4, (z + 3) % 4
    to_yp, to_yo, to_ym = ((place(v, x, z, c), t) for v in (yp, yo, ym))
    to_zp, to_zo, to_zm = ((place(y, x, v, c), t) for v in (zp, zo, zm))
    to_x = (place(y, 1 - x, z, c), t)
    to_sib = (place(y, x, z, other), t)
    to_tower = (blk, 1 - t)
    to_y = (None, to_yp, to_yo, to_ym)
    to_z = (None, to_zp, to_zo, to_zm)

    def remote(kind, k, src, dst, device):
        return pltpu.make_async_remote_copy(
            src_ref=src, dst_ref=dst,
            send_sem=send_sem.at[KIND[kind], k], recv_sem=recv_sem.at[KIND[kind], k],
            device_id=device, device_id_type=pl.DeviceIdType.MESH,
        )

    def arrived(kind, k, dst):
        remote(kind, k, dst, dst, to_sib).wait_recv()

    def sent(kind, k, src):
        remote(kind, k, src, src, to_sib).wait_send()

    def local(kind, k, src, dst):
        return pltpu.make_async_copy(src, dst, local_sem.at[LOCAL[kind], k])

    def columns(side, k):
        return pl.ds(pl.multiple_of(side * HALF + k * CUT, CUT), CUT)

    def loop(count, step):
        lax.fori_loop(0, count, lambda k, carry: (step(k), carry)[1], 0)

    staged = g_send
    own_rows = pl.ds(pl.multiple_of(c * ROWS, ROWS), ROWS)
    sib_rows = pl.ds(pl.multiple_of(other * ROWS, ROWS), ROWS)

    def load_x(k):
        return local("x", k, features.at[:, columns(c, k)], xb.at[k, y, c])

    def load_other(k):
        return local("x_other", k, features.at[:, columns(other, k)], staged.at[k])

    def load_w(k):
        return local("w", k, weights.at[:, columns(c, k)], wb.at[k, x, z, own_rows])

    def load_cot(j):
        return local("cot", j, cotangent.at[:, pl.ds(j * SPAN, SPAN)], cot.at[j])

    def start_loads(k):
        load_x(k).start()
        load_other(k).start()
        load_w(k).start()

    loop(CUTS, start_loads)
    for j in range(4):
        load_cot(j).start()
    grouped[c] = jnp.broadcast_to(group[...].astype(jnp.float32), (OWN, OWN)).T
    for j in range(4):
        part = slice(j * SPAN, (j + 1) * SPAN)
        coef[j, 0:1, :] = jnp.where(t == 0, stitch[0, 0:1, part], stitch[1, 1:2, part])
        coef[j, 1:2, :] = jnp.where(t == 0, stitch[1, 0:1, part], stitch[0, 1:2, part])
        coef[j, 2:3, :] = jnp.where(t == 0, stitch[0, 1:2, part], stitch[1, 0:1, part])
        coef[j, 3:4, :] = bias[0:1, part]

    def kept(value, core, side, k):
        lane = pad[0:1, columns(side, k)].astype(jnp.float32)
        rows = jnp.concatenate([grouped[core]] * (CUT // OWN), 1)
        return jnp.where((rows > 0.5) & (lane < 0.5), 0.0, value)

    barrier = pltpu.get_barrier_semaphore()
    partners = (to_yp, to_yo, to_ym, to_zp, to_zo, to_zm, to_x, to_sib, to_tower)
    for device in partners:
        pl.semaphore_signal(barrier, inc=1, device_id=device, device_id_type=pl.DeviceIdType.MESH)
    pl.semaphore_wait(barrier, len(partners))

    remote("keep", 0, grouped.at[c], grouped.at[c], to_sib).start()

    def x_sib(k):
        return remote("x_sib", k, staged.at[k], xb.at[k, y, c], to_sib)

    def w_sib(k):
        return remote("w_sib", k, weights.at[:, columns(other, k)], wb.at[k, x, z, own_rows], to_sib)

    def to_sibling(k):
        w_sib(k).start()
        load_other(k).wait()
        staged[k] = kept(staged[k].astype(jnp.float32), c, other, k).astype(jnp.bfloat16)
        x_sib(k).start()
        load_x(k).wait()
        xb[k, y, c] = kept(xb[k, y, c].astype(jnp.float32), c, c, k).astype(jnp.bfloat16)

    loop(CUTS, to_sibling)

    def own_out(k):
        arrived("x_sib", k, xb.at[k, y, other])
        remote("own_yp", k, xb.at[k, y], xb.at[k, y], to_yp).start()
        remote("own_ym", k, xb.at[k, y], xb.at[k, y], to_ym).start()
        load_w(k).wait()
        arrived("w_sib", k, wb.at[k, x, z, sib_rows])
        remote("w_x", k, wb.at[k, x, z], wb.at[k, x, z], to_x).start()
        remote("own_zp", k, wb.at[k, x, z], wb.at[k, x, z], to_zp).start()
        remote("own_zm", k, wb.at[k, x, z], wb.at[k, x, z], to_zm).start()

    loop(CUTS, own_out)
    for j in range(4):
        remote("cot", j, cotangent.at[:, pl.ds(j * SPAN, SPAN)], cot_in.at[j], to_tower).start()

    def pair_out(k):
        arrived("w_x", k, wb.at[k, 1 - x, z])
        remote("pair_zp", k, wb.at[k, 1 - x, z], wb.at[k, 1 - x, z], to_zp).start()
        remote("pair_zm", k, wb.at[k, 1 - x, z], wb.at[k, 1 - x, z], to_zm).start()

    loop(CUTS, pair_out)

    def forward(k):
        arrived("own_yp", k, xb.at[k, ym])
        remote("fwd_yp", k, xb.at[k, ym, 0], xb.at[k, ym, 0], to_yp).start()
        arrived("own_ym", k, xb.at[k, yp])
        remote("fwd_ym", k, xb.at[k, yp, 1], xb.at[k, yp, 1], to_ym).start()
        arrived("own_zp", k, wb.at[k, x, zm])
        remote("fwd_zp", k, wb.at[k, x, zm], wb.at[k, x, zm], to_zp).start()
        arrived("own_zm", k, wb.at[k, x, zp])
        arrived("pair_zp", k, wb.at[k, 1 - x, zm])
        arrived("pair_zm", k, wb.at[k, 1 - x, zp])
        remote("fwd_zm", k, wb.at[k, 1 - x, zp], wb.at[k, 1 - x, zp], to_zm).start()

    loop(CUTS, forward)

    for j in range(4):
        load_cot(j).wait()
        arrived("cot", j, cot_in.at[j])
    for d in ORDER:
        j = (y + d) % 4

        def combine(i, d=d, j=j):
            rows = pl.ds(pl.multiple_of(i * STRIP, STRIP), STRIP)
            value = (
                coef[j, 0:1, :] * cot[j, rows, :].astype(jnp.float32)
                + coef[j, 1:2, :] * cot_in[j, rows, :].astype(jnp.float32)
            ).astype(jnp.bfloat16)
            if d == 0:
                hg[y, rows, :] = value
            else:
                hg_send[j, rows, :] = value

        loop(OWN // STRIP, combine)
        if d:
            remote("hg", d, hg_send.at[j], hg.at[y], to_y[d]).start()

    def gathered(k):
        arrived("fwd_yp", k, xb.at[k, yo, 0])
        arrived("fwd_ym", k, xb.at[k, yo, 1])
        arrived("fwd_zp", k, wb.at[k, x, zo])
        arrived("fwd_zm", k, wb.at[k, 1 - x, zo])

    def add_block(k, b):
        pre[b] += lax.dot_general(
            xb[k, b].reshape(2 * OWN, CUT), wb[k].reshape(SPAN, CUT),
            (((1,), (1,)), ((), ())), preferred_element_type=jnp.float32,
        ).reshape(2, OWN, SPAN)

    def add_product(k):
        gathered(k)
        loop(4, lambda b: add_block(k, b))

    def clear(b):
        pre[b] = jnp.zeros((2, OWN, SPAN), jnp.float32)

    loop(4, clear)
    loop(CUTS - 1, add_product)
    gathered(CUTS - 1)

    for d in ORDER:
        b = (y + d) % 4
        add_block(CUTS - 1, b)
        remote("pre", d, pre.at[b, other], pre_in.at[b], to_sib).start()
    bias_sum[...] = jnp.zeros_like(bias_sum)

    def activate(d):
        b = (y + d) % 4
        arrived("pre", d, pre_in.at[b])
        if d:
            arrived("hg", 4 - d, hg.at[b])

        def act(i):
            rows = pl.ds(pl.multiple_of(i * STRIP, STRIP), STRIP)
            value = pre[b, c, rows, :] + pre_in[b, rows, :] + coef[y, 3:4, :]
            gate = jax.nn.sigmoid(value)
            hidden = (value * gate).astype(jnp.bfloat16)
            grad = (hg[b, rows, :].astype(jnp.float32) * gate * (1.0 + value * (1.0 - gate))).astype(jnp.bfloat16)
            pg[b, c, rows, :] = grad
            if d == 0:
                hid[y, rows, :] = hidden
            else:
                hid_send[b, rows, :] = hidden
            bias_sum[...] += jnp.sum(grad.astype(jnp.float32).reshape(STRIP // 8, 8, SPAN), 0)

        loop(OWN // STRIP, act)
        remote("pg", d, pg.at[b, c], pg.at[b, c], to_sib).start()
        if d:
            remote("hid", d, hid_send.at[b], hid.at[y], to_y[d]).start()

    def product_d(k, b):
        product = jnp.dot(
            pg[b].reshape(2 * OWN, SPAN), wb[k].reshape(SPAN, CUT), preferred_element_type=jnp.float32
        )
        return product.astype(jnp.bfloat16).reshape(2, OWN, CUT)

    def product_g(k, v):
        product = jnp.dot(
            pgt[:, v].reshape(2 * OWN, SPAN), xb[k].reshape(SPAN, CUT), preferred_element_type=jnp.float32
        )
        return product.astype(jnp.bfloat16).reshape(2, OWN, CUT)

    def opposite_d(k):
        d_opp[k] = product_d(k, yo)
        remote("opp_yp", k, d_opp.at[k, 0], relay_yp.at[k], to_yp).start()
        remote("opp_ym", k, d_opp.at[k, 1], relay_ym.at[k], to_ym).start()

    def opposite_g(k):
        g_opp[k] = product_g(k, zo)
        remote("opp_zp", k, g_opp.at[k, 0], relay_zp.at[k], to_zp).start()
        remote("opp_zm", k, g_opp.at[k, 1], relay_zm.at[k], to_zm).start()

    activate(2)
    activate(1)
    arrived("pg", 2, pg.at[yo, other])
    loop(CUTS, opposite_d)
    activate(3)
    activate(0)
    for d in (1, 3, 0):
        arrived("pg", d, pg.at[(y + d) % 4, other])

    wide = 256
    eye = (
        lax.broadcasted_iota(jnp.int32, (wide, wide), 0) == lax.broadcasted_iota(jnp.int32, (wide, wide), 1)
    ).astype(jnp.bfloat16)
    for o in range(SPAN // wide):
        flipped = lax.dot_general(
            eye, pg[:, :, :, o * wide : (o + 1) * wide].reshape(SPAN, wide),
            (((1,), (1,)), ((), ())), preferred_element_type=jnp.float32,
        )
        pgt[o // 2, (o % 2) * 2 : (o % 2) * 2 + 2] = flipped.astype(jnp.bfloat16).reshape(2, OWN, SPAN)
    loop(CUTS, opposite_g)

    def left(k):
        sent("x_sib", k, staged.at[k])
        sent("w_sib", k, wb.at[k, x, z, own_rows])
        sent("own_yp", k, xb.at[k, y])
        sent("own_ym", k, xb.at[k, y])
        sent("w_x", k, wb.at[k, x, z])
        sent("own_zp", k, wb.at[k, x, z])
        sent("own_zm", k, wb.at[k, x, z])
        sent("pair_zp", k, wb.at[k, 1 - x, z])
        sent("pair_zm", k, wb.at[k, 1 - x, z])
        sent("fwd_yp", k, xb.at[k, ym, 0])
        sent("fwd_ym", k, xb.at[k, yp, 1])
        sent("fwd_zp", k, wb.at[k, x, zm])
        sent("fwd_zm", k, wb.at[k, 1 - x, zp])

    loop(CUTS, left)
    for d in range(4):
        sent("pre", d, pre.at[d, other])
        if d:
            sent("hg", d, hg_send.at[(y + d) % 4])
    arrived("keep", 0, grouped.at[other])
    mix = hg_send

    def slot(k):
        return (k + CUTS) % (CUTS + 1)

    def g_keep(k):
        part = pl.ds(pl.multiple_of((k % (SPAN // CUT)) * CUT, CUT), CUT)
        block = k // (SPAN // CUT)
        return pre.at[block // 2, block % 2, :, part]

    def products(k):
        s = slot(k)

        def block_g(i):
            v = (zo + 1 + i) % 4
            wb[s, :, v] = product_g(k, v)

        def block_d(i):
            b = (yo + 1 + i) % 4
            xb[k, b] = product_d(k, b)

        loop(3, block_g)
        loop(3, block_d)

    def wide_sum(*terms):
        total = terms[0].astype(jnp.float32)
        for term in terms[1:]:
            total += term.astype(jnp.float32)
        return total

    def relays(k):
        s = slot(k)
        arrived("opp_yp", k, relay_yp.at[k])
        xb[k, yp, 0] = wide_sum(xb[k, yp, 0], relay_yp[k]).astype(jnp.bfloat16)
        remote("sum_yp", k, xb.at[k, yp], part_yp.at[k], to_yp).start()
        arrived("opp_ym", k, relay_ym.at[k])
        xb[k, ym, 1] = wide_sum(xb[k, ym, 1], relay_ym[k]).astype(jnp.bfloat16)
        remote("sum_ym", k, xb.at[k, ym], part_ym.at[k], to_ym).start()
        arrived("opp_zp", k, relay_zp.at[k])
        wb[s, 0, zp] = wide_sum(wb[s, 0, zp], relay_zp[k]).astype(jnp.bfloat16)
        remote("sum_zp", k, wb.at[s, :, zp], part_zp.at[k], to_zp).start()
        arrived("opp_zm", k, relay_zm.at[k])
        wb[s, 1, zm] = wide_sum(wb[s, 1, zm], relay_zm[k]).astype(jnp.bfloat16)
        remote("sum_zm", k, wb.at[s, :, zm], part_zm.at[k], to_zm).start()

    def d_own(k):
        return local("d", k, xb.at[k, y, c], feat_out.at[:, columns(c, k)])

    def d_sib(k):
        return remote("d_sib", k, xb.at[k, y, other], feat_out.at[:, columns(c, k)], to_sib)

    def g_own(k):
        return local("g", k, g_keep(k).at[own_rows], grad_out.at[:, columns(c, k)])

    def g_sib(k):
        return remote("g_sib", k, g_keep(k).at[sib_rows], grad_out.at[:, columns(c, k)], to_sib)

    def sums(k):
        s = slot(k)
        arrived("sum_zp", k, part_zp.at[k])
        arrived("sum_zm", k, part_zm.at[k])
        g_send[k] = wide_sum(wb[s, 1 - x, z], part_zp[k, 1 - x], part_zm[k, 1 - x]).astype(jnp.bfloat16)
        remote("g_x", k, g_send.at[k], g_in.at[k], to_x).start()
        g_keep(k)[...] = wide_sum(wb[s, x, z], part_zp[k, x], part_zm[k, x])
        arrived("sum_yp", k, part_yp.at[k])
        arrived("sum_ym", k, part_ym.at[k])
        for core in range(2):
            total = wide_sum(xb[k, y, core], part_yp[k, core], part_ym[k, core])
            xb[k, y, core] = kept(total, core, c, k).astype(jnp.bfloat16)
        d_own(k).start()
        d_sib(k).start()

    def ends(k):
        arrived("g_x", k, g_in.at[k])
        g_keep(k)[...] += g_in[k].astype(jnp.float32)
        g_own(k).start()
        g_sib(k).start()

    def hidden_over():
        for d in range(1, 4):
            arrived("hid", d, hid.at[(y + 4 - d) % 4])
        for j in range(4):
            remote("tow", j, hid.at[j], hid_other.at[j], to_tower).start()

    def mixing():
        for j in range(4):
            arrived("tow", j, hid_other.at[j])

            def strip(i, sums, j=j):
                rows = pl.ds(pl.multiple_of(i * STRIP, STRIP), STRIP)
                here = hid[j, rows, :].astype(jnp.float32)
                there = hid_other[j, rows, :].astype(jnp.float32)
                mix[j, rows, :] = (coef[j, 0:1, :] * here + coef[j, 2:3, :] * there).astype(jnp.bfloat16)
                up = cot[j, rows, :].astype(jnp.float32)
                return (
                    sums[0] + jnp.sum((up * here).reshape(STRIP // 8, 8, SPAN), 0),
                    sums[1] + jnp.sum((up * there).reshape(STRIP // 8, 8, SPAN), 0),
                )

            zero = jnp.zeros((8, SPAN), jnp.float32)
            here, there = lax.fori_loop(0, OWN // STRIP, strip, (zero, zero))
            here, there = jnp.sum(here, 0, keepdims=True), jnp.sum(there, 0, keepdims=True)
            vec[j : j + 1, :] = jnp.where(t == 0, here, there)
            vec[4 + j : 5 + j, :] = jnp.where(t == 0, there, here)
            local("mix", j, mix.at[j], mixed_out.at[:, pl.ds(j * SPAN, SPAN)]).start()
        bias = jnp.sum(bias_sum[...], 0, keepdims=True)
        vec[8:16, :] = jnp.where(lax.broadcasted_iota(jnp.int32, (8, SPAN), 0) == y, bias, 0.0)
        remote("v_c", 0, vec, vec_c, to_sib).start()

    def over_cores():
        arrived("v_c", 0, vec_c)
        vec_x[...] = vec[...] + vec_c[...]
        remote("v_x", 0, vec_x, vec_xin, to_x).start()

    def over_x():
        arrived("v_x", 0, vec_xin)
        vec_z[z] = vec_x[...] + vec_xin[...]
        for d in range(1, 4):
            remote("v_z", d, vec_z.at[z], vec_z.at[z], to_z[d]).start()

    def over_z():
        for d in range(1, 4):
            arrived("v_z", d, vec_z.at[(z + 4 - d) % 4])
        vec_y[y] = (vec_z[0] + vec_z[1]) + (vec_z[2] + vec_z[3])
        for d in range(1, 4):
            remote("v_y", d, vec_y.at[y], vec_y.at[y], to_y[d]).start()

    def over_y():
        for d in range(1, 4):
            arrived("v_y", d, vec_y.at[(y + 4 - d) % 4])
        vec_t[t] = (vec_y[0] + vec_y[1]) + (vec_y[2] + vec_y[3])
        remote("v_t", 0, vec_t.at[t], vec_t.at[t], to_tower).start()

    between = {0: hidden_over, 2: mixing, 3: over_cores, 4: over_x, 7: over_z, 10: over_y}

    def step(s):
        pl.when(s < CUTS)(lambda: products(s))
        pl.when(s < CUTS)(lambda: relays(s))
        pl.when((s >= 2) & (s < CUTS + 2))(lambda: sums(s - 2))
        pl.when(s >= 3)(lambda: ends(s - 3))
        for at, task in between.items():
            pl.when(s == at)(task)

    loop(CUTS + 3, step)

    arrived("v_t", 0, vec_t.at[1 - t])
    for j in range(4):
        part = slice(j * SPAN, (j + 1) * SPAN)
        for s in range(2):
            for u in range(2):
                stitch_out[s, u : u + 1, part] = vec_t[s, 4 * u + j : 4 * u + j + 1, :]
        bias_out[0:1, part] = vec_t[t, 8 + j : 9 + j, :]

    def finish(k):
        s = slot(k)
        sent("opp_yp", k, d_opp.at[k, 0])
        sent("opp_ym", k, d_opp.at[k, 1])
        sent("opp_zp", k, g_opp.at[k, 0])
        sent("opp_zm", k, g_opp.at[k, 1])
        sent("sum_yp", k, xb.at[k, yp])
        sent("sum_ym", k, xb.at[k, ym])
        sent("sum_zp", k, wb.at[s, :, zp])
        sent("sum_zm", k, wb.at[s, :, zm])
        sent("g_x", k, g_send.at[k])
        d_own(k).wait()
        d_sib(k).wait_send()
        arrived("d_sib", k, feat_out.at[:, columns(other, k)])
        g_own(k).wait()
        g_sib(k).wait_send()
        arrived("g_sib", k, grad_out.at[:, columns(other, k)])

    loop(CUTS, finish)
    for j in range(4):
        sent("cot", j, cot.at[j])
        sent("pg", j, pg.at[j, c])
        sent("tow", j, hid.at[j])
        local("mix", j, mix.at[j], mixed_out.at[:, pl.ds(j * SPAN, SPAN)]).wait()
    for d in range(1, 4):
        sent("hid", d, hid_send.at[(y + d) % 4])
        sent("v_z", d, vec_z.at[z])
        sent("v_y", d, vec_y.at[y])
    sent("v_c", 0, vec)
    sent("v_x", 0, vec_x)
    sent("v_t", 0, vec_t.at[t])
    sent("keep", 0, grouped.at[c])


def towers(*operands):
    low, wide = jnp.bfloat16, jnp.float32
    scratch = [
        ((CUTS, 4, 2, OWN, CUT), low),
        ((CUTS + 1, 2, 4, OWN, CUT), low),
        ((4, 2, OWN, SPAN), wide),
        ((4, OWN, SPAN), wide),
        ((4, 2, OWN, SPAN), low),
        ((2, 4, OWN, SPAN), low),
        ((4, OWN, SPAN), low),
        ((4, OWN, SPAN), low),
        ((4, OWN, SPAN), low),
        ((4, OWN, SPAN), low),
        ((4, OWN, SPAN), low),
        ((4, OWN, SPAN), low),
        ((4, OWN, SPAN), low),
        ((CUTS, 2, OWN, CUT), low),
        ((CUTS, 2, OWN, CUT), low),
        ((CUTS, OWN, CUT), low),
        ((CUTS, OWN, CUT), low),
        ((CUTS, 2, OWN, CUT), low),
        ((CUTS, 2, OWN, CUT), low),
        ((CUTS, OWN, CUT), low),
        ((CUTS, OWN, CUT), low),
        ((CUTS, 2, OWN, CUT), low),
        ((CUTS, 2, OWN, CUT), low),
        ((CUTS, OWN, CUT), low),
        ((CUTS, OWN, CUT), low),
        ((2, OWN, OWN), wide),
        ((4, 8, SPAN), wide),
        ((8, SPAN), wide),
        ((16, SPAN), wide),
        ((16, SPAN), wide),
        ((16, SPAN), wide),
        ((16, SPAN), wide),
        ((4, 16, SPAN), wide),
        ((4, 16, SPAN), wide),
        ((2, 16, SPAN), wide),
    ]
    anywhere = pl.BlockSpec(memory_space=pl.ANY)
    near = pl.BlockSpec(memory_space=pltpu.VMEM)
    return pl.pallas_call(
        body,
        out_shape=[
            jax.ShapeDtypeStruct((OWN, OUT), low),
            jax.ShapeDtypeStruct((OWN, FEAT), low),
            jax.ShapeDtypeStruct((ROWS, FEAT), wide),
            jax.ShapeDtypeStruct((2, 2, OUT), wide),
            jax.ShapeDtypeStruct((1, OUT), wide),
        ],
        in_specs=[anywhere] * 3 + [near] * 4,
        out_specs=[anywhere] * 3 + [near] * 2,
        scratch_shapes=[pltpu.VMEM(shape, kind) for shape, kind in scratch]
        + [
            pltpu.SemaphoreType.DMA((len(KINDS), CUTS)),
            pltpu.SemaphoreType.DMA((len(KINDS), CUTS)),
            pltpu.SemaphoreType.DMA((len(LOCALS), CUTS)),
        ],
        compiler_params=pltpu.CompilerParams(
            collective_id=0, has_side_effects=True, vmem_limit_bytes=62 * 1024 * 1024
        ),
    )(*operands)


def shards(features, group, pad_mask, weights, bias, stitch, momentum, cotangent):
    mixed, feat_grad, weight_grad, stitch_grad, bias_grad = towers(
        features[0], weights[0], cotangent[0], group[None], pad_mask[None], stitch, bias
    )
    weight_grad = weight_grad[None]
    new_momentum = momentum_rate * momentum + weight_grad
    new_weights = weights.astype(jnp.float32) - learn_rate * new_momentum
    return (mixed[None], feat_grad[None], weight_grad, bias_grad, stitch_grad, new_momentum, new_weights)


def solution(mesh):
    placed = (
        P("tower", "blk", None),
        P("blk"),
        P(),
        P("tower", "blk", None),
        P("tower", None),
        P(),
        P("tower", "blk", None),
        P("tower", "blk", None),
    )
    return jax.shard_map(
        shards,
        mesh=mesh,
        in_specs=placed,
        out_specs=(
            P("tower", "blk", None),
            P("tower", "blk", None),
            P("tower", "blk", None),
            P("tower", None),
            P(),
            P("tower", "blk", None),
            P("tower", "blk", None),
        ),
        check_vma=False,
    )
```

```python
import jax
import jax.numpy as jnp
from jax import lax
from jax.experimental import pallas as pl
from jax.experimental.pallas import tpu as pltpu
from jax.sharding import PartitionSpec as P

momentum_rate = 0.9
learn_rate = 0.0001

FEAT = 9216
OUT = 4096
HALF = FEAT // 2
OWN = 128
ROWS = 64
SPAN = 1024
CUT = 512
CUTS = HALF // CUT
STRIP = 32
ORDER = (2, 1, 3, 0)

KINDS = (
    "keep", "x_sib", "w_sib", "cot", "w_x", "own_yp", "own_ym", "own_zp", "own_zm", "pair_zp", "pair_zm",
    "fwd_yp", "fwd_ym", "fwd_zp", "fwd_zm", "hg", "pre", "pg", "hid", "tow", "opp_yp", "opp_ym", "opp_zp",
    "opp_zm", "sum_yp", "sum_ym", "sum_zp", "sum_zm", "g_x", "d_sib", "g_sib", "v_c", "v_x", "v_z", "v_y", "v_t",
)
KIND = {name: row for row, name in enumerate(KINDS)}
LOCALS = ("x", "x_other", "w", "cot", "d", "g", "mix")
LOCAL = {name: row for row, name in enumerate(LOCALS)}


def body(
    features, weights, cotangent, group, pad, stitch, bias,
    mixed_out, feat_out, grad_out, stitch_out, bias_out,
    xb, wb, pre, pre_in, pg, pgt, cot, cot_in, hg_send, hg, hid_send, hid, hid_other, d_opp, g_opp,
    relay_yp, relay_ym, part_yp, part_ym, relay_zp, relay_zm, part_zp, part_zm,
    g_send, g_in, grouped, absent, coef, bias_sum, vec, vec_c, vec_x, vec_xin, vec_z, vec_y, vec_t,
    send_sem, recv_sem, local_sem,
):
    blk, t = lax.axis_index("blk"), lax.axis_index("tower")
    y, x, z, c = blk // 16, (blk // 8) % 2, (blk // 2) % 4, blk % 2
    other = 1 - c

    def place(y, x, z, c):
        return ((y * 2 + x) * 4 + z) * 2 + c

    yp, yo, ym = (y + 1) % 4, (y + 2) % 4, (y + 3) % 4
    zp, zo, zm = (z + 1) % 4, (z + 2) % 4, (z + 3) % 4
    to_yp, to_yo, to_ym = ((place(v, x, z, c), t) for v in (yp, yo, ym))
    to_zp, to_zo, to_zm = ((place(y, x, v, c), t) for v in (zp, zo, zm))
    to_x = (place(y, 1 - x, z, c), t)
    to_sib = (place(y, x, z, other), t)
    to_tower = (blk, 1 - t)
    to_y = (None, to_yp, to_yo, to_ym)
    to_z = (None, to_zp, to_zo, to_zm)

    def remote(kind, k, src, dst, device):
        return pltpu.make_async_remote_copy(
            src_ref=src, dst_ref=dst,
            send_sem=send_sem.at[KIND[kind], k], recv_sem=recv_sem.at[KIND[kind], k],
            device_id=device, device_id_type=pl.DeviceIdType.MESH,
        )

    def arrived(kind, k, dst):
        remote(kind, k, dst, dst, to_sib).wait_recv()

    def sent(kind, k, src):
        remote(kind, k, src, src, to_sib).wait_send()

    def local(kind, k, src, dst):
        return pltpu.make_async_copy(src, dst, local_sem.at[LOCAL[kind], k])

    def columns(side, k):
        return pl.ds(pl.multiple_of(side * HALF + k * CUT, CUT), CUT)

    def loop(count, step):
        lax.fori_loop(0, count, lambda k, carry: (step(k), carry)[1], 0)

    staged = g_send
    own_rows = pl.ds(pl.multiple_of(c * ROWS, ROWS), ROWS)
    sib_rows = pl.ds(pl.multiple_of(other * ROWS, ROWS), ROWS)

    def load_x(k):
        return local("x", k, features.at[:, columns(c, k)], xb.at[k, y, c])

    def load_other(k):
        return local("x_other", k, features.at[:, columns(other, k)], staged.at[k])

    def load_w(k):
        return local("w", k, weights.at[:, columns(c, k)], wb.at[k, x, z, own_rows])

    def load_cot(j):
        return local("cot", j, cotangent.at[:, pl.ds(j * SPAN, SPAN)], cot.at[j])

    def start_loads(k):
        load_x(k).start()
        load_other(k).start()
        load_w(k).start()

    loop(CUTS, start_loads)
    for j in range(4):
        load_cot(j).start()
    grouped[c] = jnp.broadcast_to(group[...].astype(jnp.float32), (OWN, OWN)).T.astype(jnp.bfloat16)
    for j in range(4):
        part = slice(j * SPAN, (j + 1) * SPAN)
        coef[j, 0:1, :] = jnp.where(t == 0, stitch[0, 0:1, part], stitch[1, 1:2, part])
        coef[j, 1:2, :] = jnp.where(t == 0, stitch[1, 0:1, part], stitch[0, 1:2, part])
        coef[j, 2:3, :] = jnp.where(t == 0, stitch[0, 1:2, part], stitch[1, 0:1, part])
        coef[j, 3:4, :] = bias[0:1, part]

    absent[...] = 1.0 - pad[...].astype(jnp.float32).astype(jnp.bfloat16)

    def kept(value, core, side, k):
        rows = jnp.concatenate([grouped[core]] * (CUT // OWN), 1)
        return value * (1.0 - rows * absent[0:1, columns(side, k)])

    barrier = pltpu.get_barrier_semaphore()
    partners = (to_yp, to_yo, to_ym, to_zp, to_zo, to_zm, to_x, to_sib, to_tower)
    for device in partners:
        pl.semaphore_signal(barrier, inc=1, device_id=device, device_id_type=pl.DeviceIdType.MESH)
    pl.semaphore_wait(barrier, len(partners))

    remote("keep", 0, grouped.at[c], grouped.at[c], to_sib).start()

    def x_sib(k):
        return remote("x_sib", k, staged.at[k], xb.at[k, y, c], to_sib)

    def w_sib(k):
        return remote("w_sib", k, weights.at[:, columns(other, k)], wb.at[k, x, z, own_rows], to_sib)

    def to_sibling(k):
        w_sib(k).start()
        load_other(k).wait()
        staged[k] = kept(staged[k], c, other, k)
        x_sib(k).start()
        load_x(k).wait()
        xb[k, y, c] = kept(xb[k, y, c], c, c, k)

    def own_out(k):
        arrived("x_sib", k, xb.at[k, y, other])
        remote("own_yp", k, xb.at[k, y], xb.at[k, y], to_yp).start()
        remote("own_ym", k, xb.at[k, y], xb.at[k, y], to_ym).start()
        load_w(k).wait()
        arrived("w_sib", k, wb.at[k, x, z, sib_rows])
        remote("w_x", k, wb.at[k, x, z], wb.at[k, x, z], to_x).start()
        remote("own_zp", k, wb.at[k, x, z], wb.at[k, x, z], to_zp).start()
        remote("own_zm", k, wb.at[k, x, z], wb.at[k, x, z], to_zm).start()

    def first(k):
        pl.when(k < CUTS)(lambda: to_sibling(k))
        pl.when(k >= 1)(lambda: own_out(k - 1))

    loop(CUTS + 1, first)
    for j in range(4):
        remote("cot", j, cotangent.at[:, pl.ds(j * SPAN, SPAN)], cot_in.at[j], to_tower).start()

    def pair_out(k):
        arrived("w_x", k, wb.at[k, 1 - x, z])
        remote("pair_zp", k, wb.at[k, 1 - x, z], wb.at[k, 1 - x, z], to_zp).start()
        remote("pair_zm", k, wb.at[k, 1 - x, z], wb.at[k, 1 - x, z], to_zm).start()

    loop(CUTS, pair_out)

    def forward(k):
        arrived("own_yp", k, xb.at[k, ym])
        remote("fwd_yp", k, xb.at[k, ym, 0], xb.at[k, ym, 0], to_yp).start()
        arrived("own_ym", k, xb.at[k, yp])
        remote("fwd_ym", k, xb.at[k, yp, 1], xb.at[k, yp, 1], to_ym).start()
        arrived("own_zp", k, wb.at[k, x, zm])
        remote("fwd_zp", k, wb.at[k, x, zm], wb.at[k, x, zm], to_zp).start()
        arrived("own_zm", k, wb.at[k, x, zp])
        arrived("pair_zp", k, wb.at[k, 1 - x, zm])
        arrived("pair_zm", k, wb.at[k, 1 - x, zp])
        remote("fwd_zm", k, wb.at[k, 1 - x, zp], wb.at[k, 1 - x, zp], to_zm).start()

    loop(CUTS, forward)

    for j in range(4):
        load_cot(j).wait()
        arrived("cot", j, cot_in.at[j])
    for d in ORDER:
        j = (y + d) % 4

        def combine(i, d=d, j=j):
            rows = pl.ds(pl.multiple_of(i * STRIP, STRIP), STRIP)
            value = (
                coef[j, 0:1, :] * cot[j, rows, :].astype(jnp.float32)
                + coef[j, 1:2, :] * cot_in[j, rows, :].astype(jnp.float32)
            ).astype(jnp.bfloat16)
            if d == 0:
                hg[y, rows, :] = value
            else:
                hg_send[j, rows, :] = value

        loop(OWN // STRIP, combine)
        if d:
            remote("hg", d, hg_send.at[j], hg.at[y], to_y[d]).start()

    def gathered(k):
        arrived("fwd_yp", k, xb.at[k, yo, 0])
        arrived("fwd_ym", k, xb.at[k, yo, 1])
        arrived("fwd_zp", k, wb.at[k, x, zo])
        arrived("fwd_zm", k, wb.at[k, 1 - x, zo])

    def add_block(k, b):
        pre[b] += lax.dot_general(
            xb[k, b].reshape(2 * OWN, CUT), wb[k].reshape(SPAN, CUT),
            (((1,), (1,)), ((), ())), preferred_element_type=jnp.float32,
        ).reshape(2, OWN, SPAN)

    def add_product(k):
        gathered(k)
        loop(4, lambda b: add_block(k, b))

    def clear(b):
        pre[b] = jnp.zeros((2, OWN, SPAN), jnp.float32)

    loop(4, clear)
    loop(CUTS - 1, add_product)
    gathered(CUTS - 1)

    for d in ORDER:
        b = (y + d) % 4
        add_block(CUTS - 1, b)
        remote("pre", d, pre.at[b, other], pre_in.at[b], to_sib).start()
    bias_sum[...] = jnp.zeros_like(bias_sum)

    def activate(d):
        b = (y + d) % 4
        arrived("pre", d, pre_in.at[b])
        if d:
            arrived("hg", 4 - d, hg.at[b])

        def act(i):
            rows = pl.ds(pl.multiple_of(i * STRIP, STRIP), STRIP)
            value = pre[b, c, rows, :] + pre_in[b, rows, :] + coef[y, 3:4, :]
            gate = jax.nn.sigmoid(value)
            hidden = (value * gate).astype(jnp.bfloat16)
            grad = (hg[b, rows, :].astype(jnp.float32) * gate * (1.0 + value * (1.0 - gate))).astype(jnp.bfloat16)
            pg[b, c, rows, :] = grad
            if d == 0:
                hid[y, rows, :] = hidden
            else:
                hid_send[b, rows, :] = hidden
            bias_sum[...] += jnp.sum(grad.astype(jnp.float32).reshape(STRIP // 8, 8, SPAN), 0)

        loop(OWN // STRIP, act)
        remote("pg", d, pg.at[b, c], pg.at[b, c], to_sib).start()
        if d:
            remote("hid", d, hid_send.at[b], hid.at[y], to_y[d]).start()

    def product_d(k, b):
        product = jnp.dot(
            pg[b].reshape(2 * OWN, SPAN), wb[k].reshape(SPAN, CUT), preferred_element_type=jnp.float32
        )
        return product.astype(jnp.bfloat16).reshape(2, OWN, CUT)

    def product_g(k, v):
        product = jnp.dot(
            pgt[:, v].reshape(2 * OWN, SPAN), xb[k].reshape(SPAN, CUT), preferred_element_type=jnp.float32
        )
        return product.astype(jnp.bfloat16).reshape(2, OWN, CUT)

    def opposite_d(k):
        d_opp[k] = product_d(k, yo)
        remote("opp_yp", k, d_opp.at[k, 0], relay_yp.at[k], to_yp).start()
        remote("opp_ym", k, d_opp.at[k, 1], relay_ym.at[k], to_ym).start()

    def opposite_g(k):
        g_opp[k] = product_g(k, zo)
        remote("opp_zp", k, g_opp.at[k, 0], relay_zp.at[k], to_zp).start()
        remote("opp_zm", k, g_opp.at[k, 1], relay_zm.at[k], to_zm).start()

    for d in ORDER:
        activate(d)
    for d in ORDER:
        arrived("pg", d, pg.at[(y + d) % 4, other])
        if d == 2:
            loop(CUTS, opposite_d)

    wide = 256
    eye = (
        lax.broadcasted_iota(jnp.int32, (wide, wide), 0) == lax.broadcasted_iota(jnp.int32, (wide, wide), 1)
    ).astype(jnp.bfloat16)
    for o in range(SPAN // wide):
        flipped = lax.dot_general(
            eye, pg[:, :, :, o * wide : (o + 1) * wide].reshape(SPAN, wide),
            (((1,), (1,)), ((), ())), preferred_element_type=jnp.float32,
        )
        pgt[o // 2, (o % 2) * 2 : (o % 2) * 2 + 2] = flipped.astype(jnp.bfloat16).reshape(2, OWN, SPAN)
    loop(CUTS, opposite_g)

    def left(k):
        sent("x_sib", k, staged.at[k])
        sent("w_sib", k, wb.at[k, x, z, own_rows])
        sent("own_yp", k, xb.at[k, y])
        sent("own_ym", k, xb.at[k, y])
        sent("w_x", k, wb.at[k, x, z])
        sent("own_zp", k, wb.at[k, x, z])
        sent("own_zm", k, wb.at[k, x, z])
        sent("pair_zp", k, wb.at[k, 1 - x, z])
        sent("pair_zm", k, wb.at[k, 1 - x, z])
        sent("fwd_yp", k, xb.at[k, ym, 0])
        sent("fwd_ym", k, xb.at[k, yp, 1])
        sent("fwd_zp", k, wb.at[k, x, zm])
        sent("fwd_zm", k, wb.at[k, 1 - x, zp])

    loop(CUTS, left)
    for d in range(4):
        sent("pre", d, pre.at[d, other])
        if d:
            sent("hg", d, hg_send.at[(y + d) % 4])
    arrived("keep", 0, grouped.at[other])
    mix = hg_send

    def slot(k):
        return (k + CUTS) % (CUTS + 1)

    def g_keep(k):
        part = pl.ds(pl.multiple_of((k % (SPAN // CUT)) * CUT, CUT), CUT)
        block = k // (SPAN // CUT)
        return pre.at[block // 2, block % 2, :, part]

    def products(k):
        s = slot(k)

        def block_g(i):
            v = (zo + 1 + i) % 4
            wb[s, :, v] = product_g(k, v)

        def block_d(i):
            b = (yo + 1 + i) % 4
            xb[k, b] = product_d(k, b)

        loop(3, block_g)
        loop(3, block_d)

    def wide_sum(*terms):
        total = terms[0].astype(jnp.float32)
        for term in terms[1:]:
            total += term.astype(jnp.float32)
        return total

    def relays(k):
        s = slot(k)
        arrived("opp_yp", k, relay_yp.at[k])
        xb[k, yp, 0] = wide_sum(xb[k, yp, 0], relay_yp[k]).astype(jnp.bfloat16)
        remote("sum_yp", k, xb.at[k, yp], part_yp.at[k], to_yp).start()
        arrived("opp_ym", k, relay_ym.at[k])
        xb[k, ym, 1] = wide_sum(xb[k, ym, 1], relay_ym[k]).astype(jnp.bfloat16)
        remote("sum_ym", k, xb.at[k, ym], part_ym.at[k], to_ym).start()
        arrived("opp_zp", k, relay_zp.at[k])
        wb[s, 0, zp] = wide_sum(wb[s, 0, zp], relay_zp[k]).astype(jnp.bfloat16)
        remote("sum_zp", k, wb.at[s, :, zp], part_zp.at[k], to_zp).start()
        arrived("opp_zm", k, relay_zm.at[k])
        wb[s, 1, zm] = wide_sum(wb[s, 1, zm], relay_zm[k]).astype(jnp.bfloat16)
        remote("sum_zm", k, wb.at[s, :, zm], part_zm.at[k], to_zm).start()

    def d_own(k):
        return local("d", k, xb.at[k, y, c], feat_out.at[:, columns(c, k)])

    def d_sib(k):
        return remote("d_sib", k, xb.at[k, y, other], feat_out.at[:, columns(c, k)], to_sib)

    def g_own(k):
        return local("g", k, g_keep(k).at[own_rows], grad_out.at[:, columns(c, k)])

    def g_sib(k):
        return remote("g_sib", k, g_keep(k).at[sib_rows], grad_out.at[:, columns(c, k)], to_sib)

    def sums(k):
        s = slot(k)
        arrived("sum_zp", k, part_zp.at[k])
        arrived("sum_zm", k, part_zm.at[k])
        g_send[k] = wide_sum(wb[s, 1 - x, z], part_zp[k, 1 - x], part_zm[k, 1 - x]).astype(jnp.bfloat16)
        remote("g_x", k, g_send.at[k], g_in.at[k], to_x).start()
        g_keep(k)[...] = wide_sum(wb[s, x, z], part_zp[k, x], part_zm[k, x])
        arrived("sum_yp", k, part_yp.at[k])
        arrived("sum_ym", k, part_ym.at[k])
        for core in range(2):
            total = wide_sum(xb[k, y, core], part_yp[k, core], part_ym[k, core])
            xb[k, y, core] = kept(total.astype(jnp.bfloat16), core, c, k)
        d_own(k).start()
        d_sib(k).start()

    def ends(k):
        arrived("g_x", k, g_in.at[k])
        g_keep(k)[...] += g_in[k].astype(jnp.float32)
        g_own(k).start()
        g_sib(k).start()

    def hidden_over():
        for d in range(1, 4):
            arrived("hid", d, hid.at[(y + 4 - d) % 4])
        for j in range(4):
            remote("tow", j, hid.at[j], hid_other.at[j], to_tower).start()

    def mixing():
        for j in range(4):
            arrived("tow", j, hid_other.at[j])

            def strip(i, sums, j=j):
                rows = pl.ds(pl.multiple_of(i * STRIP, STRIP), STRIP)
                here = hid[j, rows, :].astype(jnp.float32)
                there = hid_other[j, rows, :].astype(jnp.float32)
                mix[j, rows, :] = (coef[j, 0:1, :] * here + coef[j, 2:3, :] * there).astype(jnp.bfloat16)
                up = cot[j, rows, :].astype(jnp.float32)
                return (
                    sums[0] + jnp.sum((up * here).reshape(STRIP // 8, 8, SPAN), 0),
                    sums[1] + jnp.sum((up * there).reshape(STRIP // 8, 8, SPAN), 0),
                )

            zero = jnp.zeros((8, SPAN), jnp.float32)
            here, there = lax.fori_loop(0, OWN // STRIP, strip, (zero, zero))
            here, there = jnp.sum(here, 0, keepdims=True), jnp.sum(there, 0, keepdims=True)
            vec[j : j + 1, :] = jnp.where(t == 0, here, there)
            vec[4 + j : 5 + j, :] = jnp.where(t == 0, there, here)
            local("mix", j, mix.at[j], mixed_out.at[:, pl.ds(j * SPAN, SPAN)]).start()
        bias = jnp.sum(bias_sum[...], 0, keepdims=True)
        vec[8:16, :] = jnp.where(lax.broadcasted_iota(jnp.int32, (8, SPAN), 0) == y, bias, 0.0)
        remote("v_c", 0, vec, vec_c, to_sib).start()

    def over_cores():
        arrived("v_c", 0, vec_c)
        vec_x[...] = vec[...] + vec_c[...]
        remote("v_x", 0, vec_x, vec_xin, to_x).start()

    def over_x():
        arrived("v_x", 0, vec_xin)
        vec_z[z] = vec_x[...] + vec_xin[...]
        for d in range(1, 4):
            remote("v_z", d, vec_z.at[z], vec_z.at[z], to_z[d]).start()

    def over_z():
        for d in range(1, 4):
            arrived("v_z", d, vec_z.at[(z + 4 - d) % 4])
        vec_y[y] = (vec_z[0] + vec_z[1]) + (vec_z[2] + vec_z[3])
        for d in range(1, 4):
            remote("v_y", d, vec_y.at[y], vec_y.at[y], to_y[d]).start()

    def over_y():
        for d in range(1, 4):
            arrived("v_y", d, vec_y.at[(y + 4 - d) % 4])
        vec_t[t] = (vec_y[0] + vec_y[1]) + (vec_y[2] + vec_y[3])
        remote("v_t", 0, vec_t.at[t], vec_t.at[t], to_tower).start()

    between = {0: (hidden_over,), 3: (mixing, over_cores), 4: (over_x,), 7: (over_z,), 9: (over_y,)}

    def step(s):
        pl.when(s < CUTS)(lambda: products(s))
        pl.when(s < CUTS)(lambda: relays(s))
        pl.when((s >= 2) & (s < CUTS + 2))(lambda: sums(s - 2))
        pl.when(s >= 3)(lambda: ends(s - 3))
        for at, tasks in between.items():

            @pl.when(s == at)
            def _(tasks=tasks):
                for task in tasks:
                    task()

    loop(CUTS + 3, step)

    arrived("v_t", 0, vec_t.at[1 - t])
    for j in range(4):
        part = slice(j * SPAN, (j + 1) * SPAN)
        for s in range(2):
            for u in range(2):
                stitch_out[s, u : u + 1, part] = vec_t[s, 4 * u + j : 4 * u + j + 1, :]
        bias_out[0:1, part] = vec_t[t, 8 + j : 9 + j, :]

    def finish(k):
        s = slot(k)
        sent("opp_yp", k, d_opp.at[k, 0])
        sent("opp_ym", k, d_opp.at[k, 1])
        sent("opp_zp", k, g_opp.at[k, 0])
        sent("opp_zm", k, g_opp.at[k, 1])
        sent("sum_yp", k, xb.at[k, yp])
        sent("sum_ym", k, xb.at[k, ym])
        sent("sum_zp", k, wb.at[s, :, zp])
        sent("sum_zm", k, wb.at[s, :, zm])
        sent("g_x", k, g_send.at[k])
        d_own(k).wait()
        d_sib(k).wait_send()
        arrived("d_sib", k, feat_out.at[:, columns(other, k)])
        g_own(k).wait()
        g_sib(k).wait_send()
        arrived("g_sib", k, grad_out.at[:, columns(other, k)])

    loop(CUTS, finish)
    for j in range(4):
        sent("cot", j, cot.at[j])
        sent("pg", j, pg.at[j, c])
        sent("tow", j, hid.at[j])
        local("mix", j, mix.at[j], mixed_out.at[:, pl.ds(j * SPAN, SPAN)]).wait()
    for d in range(1, 4):
        sent("hid", d, hid_send.at[(y + d) % 4])
        sent("v_z", d, vec_z.at[z])
        sent("v_y", d, vec_y.at[y])
    sent("v_c", 0, vec)
    sent("v_x", 0, vec_x)
    sent("v_t", 0, vec_t.at[t])
    sent("keep", 0, grouped.at[c])


def towers(*operands):
    low, wide = jnp.bfloat16, jnp.float32
    scratch = [
        ((CUTS, 4, 2, OWN, CUT), low),
        ((CUTS + 1, 2, 4, OWN, CUT), low),
        ((4, 2, OWN, SPAN), wide),
        ((4, OWN, SPAN), wide),
        ((4, 2, OWN, SPAN), low),
        ((2, 4, OWN, SPAN), low),
        ((4, OWN, SPAN), low),
        ((4, OWN, SPAN), low),
        ((4, OWN, SPAN), low),
        ((4, OWN, SPAN), low),
        ((4, OWN, SPAN), low),
        ((4, OWN, SPAN), low),
        ((4, OWN, SPAN), low),
        ((CUTS, 2, OWN, CUT), low),
        ((CUTS, 2, OWN, CUT), low),
        ((CUTS, OWN, CUT), low),
        ((CUTS, OWN, CUT), low),
        ((CUTS, 2, OWN, CUT), low),
        ((CUTS, 2, OWN, CUT), low),
        ((CUTS, OWN, CUT), low),
        ((CUTS, OWN, CUT), low),
        ((CUTS, 2, OWN, CUT), low),
        ((CUTS, 2, OWN, CUT), low),
        ((CUTS, OWN, CUT), low),
        ((CUTS, OWN, CUT), low),
        ((2, OWN, OWN), low),
        ((1, FEAT), low),
        ((4, 8, SPAN), wide),
        ((8, SPAN), wide),
        ((16, SPAN), wide),
        ((16, SPAN), wide),
        ((16, SPAN), wide),
        ((16, SPAN), wide),
        ((4, 16, SPAN), wide),
        ((4, 16, SPAN), wide),
        ((2, 16, SPAN), wide),
    ]
    anywhere = pl.BlockSpec(memory_space=pl.ANY)
    near = pl.BlockSpec(memory_space=pltpu.VMEM)
    return pl.pallas_call(
        body,
        out_shape=[
            jax.ShapeDtypeStruct((OWN, OUT), low),
            jax.ShapeDtypeStruct((OWN, FEAT), low),
            jax.ShapeDtypeStruct((ROWS, FEAT), wide),
            jax.ShapeDtypeStruct((2, 2, OUT), wide),
            jax.ShapeDtypeStruct((1, OUT), wide),
        ],
        in_specs=[anywhere] * 3 + [near] * 4,
        out_specs=[anywhere] * 3 + [near] * 2,
        scratch_shapes=[pltpu.VMEM(shape, kind) for shape, kind in scratch]
        + [
            pltpu.SemaphoreType.DMA((len(KINDS), CUTS)),
            pltpu.SemaphoreType.DMA((len(KINDS), CUTS)),
            pltpu.SemaphoreType.DMA((len(LOCALS), CUTS)),
        ],
        compiler_params=pltpu.CompilerParams(
            collective_id=0, has_side_effects=True, vmem_limit_bytes=59 * 1024 * 1024
        ),
    )(*operands)


def shards(features, group, pad_mask, weights, bias, stitch, momentum, cotangent):
    mixed, feat_grad, weight_grad, stitch_grad, bias_grad = towers(
        features[0], weights[0], cotangent[0], group[None], pad_mask[None], stitch, bias
    )
    weight_grad = weight_grad[None]
    new_momentum = momentum_rate * momentum + weight_grad
    new_weights = weights.astype(jnp.float32) - learn_rate * new_momentum
    return (mixed[None], feat_grad[None], weight_grad, bias_grad, stitch_grad, new_momentum, new_weights)


def solution(mesh):
    placed = (
        P("tower", "blk", None),
        P("blk"),
        P(),
        P("tower", "blk", None),
        P("tower", None),
        P(),
        P("tower", "blk", None),
        P("tower", "blk", None),
    )
    return jax.shard_map(
        shards,
        mesh=mesh,
        in_specs=placed,
        out_specs=(
            P("tower", "blk", None),
            P("tower", "blk", None),
            P("tower", "blk", None),
            P("tower", None),
            P(),
            P("tower", "blk", None),
            P("tower", "blk", None),
        ),
        check_vma=False,
    )
```

```python
import enum

import jax
import jax.numpy as jnp
from jax import lax
from jax.experimental import pallas as pl
from jax.experimental.pallas import tpu as pltpu
from jax.sharding import PartitionSpec as P

momentum_rate = 0.9
learn_rate = 0.0001

FEAT = 9216
OUT = 4096
HALF = FEAT // 2
OWN = 128
ROWS = 64
SPAN = 1024
CUT = 512
CUTS = HALF // CUT
LATE = 1
EARLY = CUTS - LATE
PARTS = 4
STRIP = 32
ORDER = (2, 1, 3, 0)


class Kind(enum.IntEnum):
    (
        x_sib, w_sib, w_x, own_yp, own_ym, own_zp, own_zm, pair_zp, pair_zm, sib_yp, sib_ym, fwd_yp, fwd_ym, fwd_zp, fwd_zm,
        opp_yp, opp_ym, opp_zp, opp_zm, sum_yp, sum_ym, sum_zp, sum_zm, g_x, d_sib, g_sib, late_opp_zp, late_opp_zm,
        late_sum_zp, late_sum_zm, keep, cot, hg, pre, pg, hid, tow, gb_x, v_c, v_x, v_z, v_y, v_t, v_b,
    ) = range(44)


class Local(enum.IntEnum):
    w, cot, d, g, mix, small, small_1, small_2, small_3 = range(9)


ROWED = (
    Kind.x_sib, Kind.w_sib, Kind.w_x, Kind.own_yp, Kind.own_ym, Kind.own_zp, Kind.own_zm, Kind.pair_zp, Kind.pair_zm,
    Kind.sib_yp, Kind.sib_ym, Kind.fwd_yp, Kind.fwd_ym, Kind.fwd_zp, Kind.fwd_zm,
)
AGAIN = {
    Kind.opp_yp: Kind.own_yp, Kind.opp_ym: Kind.own_ym, Kind.opp_zp: Kind.own_zp, Kind.opp_zm: Kind.own_zm, Kind.sum_yp:
    Kind.pair_zp, Kind.sum_ym: Kind.pair_zm, Kind.sum_zp: Kind.x_sib, Kind.sum_zm: Kind.w_x, Kind.g_x: Kind.w_sib,
    Kind.d_sib: Kind.fwd_yp, Kind.g_sib: Kind.fwd_ym, Kind.late_opp_zp: Kind.own_zp, Kind.late_opp_zm: Kind.own_zm,
    Kind.late_sum_zp: Kind.x_sib, Kind.late_sum_zm: Kind.w_x,
}
FEW = {
    Kind.keep: 1, Kind.cot: 1, Kind.hg: 4, Kind.pre: 4, Kind.pg: 4, Kind.hid: 1, Kind.tow: 1, Kind.gb_x: LATE, Kind.v_c: 1,
    Kind.v_x: 1, Kind.v_z: 1, Kind.v_y: 1, Kind.v_t: 1, Kind.v_b: 1,
}
ROW = {kind: row for row, kind in enumerate(ROWED)}
ROW.update({kind: ROW[before] for kind, before in AGAIN.items()})
FIRST = {kind: sum(list(FEW.values())[:place]) for place, kind in enumerate(FEW)}


def body(
    features, weights, cotangent, group_in, pad_in, stitch_in, bias_in,
    mixed_out, feat_out, grad_out, stitch_out, bias_out,
    xb, wb, pre, pre_in, pg, pgt, cot, cot_in, hg_send, hg, hid, hid_other, d_opp, g_opp, late_out, late,
    relay_yp, relay_ym, part_yp, part_ym, relay_zp, relay_zm, part_zp, part_zm,
    g_send, g_in, group, pad, stitch, bias, stitch_sum, bias_total, grouped, absent, coef, bias_sum, vec, vec_c, vec_x, vec_xin, vec_z, vec_y, vec_t,
    send_sem, row_sem, few_sem, load_sem, local_sem,
):
    blk, t = lax.axis_index("blk"), lax.axis_index("tower")
    y, x, z, c = blk // 16, (blk // 8) % 2, (blk // 2) % 4, blk % 2
    other = 1 - c

    def place(y, x, z, c):
        return ((y * 2 + x) * 4 + z) * 2 + c

    yp, yo, ym = (y + 1) % 4, (y + 2) % 4, (y + 3) % 4
    zp, zo, zm = (z + 1) % 4, (z + 2) % 4, (z + 3) % 4
    to_yp, to_yo, to_ym = ((place(v, x, z, c), t) for v in (yp, yo, ym))
    to_zp, to_zo, to_zm = ((place(y, x, v, c), t) for v in (zp, zo, zm))
    to_x = (place(y, 1 - x, z, c), t)
    to_sib = (place(y, x, z, other), t)
    to_tower = (blk, 1 - t)
    to_y = (None, to_yp, to_yo, to_ym)
    to_z = (None, to_zp, to_zo, to_zm)

    def remote(kind, k, src, dst, device):
        if kind in ROW:
            landed = row_sem.at[ROW[kind], k]
        else:
            landed = few_sem.at[FIRST[kind] + (k if FEW[kind] > 1 else 0)]
        return pltpu.make_async_remote_copy(
            src_ref=src, dst_ref=dst, send_sem=send_sem.at[kind], recv_sem=landed,
            device_id=device, device_id_type=pl.DeviceIdType.MESH,
        )

    def arrived(kind, k, dst):
        remote(kind, k, dst, dst, to_sib).wait_recv()

    def sent(kind, src):
        remote(kind, 0, src, src, to_sib).wait_send()

    def local(kind, src, dst):
        return pltpu.make_async_copy(src, dst, local_sem.at[kind])

    def columns(side, k):
        return pl.ds(pl.multiple_of(side * HALF + k * CUT, CUT), CUT)

    def loop(count, step):
        lax.fori_loop(0, count, lambda k, carry: (step(k), carry)[1], 0)

    hid_send = cot_in
    staged = g_send
    TOP, LOW = pl.ds(0, OWN // 2), pl.ds(OWN // 2, OWN // 2)
    own_rows = pl.ds(pl.multiple_of(c * ROWS, ROWS), ROWS)
    sib_rows = pl.ds(pl.multiple_of(other * ROWS, ROWS), ROWS)

    def load_x(k):
        return pltpu.make_async_copy(features.at[:, columns(c, k)], xb.at[k, y, c], load_sem.at[k])

    def load_other(k):
        return pltpu.make_async_copy(features.at[:, columns(other, k)], staged.at[k], load_sem.at[k])

    def load_w(k):
        return local(Local.w, weights.at[:, columns(c, k)], wb.at[k, x, z, own_rows])

    def start_loads(k):
        load_x(k).start()
        load_other(k).start()
        load_w(k).start()

    small = [
        local(Local.small + i, src, dst)
        for i, (src, dst) in enumerate(((group_in, group), (pad_in, pad), (stitch_in, stitch), (bias_in, bias)))
    ]
    for copy in small:
        copy.start()
    loop(CUTS, start_loads)
    for j in range(4):
        local(Local.cot, cotangent.at[:, pl.ds(j * SPAN, SPAN)], cot.at[j]).start()

    barrier = pltpu.get_barrier_semaphore()
    partners = (to_yp, to_yo, to_ym, to_zp, to_zo, to_zm, to_x, to_sib, to_tower)
    for device in partners:
        pl.semaphore_signal(barrier, inc=1, device_id=device, device_id_type=pl.DeviceIdType.MESH)

    for copy in small:
        copy.wait()
    grouped[c] = jnp.broadcast_to(group[...].astype(jnp.float32), (OWN, OWN)).T.astype(jnp.bfloat16)
    for j in range(4):
        part = slice(j * SPAN, (j + 1) * SPAN)
        coef[j, 0:1, :] = jnp.where(t == 0, stitch[0, 0:1, part], stitch[1, 1:2, part])
        coef[j, 1:2, :] = jnp.where(t == 0, stitch[1, 0:1, part], stitch[0, 1:2, part])
        coef[j, 2:3, :] = jnp.where(t == 0, stitch[0, 1:2, part], stitch[1, 0:1, part])
        coef[j, 3:4, :] = bias[0:1, part]

    absent[...] = 1.0 - pad[...].astype(jnp.float32).astype(jnp.bfloat16)

    def kept(value, core, side, k):
        rows = jnp.concatenate([grouped[core]] * (CUT // OWN), 1)
        return value * (1.0 - rows * absent[0:1, columns(side, k)])

    def masked(k):
        pltpu.make_async_copy(xb.at[k, y], xb.at[k, y], load_sem.at[k]).wait()
        staged[k] = kept(staged[k], c, other, k)
        xb[k, y, c] = kept(xb[k, y, c], c, c, k)

    masked(0)
    pl.semaphore_wait(barrier, len(partners))

    remote(Kind.keep, 0, grouped.at[c], grouped.at[c], to_sib).start()

    def x_sib(k):
        return remote(Kind.x_sib, k, staged.at[k], xb.at[k, y, c], to_sib)

    def w_sib(k):
        return remote(Kind.w_sib, k, weights.at[:, columns(other, k)], wb.at[k, x, z, own_rows], to_sib)

    def to_sibling(k):
        w_sib(k).start()
        pl.when(k > 0)(lambda: masked(k))
        x_sib(k).start()
        remote(Kind.own_yp, k, xb.at[k, y, c], xb.at[k, y, c], to_yp).start()
        remote(Kind.own_ym, k, xb.at[k, y, c], xb.at[k, y, c], to_ym).start()

    def own_out(k):
        arrived(Kind.x_sib, k, xb.at[k, y, other])
        remote(Kind.sib_yp, k, xb.at[k, y, other], xb.at[k, y, other], to_yp).start()
        remote(Kind.sib_ym, k, xb.at[k, y, other], xb.at[k, y, other], to_ym).start()
        arrived(Kind.w_sib, k, wb.at[k, x, z, sib_rows])
        remote(Kind.w_x, k, wb.at[k, x, z], wb.at[k, x, z], to_x).start()
        remote(Kind.own_zp, k, wb.at[k, x, z], wb.at[k, x, z], to_zp).start()
        remote(Kind.own_zm, k, wb.at[k, x, z], wb.at[k, x, z], to_zm).start()

    every_w = wb.at[:CUTS, x, z]

    def first(k):
        pl.when(k < CUTS)(lambda: to_sibling(k))

        @pl.when(k == 0)
        def _():
            every = wb.at[:CUTS, x, z, own_rows]
            local(Local.w, every, every).wait()

        pl.when(k >= 1)(lambda: own_out(k - 1))

    loop(CUTS + 1, first)
    for j in range(4):
        remote(Kind.cot, j, cotangent.at[:, pl.ds(j * SPAN, SPAN)], cot_in.at[j], to_tower).start()

    def pair_out(k):
        arrived(Kind.w_x, k, wb.at[k, 1 - x, z])
        remote(Kind.pair_zp, k, wb.at[k, 1 - x, z], wb.at[k, 1 - x, z], to_zp).start()
        remote(Kind.pair_zm, k, wb.at[k, 1 - x, z], wb.at[k, 1 - x, z], to_zm).start()

    loop(CUTS, pair_out)

    def forward(k):
        arrived(Kind.own_yp, k, xb.at[k, ym, c])
        arrived(Kind.sib_yp, k, xb.at[k, ym, other])
        remote(Kind.fwd_yp, k, xb.at[k, ym, 0], xb.at[k, ym, 0], to_yp).start()
        arrived(Kind.own_ym, k, xb.at[k, yp, c])
        arrived(Kind.sib_ym, k, xb.at[k, yp, other])
        remote(Kind.fwd_ym, k, xb.at[k, yp, 1], xb.at[k, yp, 1], to_ym).start()
        arrived(Kind.own_zp, k, wb.at[k, x, zm])
        remote(Kind.fwd_zp, k, wb.at[k, x, zm], wb.at[k, x, zm], to_zp).start()
        arrived(Kind.own_zm, k, wb.at[k, x, zp])
        arrived(Kind.pair_zp, k, wb.at[k, 1 - x, zm])
        arrived(Kind.pair_zm, k, wb.at[k, 1 - x, zp])
        remote(Kind.fwd_zm, k, wb.at[k, 1 - x, zp], wb.at[k, 1 - x, zp], to_zm).start()

    loop(CUTS, forward)

    local(Local.cot, cot, cot).wait()
    arrived(Kind.cot, 0, cot_in)
    for d in ORDER:
        j = (y + d) % 4

        def combine(i, d=d, j=j):
            rows = pl.ds(pl.multiple_of(i * STRIP, STRIP), STRIP)
            value = (
                coef[j, 0:1, :] * cot[j, rows, :].astype(jnp.float32)
                + coef[j, 1:2, :] * cot_in[j, rows, :].astype(jnp.float32)
            ).astype(jnp.bfloat16)
            if d == 0:
                hg[y, rows, :] = value
            else:
                hg_send[j, rows, :] = value

        loop(OWN // STRIP, combine)
        if d:
            remote(Kind.hg, d, hg_send.at[j], hg.at[y], to_y[d]).start()

    def gathered(k):
        arrived(Kind.fwd_yp, k, xb.at[k, yo, 0])
        arrived(Kind.fwd_ym, k, xb.at[k, yo, 1])
        arrived(Kind.fwd_zp, k, wb.at[k, x, zo])
        arrived(Kind.fwd_zm, k, wb.at[k, 1 - x, zo])

    def add_block(k, b):
        pre[b] += lax.dot_general(
            xb[k, b].reshape(2 * OWN, CUT), wb[k].reshape(SPAN, CUT),
            (((1,), (1,)), ((), ())), preferred_element_type=jnp.float32,
        ).reshape(2, OWN, SPAN)

    def add_product(k):
        gathered(k)
        loop(4, lambda b: add_block(k, b))

    def clear(b):
        pre[b] = jnp.zeros((2, OWN, SPAN), jnp.float32)

    loop(4, clear)
    loop(CUTS - 1, add_product)
    gathered(CUTS - 1)

    for d in ORDER:
        b = (y + d) % 4
        add_block(CUTS - 1, b)
        remote(Kind.pre, d, pre.at[b, other], pre_in.at[b], to_sib).start()
    bias_sum[...] = jnp.zeros_like(bias_sum)

    def activate(d):
        b = (y + d) % 4
        arrived(Kind.pre, d, pre_in.at[b])
        if d:
            arrived(Kind.hg, 4 - d, hg.at[b])

        def act(i):
            rows = pl.ds(pl.multiple_of(i * STRIP, STRIP), STRIP)
            value = pre[b, c, rows, :] + pre_in[b, rows, :] + coef[y, 3:4, :]
            gate = jax.nn.sigmoid(value)
            hidden = (value * gate).astype(jnp.bfloat16)
            grad = (hg[b, rows, :].astype(jnp.float32) * gate * (1.0 + value * (1.0 - gate))).astype(jnp.bfloat16)
            pg[b, c, rows, :] = grad
            if d == 0:
                hid[y, rows, :] = hidden
            else:
                hid_send[b, rows, :] = hidden
            bias_sum[...] += jnp.sum(grad.astype(jnp.float32).reshape(STRIP // 8, 8, SPAN), 0)

        loop(OWN // STRIP, act)
        remote(Kind.pg, d, pg.at[b, c], pg.at[b, c], to_sib).start()
        if d:
            remote(Kind.hid, d, hid_send.at[b], hid.at[y], to_y[d]).start()

    def product_d(k, b):
        product = jnp.dot(
            pg[b].reshape(2 * OWN, SPAN), wb[k].reshape(SPAN, CUT), preferred_element_type=jnp.float32
        )
        return product.astype(jnp.bfloat16).reshape(2, OWN, CUT)

    def product_late(k, side):
        return jnp.dot(
            pgt[side].reshape(4 * OWN, SPAN), xb[k].reshape(SPAN, CUT), preferred_element_type=jnp.float32
        ).reshape(4, OWN, CUT)

    def product_g(k, v):
        product = jnp.dot(
            pgt[:, v].reshape(2 * OWN, SPAN), xb[k].reshape(SPAN, CUT), preferred_element_type=jnp.float32
        )
        return product.astype(jnp.bfloat16).reshape(2, OWN, CUT)

    def late_away(i):
        late_out[i] = product_late(EARLY + i, 1 - x).astype(jnp.bfloat16)
        remote(Kind.gb_x, i, late_out.at[i], late.at[i], to_x).start()

    def opposite_d(k):
        d_opp[k] = product_d(k, yo)
        remote(Kind.opp_yp, k, d_opp.at[k, 0], relay_yp.at[k], to_yp).start()
        remote(Kind.opp_ym, k, d_opp.at[k, 1], relay_ym.at[k], to_ym).start()

    def opposite_g(k):
        g_opp[k] = product_g(k, zo)
        remote(Kind.opp_zp, k, g_opp.at[k, 0], relay_zp.at[k], to_zp).start()
        remote(Kind.opp_zm, k, g_opp.at[k, 1], relay_zm.at[k], to_zm).start()

    for d in ORDER:
        activate(d)
    for d in ORDER:
        arrived(Kind.pg, d, pg.at[(y + d) % 4, other])
        if d == 2:
            loop(CUTS, opposite_d)

    wide = 256
    eye = (
        lax.broadcasted_iota(jnp.int32, (wide, wide), 0) == lax.broadcasted_iota(jnp.int32, (wide, wide), 1)
    ).astype(jnp.bfloat16)
    for o in range(SPAN // wide):
        flipped = lax.dot_general(
            eye, pg[:, :, :, o * wide : (o + 1) * wide].reshape(SPAN, wide),
            (((1,), (1,)), ((), ())), preferred_element_type=jnp.float32,
        )
        pgt[o // 2, (o % 2) * 2 : (o % 2) * 2 + 2] = flipped.astype(jnp.bfloat16).reshape(2, OWN, SPAN)
    loop(EARLY, opposite_g)
    arrived(Kind.hid, 0, hid.at[:3])
    for j in range(4):
        remote(Kind.tow, j, hid.at[j], hid_other.at[j], to_tower).start()
    loop(LATE, late_away)

    sent(Kind.x_sib, staged)
    sent(Kind.w_sib, wb.at[:CUTS, x, z, own_rows])
    for kind in (Kind.own_yp, Kind.own_ym, Kind.sib_yp, Kind.sib_ym, Kind.fwd_yp, Kind.fwd_ym):
        sent(kind, xb.at[:, y, 0])
    for kind in (Kind.w_x, Kind.own_zp, Kind.own_zm, Kind.pair_zp, Kind.pair_zm, Kind.fwd_zp, Kind.fwd_zm):
        sent(kind, every_w)
    sent(Kind.pre, pre_in)
    sent(Kind.hg, hg_send.at[:3])
    arrived(Kind.keep, 0, grouped.at[other])
    mix = hg_send

    def slot(k):
        return (k + CUTS) % (CUTS + 1)

    def g_keep(k):
        part = pl.ds(pl.multiple_of((k % (SPAN // CUT)) * CUT, CUT), CUT)
        block = k // (SPAN // CUT)
        return pre.at[block // 2, block % 2, :, part]

    def products(k):
        s = slot(k)

        def block_g(i):
            v = (zo + 1 + i) % 4
            wb[s, :, v] = product_g(k, v)

        def block_d(i):
            b = (yo + 1 + i) % 4
            xb[k, b] = product_d(k, b)

        pl.when(k < EARLY)(lambda: loop(3, block_g))
        loop(3, block_d)

    def late_in(i):
        k = EARLY + i
        arrived(Kind.gb_x, i, late.at[i])

        late[i] = (product_late(k, x) + late[i].astype(jnp.float32)).astype(jnp.bfloat16)
        remote(Kind.late_opp_zp, k, late.at[i, zo, TOP], relay_zp.at[k, TOP], to_zp).start()
        remote(Kind.late_opp_zm, k, late.at[i, zo, LOW], relay_zm.at[k, TOP], to_zm).start()

    def wide_sum(*terms):
        total = terms[0].astype(jnp.float32)
        for term in terms[1:]:
            total += term.astype(jnp.float32)
        return total

    def relays(k):
        arrived(Kind.opp_yp, k, relay_yp.at[k])
        xb[k, yp, 0] = wide_sum(xb[k, yp, 0], relay_yp[k]).astype(jnp.bfloat16)
        remote(Kind.sum_yp, k, xb.at[k, yp], part_yp.at[k], to_yp).start()
        arrived(Kind.opp_ym, k, relay_ym.at[k])
        xb[k, ym, 1] = wide_sum(xb[k, ym, 1], relay_ym[k]).astype(jnp.bfloat16)
        remote(Kind.sum_ym, k, xb.at[k, ym], part_ym.at[k], to_ym).start()
        pl.when(k < EARLY)(lambda: relays_z(k))
        pl.when(k >= EARLY)(lambda: relays_late(k))

    def relays_z(k):
        s = slot(k)
        arrived(Kind.opp_zp, k, relay_zp.at[k])
        wb[s, 0, zp] = wide_sum(wb[s, 0, zp], relay_zp[k]).astype(jnp.bfloat16)
        remote(Kind.sum_zp, k, wb.at[s, :, zp], part_zp.at[k], to_zp).start()
        arrived(Kind.opp_zm, k, relay_zm.at[k])
        wb[s, 1, zm] = wide_sum(wb[s, 1, zm], relay_zm[k]).astype(jnp.bfloat16)
        remote(Kind.sum_zm, k, wb.at[s, :, zm], part_zm.at[k], to_zm).start()

    def relays_late(k):
        i = k - EARLY
        arrived(Kind.late_opp_zp, k, relay_zp.at[k, TOP])
        late[i, zp, TOP] = wide_sum(late[i, zp, TOP], relay_zp[k, TOP]).astype(jnp.bfloat16)
        remote(Kind.late_sum_zp, k, late.at[i, zp], part_zp.at[k, 0], to_zp).start()
        arrived(Kind.late_opp_zm, k, relay_zm.at[k, TOP])
        late[i, zm, LOW] = wide_sum(late[i, zm, LOW], relay_zm[k, TOP]).astype(jnp.bfloat16)
        remote(Kind.late_sum_zm, k, late.at[i, zm], part_zm.at[k, 0], to_zm).start()

    def d_own(k):
        return local(Local.d, xb.at[k, y, c], feat_out.at[:, columns(c, k)])

    def d_sib(k):
        return remote(Kind.d_sib, k, xb.at[k, y, other], feat_out.at[:, columns(c, k)], to_sib)

    def g_own(k):
        return local(Local.g, g_keep(k).at[own_rows], grad_out.at[:, columns(c, k)])

    def g_sib(k):
        return remote(Kind.g_sib, k, g_keep(k).at[sib_rows], grad_out.at[:, columns(c, k)], to_sib)

    def sums_z(k):
        s = slot(k)
        arrived(Kind.sum_zp, k, part_zp.at[k])
        arrived(Kind.sum_zm, k, part_zm.at[k])
        g_send[k] = wide_sum(wb[s, 1 - x, z], part_zp[k, 1 - x], part_zm[k, 1 - x]).astype(jnp.bfloat16)
        remote(Kind.g_x, k, g_send.at[k], g_in.at[k], to_x).start()
        g_keep(k)[...] = wide_sum(wb[s, x, z], part_zp[k, x], part_zm[k, x])

    def sums_late(k):
        arrived(Kind.late_sum_zp, k, part_zp.at[k, 0])
        arrived(Kind.late_sum_zm, k, part_zm.at[k, 0])
        g_keep(k)[...] = wide_sum(late[k - EARLY, z], part_zp[k, 0], part_zm[k, 0])
        g_own(k).start()
        g_sib(k).start()

    def sums(k):
        pl.when(k < EARLY)(lambda: sums_z(k))
        pl.when(k >= EARLY)(lambda: sums_late(k))
        arrived(Kind.sum_yp, k, part_yp.at[k])
        arrived(Kind.sum_ym, k, part_ym.at[k])
        for core in range(2):
            total = wide_sum(xb[k, y, core], part_yp[k, core], part_ym[k, core])
            xb[k, y, core] = kept(total.astype(jnp.bfloat16), core, c, k)
        d_own(k).start()
        d_sib(k).start()

    def ends(k):
        arrived(Kind.g_x, k, g_in.at[k])
        g_keep(k)[...] += g_in[k].astype(jnp.float32)
        g_own(k).start()
        g_sib(k).start()

    def mixing():
        arrived(Kind.tow, 0, hid_other)
        for j in range(4):

            def strip(i, sums, j=j):
                rows = pl.ds(pl.multiple_of(i * STRIP, STRIP), STRIP)
                here = hid[j, rows, :].astype(jnp.float32)
                there = hid_other[j, rows, :].astype(jnp.float32)
                mix[j, rows, :] = (coef[j, 0:1, :] * here + coef[j, 2:3, :] * there).astype(jnp.bfloat16)
                up = cot[j, rows, :].astype(jnp.float32)
                return (
                    sums[0] + jnp.sum((up * here).reshape(STRIP // 8, 8, SPAN), 0),
                    sums[1] + jnp.sum((up * there).reshape(STRIP // 8, 8, SPAN), 0),
                )

            zero = jnp.zeros((8, SPAN), jnp.float32)
            here, there = lax.fori_loop(0, OWN // STRIP, strip, (zero, zero))
            here, there = jnp.sum(here, 0, keepdims=True), jnp.sum(there, 0, keepdims=True)
            for h in range(2):
                part = slice(h * SPAN // 2, (h + 1) * SPAN // 2)
                vec[h, j : j + 1, :] = jnp.where(t == 0, here[:, part], there[:, part])
                vec[h, 4 + j : 5 + j, :] = jnp.where(t == 0, there[:, part], here[:, part])
            local(Local.mix, mix.at[j], mixed_out.at[:, pl.ds(j * SPAN, SPAN)]).start()
        bias = jnp.sum(bias_sum[...], 0, keepdims=True)
        bias = jnp.where(lax.broadcasted_iota(jnp.int32, (8, SPAN), 0) == y, bias, 0.0)
        for h in range(2):
            vec[h, 8:16, :] = bias[:, h * SPAN // 2 : (h + 1) * SPAN // 2]
        remote(Kind.v_c, 0, vec.at[other], vec_c, to_sib).start()

    def over_cores():
        arrived(Kind.v_c, 0, vec_c)
        vec_x[...] = vec[c] + vec_c[...]
        remote(Kind.v_x, 0, vec_x, vec_xin, to_x).start()

    def over_x():
        arrived(Kind.v_x, 0, vec_xin)
        vec_z[z] = vec_x[...] + vec_xin[...]
        for d in range(1, 4):
            remote(Kind.v_z, d, vec_z.at[z], vec_z.at[z], to_z[d]).start()

    def over_z():
        arrived(Kind.v_z, 0, vec_z.at[:3])
        vec_y[y] = (vec_z[0] + vec_z[1]) + (vec_z[2] + vec_z[3])
        for d in range(1, 4):
            remote(Kind.v_y, d, vec_y.at[y], vec_y.at[y], to_y[d]).start()

    def over_y():
        arrived(Kind.v_y, 0, vec_y.at[:3])
        vec_t[c, t] = (vec_y[0] + vec_y[1]) + (vec_y[2] + vec_y[3])
        remote(Kind.v_t, 0, vec_t.at[c, t], vec_t.at[c, t], to_tower).start()

    def over_towers():
        arrived(Kind.v_t, 0, vec_t.at[c, 1 - t])
        remote(Kind.v_b, 0, vec_t.at[c], vec_t.at[c], to_sib).start()

    between = {
        3: (mixing, over_cores), 4: (lambda: late_in(0), over_x,), 6: (over_z,), 8: (over_y,), 9: (over_towers,),
    }

    def step(s):
        pl.when(s < CUTS)(lambda: products(s))
        pl.when(s < CUTS)(lambda: relays(s))
        pl.when((s >= 2) & (s < CUTS + 2))(lambda: sums(s - 2))
        pl.when((s >= 3) & (s < EARLY + 3))(lambda: ends(s - 3))
        for at, tasks in between.items():

            @pl.when(s == at)
            def _(tasks=tasks):
                for task in tasks:
                    task()

    loop(CUTS + 2, step)

    arrived(Kind.v_b, 0, vec_t.at[other])
    for j in range(4):
        for h in range(2):
            part = slice((2 * j + h) * SPAN // 2, (2 * j + h + 1) * SPAN // 2)
            for s in range(2):
                for u in range(2):
                    stitch_sum[s, u : u + 1, part] = vec_t[h, s, 4 * u + j : 4 * u + j + 1, :]
            bias_total[0:1, part] = vec_t[h, t, 8 + j : 9 + j, :]
    small_out = [local(Local.small, stitch_sum, stitch_out), local(Local.small_1, bias_total, bias_out)]
    for copy in small_out:
        copy.start()

    def landed(k):
        arrived(Kind.d_sib, k, feat_out.at[:, columns(other, k)])
        arrived(Kind.g_sib, k, grad_out.at[:, columns(other, k)])

    loop(CUTS, landed)
    sent(Kind.opp_yp, d_opp.at[:, 0])
    sent(Kind.opp_ym, d_opp.at[:, 0])
    sent(Kind.sum_yp, xb.at[:, y])
    sent(Kind.sum_ym, xb.at[:, y])
    sent(Kind.opp_zp, g_opp.at[:, 0])
    sent(Kind.opp_zm, g_opp.at[:, 0])
    sent(Kind.sum_zp, g_opp)
    sent(Kind.sum_zm, g_opp)
    sent(Kind.late_opp_zp, late.at[:, 0, TOP])
    sent(Kind.late_opp_zm, late.at[:, 0, TOP])
    sent(Kind.late_sum_zp, late.at[:, 0])
    sent(Kind.late_sum_zm, late.at[:, 0])
    sent(Kind.g_x, g_send.at[:EARLY])
    sent(Kind.gb_x, late_out)
    local(Local.d, xb.at[:, y, 0], xb.at[:, y, 0]).wait()
    sent(Kind.d_sib, xb.at[:, y, 0])
    half = grad_out.at[:, pl.ds(pl.multiple_of(c * HALF, HALF), HALF)]
    local(Local.g, half, half).wait()
    sent(Kind.g_sib, half)
    sent(Kind.cot, cot)
    sent(Kind.pg, pg.at[:, 0])
    sent(Kind.tow, hid)
    sent(Kind.hid, hid.at[:3])
    local(Local.mix, mix, mix).wait()
    sent(Kind.v_z, vec_z.at[:3])
    sent(Kind.v_y, vec_y.at[:3])
    sent(Kind.v_c, vec_c)
    sent(Kind.v_x, vec_x)
    sent(Kind.v_t, vec_c)
    sent(Kind.v_b, vec_t.at[c])
    sent(Kind.keep, grouped.at[c])
    for copy in small_out:
        copy.wait()


def towers(*operands):
    low, wide = jnp.bfloat16, jnp.float32
    scratch = [
        ((CUTS, 4, 2, OWN, CUT), low),
        ((CUTS + 1, 2, 4, OWN, CUT), low),
        ((4, 2, OWN, SPAN), wide),
        ((4, OWN, SPAN), wide),
        ((4, 2, OWN, SPAN), low),
        ((2, 4, OWN, SPAN), low),
        ((4, OWN, SPAN), low),
        ((4, OWN, SPAN), low),
        ((4, OWN, SPAN), low),
        ((4, OWN, SPAN), low),
        ((4, OWN, SPAN), low),
        ((4, OWN, SPAN), low),
        ((CUTS, 2, OWN, CUT), low),
        ((EARLY, 2, OWN, CUT), low),
        ((LATE, 4, OWN, CUT), low),
        ((LATE, 4, OWN, CUT), low),
        ((CUTS, OWN, CUT), low),
        ((CUTS, OWN, CUT), low),
        ((CUTS, 2, OWN, CUT), low),
        ((CUTS, 2, OWN, CUT), low),
        ((CUTS, OWN, CUT), low),
        ((CUTS, OWN, CUT), low),
        ((CUTS, 2, OWN, CUT), low),
        ((CUTS, 2, OWN, CUT), low),
        ((CUTS, OWN, CUT), low),
        ((CUTS, OWN, CUT), low),
        ((1, OWN), jnp.int32),
        ((1, FEAT), jnp.int32),
        ((2, 2, OUT), wide),
        ((1, OUT), wide),
        ((2, 2, OUT), wide),
        ((1, OUT), wide),
        ((2, OWN, OWN), low),
        ((1, FEAT), low),
        ((4, 8, SPAN), wide),
        ((8, SPAN), wide),
        ((2, 16, SPAN // 2), wide),
        ((16, SPAN // 2), wide),
        ((16, SPAN // 2), wide),
        ((16, SPAN // 2), wide),
        ((4, 16, SPAN // 2), wide),
        ((4, 16, SPAN // 2), wide),
        ((2, 2, 16, SPAN // 2), wide),
    ]
    anywhere = pl.BlockSpec(memory_space=pl.ANY)
    return pl.pallas_call(
        body,
        out_shape=[
            jax.ShapeDtypeStruct((OWN, OUT), low),
            jax.ShapeDtypeStruct((OWN, FEAT), low),
            jax.ShapeDtypeStruct((ROWS, FEAT), wide),
            jax.ShapeDtypeStruct((2, 2, OUT), wide),
            jax.ShapeDtypeStruct((1, OUT), wide),
        ],
        in_specs=[anywhere] * 7,
        out_specs=[anywhere] * 5,
        scratch_shapes=[pltpu.VMEM(shape, kind) for shape, kind in scratch]
        + [
            pltpu.SemaphoreType.DMA((len(Kind),)),
            pltpu.SemaphoreType.DMA((len(ROWED), CUTS)),
            pltpu.SemaphoreType.DMA((sum(FEW.values()),)),
            pltpu.SemaphoreType.DMA((CUTS,)),
            pltpu.SemaphoreType.DMA((len(Local),)),
        ],
        compiler_params=pltpu.CompilerParams(
            collective_id=0, has_side_effects=True, vmem_limit_bytes=60 * 1024 * 1024
        ),
    )(*operands)


def closing(
    mixed_in, feat_in, grad_in, stitch_in, bias_in, momentum, weights,
    mixed, feat, grad, stitch, bias, new_momentum, new_weights,
    mixed_here, feat_here, stitch_here, bias_here, grad_here, momentum_here, weights_here, result, sem,
):
    def pieces(row, count, src, dst):
        size = src.shape[0] // count
        return [
            pltpu.make_async_copy(src.at[pl.ds(i * size, size)], dst.at[pl.ds(i * size, size)], sem.at[row + i])
            for i in range(count)
        ]

    through = [
        (pieces(row, count, src, here), pieces(row + count, count, here, dst))
        for row, count, src, here, dst in (
            (0, 2, feat_in, feat_here, feat), (4, 2, mixed_in, mixed_here, mixed),
            (8, 1, stitch_in, stitch_here, stitch), (10, 1, bias_in, bias_here, bias),
        )
    ]
    for inward, _ in through:
        for copy in inward:
            copy.start()
    loads = list(zip(
        pieces(12, PARTS, grad_in, grad_here), pieces(12 + PARTS, PARTS, momentum, momentum_here),
        pieces(12 + 2 * PARTS, PARTS, weights, weights_here),
    ))
    for copies in loads:
        for copy in copies:
            copy.start()
    for inward, outward in through:
        for before, after in zip(inward, outward):
            before.wait()
            after.start()
    stores = list(zip(
        pieces(12 + 3 * PARTS, PARTS, grad_here, grad), pieces(12 + 4 * PARTS, PARTS, momentum_here, new_momentum),
        pieces(12 + 5 * PARTS, PARTS, result, new_weights),
    ))
    for i in range(PARTS):
        rows = slice(i * ROWS // PARTS, (i + 1) * ROWS // PARTS)
        loads[i][0].wait()
        stores[i][0].start()
        loads[i][1].wait()
        moved = momentum_rate * momentum_here[rows] + grad_here[rows]
        momentum_here[rows] = moved
        stores[i][1].start()
        loads[i][2].wait()
        result[rows] = weights_here[rows].astype(jnp.float32) - learn_rate * moved
        stores[i][2].start()
    for _, outward in through:
        for copy in outward:
            copy.wait()
    for copies in stores:
        for copy in copies:
            copy.wait()


def close(*operands):
    anywhere = pl.BlockSpec(memory_space=pl.ANY)
    passed, updated = operands[:5], operands[5]
    shapes = [jax.ShapeDtypeStruct(v.shape, v.dtype) for v in (*passed, updated, updated)]
    held = [*passed[:2], *passed[3:], passed[2], *operands[5:], updated]
    return pl.pallas_call(
        closing,
        out_shape=shapes,
        in_specs=[anywhere] * 7,
        out_specs=[anywhere] * 7,
        scratch_shapes=[pltpu.VMEM(v.shape, v.dtype) for v in held] + [pltpu.SemaphoreType.DMA((12 + 6 * PARTS,))],
        compiler_params=pltpu.CompilerParams(vmem_limit_bytes=60 * 1024 * 1024),
        cost_estimate=pl.CostEstimate(flops=0, bytes_accessed=20_000_000, transcendentals=0),
    )(*operands)


def shards(features, group, pad_mask, weights, bias, stitch, momentum, cotangent):
    sums = towers(features[0], weights[0], cotangent[0], group[None], pad_mask[None], stitch, bias)
    mixed, feat_grad, weight_grad, stitch_grad, bias_grad, new_momentum, new_weights = close(
        *sums, momentum[0], weights[0]
    )
    return (
        mixed[None], feat_grad[None], weight_grad[None], bias_grad, stitch_grad, new_momentum[None], new_weights[None]
    )


def solution(mesh):
    placed = (
        P("tower", "blk", None),
        P("blk"),
        P(),
        P("tower", "blk", None),
        P("tower", None),
        P(),
        P("tower", "blk", None),
        P("tower", "blk", None),
    )
    return jax.shard_map(
        shards,
        mesh=mesh,
        in_specs=placed,
        out_specs=(
            P("tower", "blk", None),
            P("tower", "blk", None),
            P("tower", "blk", None),
            P("tower", None),
            P(),
            P("tower", "blk", None),
            P("tower", "blk", None),
        ),
        check_vma=False,
    )
```

```python
import enum

import jax
import jax.numpy as jnp
from jax import lax
from jax.experimental import pallas as pl
from jax.experimental.pallas import tpu as pltpu
from jax.sharding import PartitionSpec as P

momentum_rate = 0.9
learn_rate = 0.0001

FEAT = 9216
OUT = 4096
HALF = FEAT // 2
OWN = 128
ROWS = 64
SPAN = 1024
CUT = 512
CUTS = HALF // CUT
LATE = 1
EARLY = CUTS - LATE
PARTS = 4
GRANT = 56 << 20
STRIP = 32
ORDER = (2, 1, 3, 0)


class Kind(enum.IntEnum):
    (
        x_sib, w_sib, w_x, own_yp, own_ym, own_zp, own_zm, pair_zp, pair_zm, sib_yp, sib_ym, fwd_yp, fwd_ym, fwd_zp, fwd_zm,
        opp_yp, opp_ym, opp_zp, opp_zm, sum_yp, sum_ym, sum_zp, sum_zm, g_x, d_sib, g_sib, late_opp_zp, late_opp_zm,
        late_sum_zp, late_sum_zm, keep, cot, hg, pre, pg, hid, tow, gb_x, v_c, v_x, v_z, v_y, v_t, v_b,
    ) = range(44)


class Local(enum.IntEnum):
    w, cot, d, g, small, small_1, small_2, small_3 = range(8)


ROWED = (
    Kind.x_sib, Kind.w_sib, Kind.w_x, Kind.own_yp, Kind.own_ym, Kind.own_zp, Kind.own_zm, Kind.pair_zp, Kind.pair_zm,
    Kind.sib_yp, Kind.sib_ym, Kind.fwd_yp, Kind.fwd_ym, Kind.fwd_zp, Kind.fwd_zm,
)
AGAIN = {
    Kind.opp_yp: Kind.own_yp, Kind.opp_ym: Kind.own_ym, Kind.opp_zp: Kind.own_zp, Kind.opp_zm: Kind.own_zm, Kind.sum_yp:
    Kind.pair_zp, Kind.sum_ym: Kind.pair_zm, Kind.sum_zp: Kind.x_sib, Kind.sum_zm: Kind.w_x, Kind.g_x: Kind.w_sib,
    Kind.d_sib: Kind.fwd_yp, Kind.g_sib: Kind.fwd_ym, Kind.late_opp_zp: Kind.own_zp, Kind.late_opp_zm: Kind.own_zm,
    Kind.late_sum_zp: Kind.x_sib, Kind.late_sum_zm: Kind.w_x,
}
FEW = {
    Kind.keep: 1, Kind.cot: 1, Kind.hg: 4, Kind.pre: 4, Kind.pg: 4, Kind.hid: 1, Kind.tow: 1, Kind.gb_x: LATE, Kind.v_c: 1,
    Kind.v_x: 1, Kind.v_z: 1, Kind.v_y: 1, Kind.v_t: 1, Kind.v_b: 1,
}
ROW = {kind: row for row, kind in enumerate(ROWED)}
ROW.update({kind: ROW[before] for kind, before in AGAIN.items()})
FIRST = {kind: sum(list(FEW.values())[:place]) for place, kind in enumerate(FEW)}


def body(
    features, weights, cotangent, group_in, pad_in, stitch_in, bias_in,
    mixed_out, feat_out, grad_out, vec_t,
    xb, wb, pre, pg, pgt, cot, cot_in, hg_send, hg, hid, d_opp, g_opp, late,
    relay_yp, relay_ym, part_yp, part_ym, relay_zp, relay_zm, part_zp, part_zm,
    g_send, g_in, group, pad, stitch, bias, grouped, absent, coef, bias_sum, vec, vec_c, vec_x, vec_xin, vec_z, vec_y,
    send_sem, row_sem, few_sem, load_sem, local_sem, room_sem,
):
    blk, t = lax.axis_index("blk"), lax.axis_index("tower")
    y, x, z, c = blk // 16, (blk // 8) % 2, (blk // 2) % 4, blk % 2
    other = 1 - c

    def place(y, x, z, c):
        return ((y * 2 + x) * 4 + z) * 2 + c

    yp, yo, ym = (y + 1) % 4, (y + 2) % 4, (y + 3) % 4
    zp, zo, zm = (z + 1) % 4, (z + 2) % 4, (z + 3) % 4
    to_yp, to_yo, to_ym = ((place(v, x, z, c), t) for v in (yp, yo, ym))
    to_zp, to_zo, to_zm = ((place(y, x, v, c), t) for v in (zp, zo, zm))
    to_x = (place(y, 1 - x, z, c), t)
    to_sib = (place(y, x, z, other), t)
    to_tower = (blk, 1 - t)
    to_y = (None, to_yp, to_yo, to_ym)
    to_z = (None, to_zp, to_zo, to_zm)

    def remote(kind, k, src, dst, device):
        if kind in ROW:
            landed = row_sem.at[ROW[kind], k]
        else:
            landed = few_sem.at[FIRST[kind] + (k if FEW[kind] > 1 else 0)]
        return pltpu.make_async_remote_copy(
            src_ref=src, dst_ref=dst, send_sem=send_sem.at[kind], recv_sem=landed,
            device_id=device, device_id_type=pl.DeviceIdType.MESH,
        )

    def arrived(kind, k, dst):
        remote(kind, k, dst, dst, to_sib).wait_recv()

    def sent(kind, src):
        remote(kind, 0, src, src, to_sib).wait_send()

    def local(kind, src, dst):
        return pltpu.make_async_copy(src, dst, local_sem.at[kind])

    def columns(side, k):
        return pl.ds(pl.multiple_of(side * HALF + k * CUT, CUT), CUT)

    def loop(count, step):
        lax.fori_loop(0, count, lambda k, carry: (step(k), carry)[1], 0)

    hid_other = hg
    late_out = hg_send.at[:, :, :CUT]
    hid_send = cot_in
    staged = g_send
    TOP, LOW = pl.ds(0, OWN // 2), pl.ds(OWN // 2, OWN // 2)
    own_rows = pl.ds(pl.multiple_of(c * ROWS, ROWS), ROWS)
    sib_rows = pl.ds(pl.multiple_of(other * ROWS, ROWS), ROWS)

    def load_x(k):
        return pltpu.make_async_copy(features.at[:, columns(c, k)], xb.at[k, y, c], load_sem.at[k])

    def load_other(k):
        return pltpu.make_async_copy(features.at[:, columns(other, k)], staged.at[k], load_sem.at[k])

    def load_w(k):
        return local(Local.w, weights.at[:, columns(c, k)], wb.at[k, x, z, own_rows])

    def start_loads(k):
        load_x(k).start()
        load_other(k).start()
        load_w(k).start()

    small = [
        local(Local.small + i, src, dst)
        for i, (src, dst) in enumerate(((group_in, group), (pad_in, pad), (stitch_in, stitch), (bias_in, bias)))
    ]
    for copy in small:
        copy.start()
    loop(CUTS, start_loads)
    for j in range(4):
        local(Local.cot, cotangent.at[:, pl.ds(j * SPAN, SPAN)], cot.at[j]).start()

    barrier = pltpu.get_barrier_semaphore()
    partners = (to_yp, to_yo, to_ym, to_zp, to_zo, to_zm, to_x, to_sib, to_tower)
    for device in partners:
        pl.semaphore_signal(barrier, inc=1, device_id=device, device_id_type=pl.DeviceIdType.MESH)

    for copy in small:
        copy.wait()
    grouped[c] = jnp.broadcast_to(group[...].astype(jnp.float32), (OWN, OWN)).T.astype(jnp.bfloat16)
    for j in range(4):
        part = slice(j * SPAN, (j + 1) * SPAN)
        coef[j, 0:1, :] = jnp.where(t == 0, stitch[0, 0:1, part], stitch[1, 1:2, part])
        coef[j, 1:2, :] = jnp.where(t == 0, stitch[1, 0:1, part], stitch[0, 1:2, part])
        coef[j, 2:3, :] = jnp.where(t == 0, stitch[0, 1:2, part], stitch[1, 0:1, part])
        coef[j, 3:4, :] = bias[0:1, part]

    absent[...] = 1.0 - pad[...].astype(jnp.float32).astype(jnp.bfloat16)

    def kept(value, core, side, k):
        rows = jnp.concatenate([grouped[core]] * (CUT // OWN), 1)
        return value * (1.0 - rows * absent[0:1, columns(side, k)])

    def masked(k):
        pltpu.make_async_copy(xb.at[k, y], xb.at[k, y], load_sem.at[k]).wait()
        staged[k] = kept(staged[k], c, other, k)
        xb[k, y, c] = kept(xb[k, y, c], c, c, k)

    masked(0)
    pl.semaphore_wait(barrier, len(partners))

    remote(Kind.keep, 0, grouped.at[c], grouped.at[c], to_sib).start()

    def x_sib(k):
        return remote(Kind.x_sib, k, staged.at[k], xb.at[k, y, c], to_sib)

    def w_sib(k):
        return remote(Kind.w_sib, k, weights.at[:, columns(other, k)], wb.at[k, x, z, own_rows], to_sib)

    def to_sibling(k):
        w_sib(k).start()
        pl.when(k > 0)(lambda: masked(k))
        x_sib(k).start()
        remote(Kind.own_yp, k, xb.at[k, y, c], xb.at[k, y, c], to_yp).start()
        remote(Kind.own_ym, k, xb.at[k, y, c], xb.at[k, y, c], to_ym).start()

    def own_out(k):
        arrived(Kind.x_sib, k, xb.at[k, y, other])
        remote(Kind.sib_yp, k, xb.at[k, y, other], xb.at[k, y, other], to_yp).start()
        remote(Kind.sib_ym, k, xb.at[k, y, other], xb.at[k, y, other], to_ym).start()
        arrived(Kind.w_sib, k, wb.at[k, x, z, sib_rows])
        remote(Kind.w_x, k, wb.at[k, x, z], wb.at[k, x, z], to_x).start()
        remote(Kind.own_zp, k, wb.at[k, x, z], wb.at[k, x, z], to_zp).start()
        remote(Kind.own_zm, k, wb.at[k, x, z], wb.at[k, x, z], to_zm).start()

    every_w = wb.at[:CUTS, x, z]

    def first(k):
        pl.when(k < CUTS)(lambda: to_sibling(k))

        @pl.when(k == 0)
        def _():
            every = wb.at[:CUTS, x, z, own_rows]
            local(Local.w, every, every).wait()

        pl.when(k >= 1)(lambda: own_out(k - 1))

    loop(CUTS + 1, first)
    for j in range(4):
        remote(Kind.cot, j, cotangent.at[:, pl.ds(j * SPAN, SPAN)], cot_in.at[j], to_tower).start()

    def pair_out(k):
        arrived(Kind.w_x, k, wb.at[k, 1 - x, z])
        remote(Kind.pair_zp, k, wb.at[k, 1 - x, z], wb.at[k, 1 - x, z], to_zp).start()
        remote(Kind.pair_zm, k, wb.at[k, 1 - x, z], wb.at[k, 1 - x, z], to_zm).start()

    loop(CUTS, pair_out)

    def forward(k):
        arrived(Kind.own_yp, k, xb.at[k, ym, c])
        arrived(Kind.sib_yp, k, xb.at[k, ym, other])
        remote(Kind.fwd_yp, k, xb.at[k, ym, 0], xb.at[k, ym, 0], to_yp).start()
        arrived(Kind.own_ym, k, xb.at[k, yp, c])
        arrived(Kind.sib_ym, k, xb.at[k, yp, other])
        remote(Kind.fwd_ym, k, xb.at[k, yp, 1], xb.at[k, yp, 1], to_ym).start()
        arrived(Kind.own_zp, k, wb.at[k, x, zm])
        remote(Kind.fwd_zp, k, wb.at[k, x, zm], wb.at[k, x, zm], to_zp).start()
        arrived(Kind.own_zm, k, wb.at[k, x, zp])
        arrived(Kind.pair_zp, k, wb.at[k, 1 - x, zm])
        arrived(Kind.pair_zm, k, wb.at[k, 1 - x, zp])
        remote(Kind.fwd_zm, k, wb.at[k, 1 - x, zp], wb.at[k, 1 - x, zp], to_zm).start()

    loop(CUTS, forward)

    local(Local.cot, cot, cot).wait()
    arrived(Kind.cot, 0, cot_in)
    for d in ORDER:
        j = (y + d) % 4

        def combine(i, d=d, j=j):
            rows = pl.ds(pl.multiple_of(i * STRIP, STRIP), STRIP)
            value = (
                coef[j, 0:1, :] * cot[j, rows, :].astype(jnp.float32)
                + coef[j, 1:2, :] * cot_in[j, rows, :].astype(jnp.float32)
            ).astype(jnp.bfloat16)
            if d == 0:
                hg[y, rows, :] = value
            else:
                hg_send[j, rows, :] = value

        loop(OWN // STRIP, combine)
        if d:
            remote(Kind.hg, d, hg_send.at[j], hg.at[y], to_y[d]).start()

    def pre_in(i):
        return grad_out.at[:, pl.ds(pl.multiple_of(i * SPAN, SPAN), SPAN)]

    def gathered(k):
        arrived(Kind.fwd_yp, k, xb.at[k, yo, 0])
        arrived(Kind.fwd_ym, k, xb.at[k, yo, 1])
        arrived(Kind.fwd_zp, k, wb.at[k, x, zo])
        arrived(Kind.fwd_zm, k, wb.at[k, 1 - x, zo])

    def add_block(k, b):
        pre[b] += lax.dot_general(
            xb[k, b].reshape(2 * OWN, CUT), wb[k].reshape(SPAN, CUT),
            (((1,), (1,)), ((), ())), preferred_element_type=jnp.float32,
        ).reshape(2, OWN, SPAN)

    def add_product(k):
        gathered(k)
        loop(4, lambda b: add_block(k, b))

    def clear(b):
        pre[b] = jnp.zeros((2, OWN, SPAN), jnp.float32)

    loop(4, clear)
    loop(CUTS - 1, add_product)
    gathered(CUTS - 1)

    for d in ORDER:
        b = (y + d) % 4
        add_block(CUTS - 1, b)
        for h in range(2):
            part = pl.ds(h * ROWS, ROWS)
            remote(Kind.pre, d, pre.at[b, other, part], pre_in(2 * d + h), to_sib).start()
    bias_sum[...] = jnp.zeros_like(bias_sum)

    def activate(d):
        b = (y + d) % 4
        arrived(Kind.pre, d, pre.at[b, other])
        if d:
            arrived(Kind.hg, 4 - d, hg.at[b])

        def act(i):
            rows = pl.ds(pl.multiple_of(i * STRIP, STRIP), STRIP)
            per = ROWS // STRIP
            rows_in = pl.ds(pl.multiple_of((i % per) * STRIP, STRIP), STRIP)
            value = pre[b, c, rows, :] + pre_in(2 * d + i // per)[rows_in, :] + coef[y, 3:4, :]
            gate = jax.nn.sigmoid(value)
            hidden = (value * gate).astype(jnp.bfloat16)
            grad = (hg[b, rows, :].astype(jnp.float32) * gate * (1.0 + value * (1.0 - gate))).astype(jnp.bfloat16)
            pg[b, c, rows, :] = grad
            if d == 0:
                hid[y, rows, :] = hidden
            else:
                hid_send[b, rows, :] = hidden
            bias_sum[...] += jnp.sum(grad.astype(jnp.float32).reshape(STRIP // 8, 8, SPAN), 0)

        loop(OWN // STRIP, act)
        remote(Kind.pg, d, pg.at[b, c], pg.at[b, c], to_sib).start()
        if d:
            remote(Kind.hid, d, hid_send.at[b], hid.at[y], to_y[d]).start()

    def product_d(k, b):
        product = jnp.dot(
            pg[b].reshape(2 * OWN, SPAN), wb[k].reshape(SPAN, CUT), preferred_element_type=jnp.float32
        )
        return product.astype(jnp.bfloat16).reshape(2, OWN, CUT)

    def product_late(k, side):
        return jnp.dot(
            pgt[side].reshape(4 * OWN, SPAN), xb[k].reshape(SPAN, CUT), preferred_element_type=jnp.float32
        ).reshape(4, OWN, CUT)

    def product_g(k, v):
        product = jnp.dot(
            pgt[:, v].reshape(2 * OWN, SPAN), xb[k].reshape(SPAN, CUT), preferred_element_type=jnp.float32
        )
        return product.astype(jnp.bfloat16).reshape(2, OWN, CUT)

    def late_away(i):
        late_out[...] = product_late(EARLY + i, 1 - x).astype(jnp.bfloat16)
        remote(Kind.gb_x, i, late_out, late.at[i], to_x).start()

    def opposite_d(k):
        d_opp[k] = product_d(k, yo)
        remote(Kind.opp_yp, k, d_opp.at[k, 0], relay_yp.at[k], to_yp).start()
        remote(Kind.opp_ym, k, d_opp.at[k, 1], relay_ym.at[k], to_ym).start()

    def opposite_g(k):
        g_opp[k] = product_g(k, zo)
        remote(Kind.opp_zp, k, g_opp.at[k, 0], relay_zp.at[k], to_zp).start()
        remote(Kind.opp_zm, k, g_opp.at[k, 1], relay_zm.at[k], to_zm).start()

    for d in ORDER:
        activate(d)
    pl.semaphore_signal(room_sem, inc=1, device_id=to_tower, device_id_type=pl.DeviceIdType.MESH)
    for d in ORDER:
        arrived(Kind.pg, d, pg.at[(y + d) % 4, other])
        if d == 2:
            loop(CUTS, opposite_d)

    wide = 256
    eye = (
        lax.broadcasted_iota(jnp.int32, (wide, wide), 0) == lax.broadcasted_iota(jnp.int32, (wide, wide), 1)
    ).astype(jnp.bfloat16)
    for o in range(SPAN // wide):
        flipped = lax.dot_general(
            eye, pg[:, :, :, o * wide : (o + 1) * wide].reshape(SPAN, wide),
            (((1,), (1,)), ((), ())), preferred_element_type=jnp.float32,
        )
        pgt[o // 2, (o % 2) * 2 : (o % 2) * 2 + 2] = flipped.astype(jnp.bfloat16).reshape(2, OWN, SPAN)
    loop(EARLY, opposite_g)
    arrived(Kind.hid, 0, hid.at[:3])
    pl.semaphore_wait(room_sem, 1)
    for j in range(4):
        remote(Kind.tow, j, hid.at[j], hid_other.at[j], to_tower).start()
    sent(Kind.hg, hg_send.at[:3])
    loop(LATE, late_away)

    sent(Kind.x_sib, staged)
    sent(Kind.w_sib, wb.at[:CUTS, x, z, own_rows])
    for kind in (Kind.own_yp, Kind.own_ym, Kind.sib_yp, Kind.sib_ym, Kind.fwd_yp, Kind.fwd_ym):
        sent(kind, xb.at[:, y, 0])
    for kind in (Kind.w_x, Kind.own_zp, Kind.own_zm, Kind.pair_zp, Kind.pair_zm, Kind.fwd_zp, Kind.fwd_zm):
        sent(kind, every_w)
    sent(Kind.pre, pre.at[:, other])
    arrived(Kind.keep, 0, grouped.at[other])

    def slot(k):
        return (k + CUTS) % (CUTS + 1)

    def g_keep(k):
        part = pl.ds(pl.multiple_of((k % (SPAN // CUT)) * CUT, CUT), CUT)
        block = k // (SPAN // CUT)
        return pre.at[block // 2, block % 2, :, part]

    def products(k):
        s = slot(k)

        def block_g(i):
            v = (zo + 1 + i) % 4
            wb[s, :, v] = product_g(k, v)

        def block_d(i):
            b = (yo + 1 + i) % 4
            xb[k, b] = product_d(k, b)

        pl.when(k < EARLY)(lambda: loop(3, block_g))
        loop(3, block_d)

    def late_in(i):
        k = EARLY + i
        arrived(Kind.gb_x, i, late.at[i])

        late[i] = (product_late(k, x) + late[i].astype(jnp.float32)).astype(jnp.bfloat16)
        remote(Kind.late_opp_zp, k, late.at[i, zo, TOP], relay_zp.at[k, TOP], to_zp).start()
        remote(Kind.late_opp_zm, k, late.at[i, zo, LOW], relay_zm.at[k, TOP], to_zm).start()

    def wide_sum(*terms):
        total = terms[0].astype(jnp.float32)
        for term in terms[1:]:
            total += term.astype(jnp.float32)
        return total

    def relays(k):
        arrived(Kind.opp_yp, k, relay_yp.at[k])
        xb[k, yp, 0] = wide_sum(xb[k, yp, 0], relay_yp[k]).astype(jnp.bfloat16)
        remote(Kind.sum_yp, k, xb.at[k, yp], part_yp.at[k], to_yp).start()
        arrived(Kind.opp_ym, k, relay_ym.at[k])
        xb[k, ym, 1] = wide_sum(xb[k, ym, 1], relay_ym[k]).astype(jnp.bfloat16)
        remote(Kind.sum_ym, k, xb.at[k, ym], part_ym.at[k], to_ym).start()
        pl.when(k < EARLY)(lambda: relays_z(k))
        pl.when(k >= EARLY)(lambda: relays_late(k))

    def relays_z(k):
        s = slot(k)
        arrived(Kind.opp_zp, k, relay_zp.at[k])
        wb[s, 0, zp] = wide_sum(wb[s, 0, zp], relay_zp[k]).astype(jnp.bfloat16)
        remote(Kind.sum_zp, k, wb.at[s, :, zp], part_zp.at[k], to_zp).start()
        arrived(Kind.opp_zm, k, relay_zm.at[k])
        wb[s, 1, zm] = wide_sum(wb[s, 1, zm], relay_zm[k]).astype(jnp.bfloat16)
        remote(Kind.sum_zm, k, wb.at[s, :, zm], part_zm.at[k], to_zm).start()

    def relays_late(k):
        i = k - EARLY
        arrived(Kind.late_opp_zp, k, relay_zp.at[k, TOP])
        late[i, zp, TOP] = wide_sum(late[i, zp, TOP], relay_zp[k, TOP]).astype(jnp.bfloat16)
        remote(Kind.late_sum_zp, k, late.at[i, zp], part_zp.at[k, 0], to_zp).start()
        arrived(Kind.late_opp_zm, k, relay_zm.at[k, TOP])
        late[i, zm, LOW] = wide_sum(late[i, zm, LOW], relay_zm[k, TOP]).astype(jnp.bfloat16)
        remote(Kind.late_sum_zm, k, late.at[i, zm], part_zm.at[k, 0], to_zm).start()

    def d_own(k):
        return local(Local.d, xb.at[k, y, c], feat_out.at[:, columns(c, k)])

    def d_sib(k):
        return remote(Kind.d_sib, k, xb.at[k, y, other], feat_out.at[:, columns(c, k)], to_sib)

    def g_own(k):
        return local(Local.g, g_keep(k).at[own_rows], grad_out.at[:, columns(c, k)])

    def g_sib(k):
        return remote(Kind.g_sib, k, g_keep(k).at[sib_rows], grad_out.at[:, columns(c, k)], to_sib)

    def sums_z(k):
        s = slot(k)
        arrived(Kind.sum_zp, k, part_zp.at[k])
        arrived(Kind.sum_zm, k, part_zm.at[k])
        g_send[k] = wide_sum(wb[s, 1 - x, z], part_zp[k, 1 - x], part_zm[k, 1 - x]).astype(jnp.bfloat16)
        remote(Kind.g_x, k, g_send.at[k], g_in.at[k], to_x).start()
        g_keep(k)[...] = wide_sum(wb[s, x, z], part_zp[k, x], part_zm[k, x])

    def sums_late(k):
        arrived(Kind.late_sum_zp, k, part_zp.at[k, 0])
        arrived(Kind.late_sum_zm, k, part_zm.at[k, 0])
        g_keep(k)[...] = wide_sum(late[k - EARLY, z], part_zp[k, 0], part_zm[k, 0])
        g_own(k).start()
        g_sib(k).start()

    def sums(k):
        pl.when(k < EARLY)(lambda: sums_z(k))
        pl.when(k >= EARLY)(lambda: sums_late(k))
        arrived(Kind.sum_yp, k, part_yp.at[k])
        arrived(Kind.sum_ym, k, part_ym.at[k])
        for core in range(2):
            total = wide_sum(xb[k, y, core], part_yp[k, core], part_ym[k, core])
            xb[k, y, core] = kept(total.astype(jnp.bfloat16), core, c, k)
        d_own(k).start()
        d_sib(k).start()

    def ends(k):
        arrived(Kind.g_x, k, g_in.at[k])
        g_keep(k)[...] += g_in[k].astype(jnp.float32)
        g_own(k).start()
        g_sib(k).start()

    def mixing():
        arrived(Kind.tow, 0, hid_other)
        for j in range(4):

            def strip(i, sums, j=j):
                rows = pl.ds(pl.multiple_of(i * STRIP, STRIP), STRIP)
                here = hid[j, rows, :].astype(jnp.float32)
                there = hid_other[j, rows, :].astype(jnp.float32)
                mixed_out[rows, j * SPAN : (j + 1) * SPAN] = (coef[j, 0:1, :] * here + coef[j, 2:3, :] * there).astype(jnp.bfloat16)
                up = cot[j, rows, :].astype(jnp.float32)
                return (
                    sums[0] + jnp.sum((up * here).reshape(STRIP // 8, 8, SPAN), 0),
                    sums[1] + jnp.sum((up * there).reshape(STRIP // 8, 8, SPAN), 0),
                )

            zero = jnp.zeros((8, SPAN), jnp.float32)
            here, there = lax.fori_loop(0, OWN // STRIP, strip, (zero, zero))
            here, there = jnp.sum(here, 0, keepdims=True), jnp.sum(there, 0, keepdims=True)
            for h in range(2):
                part = slice(h * SPAN // 2, (h + 1) * SPAN // 2)
                vec[h, j : j + 1, :] = jnp.where(t == 0, here[:, part], there[:, part])
                vec[h, 4 + j : 5 + j, :] = jnp.where(t == 0, there[:, part], here[:, part])
        bias = jnp.sum(bias_sum[...], 0, keepdims=True)
        bias = jnp.where(lax.broadcasted_iota(jnp.int32, (8, SPAN), 0) == y, bias, 0.0)
        for h in range(2):
            vec[h, 8:16, :] = bias[:, h * SPAN // 2 : (h + 1) * SPAN // 2]
        remote(Kind.v_c, 0, vec.at[other], vec_c, to_sib).start()

    def over_cores():
        arrived(Kind.v_c, 0, vec_c)
        vec_x[...] = vec[c] + vec_c[...]
        remote(Kind.v_x, 0, vec_x, vec_xin, to_x).start()

    def over_x():
        arrived(Kind.v_x, 0, vec_xin)
        vec_z[z] = vec_x[...] + vec_xin[...]
        for d in range(1, 4):
            remote(Kind.v_z, d, vec_z.at[z], vec_z.at[z], to_z[d]).start()

    def over_z():
        arrived(Kind.v_z, 0, vec_z.at[:3])
        vec_y[y] = (vec_z[0] + vec_z[1]) + (vec_z[2] + vec_z[3])
        for d in range(1, 4):
            remote(Kind.v_y, d, vec_y.at[y], vec_y.at[y], to_y[d]).start()

    def over_y():
        arrived(Kind.v_y, 0, vec_y.at[:3])
        vec_t[c, t] = (vec_y[0] + vec_y[1]) + (vec_y[2] + vec_y[3])
        remote(Kind.v_t, 0, vec_t.at[c, t], vec_t.at[c, t], to_tower).start()

    def over_towers():
        arrived(Kind.v_t, 0, vec_t.at[c, 1 - t])
        remote(Kind.v_b, 0, vec_t.at[c], vec_t.at[c], to_sib).start()

    between = {
        3: (mixing, over_cores), 4: (lambda: late_in(0), over_x,), 6: (over_z,), 8: (over_y,), 9: (over_towers,),
    }

    def step(s):
        pl.when(s < CUTS)(lambda: products(s))
        pl.when(s < CUTS)(lambda: relays(s))
        pl.when((s >= 2) & (s < CUTS + 2))(lambda: sums(s - 2))
        pl.when((s >= 3) & (s < EARLY + 3))(lambda: ends(s - 3))
        for at, tasks in between.items():

            @pl.when(s == at)
            def _(tasks=tasks):
                for task in tasks:
                    task()

    loop(CUTS + 2, step)

    arrived(Kind.v_b, 0, vec_t.at[other])

    def landed(k):
        arrived(Kind.d_sib, k, feat_out.at[:, columns(other, k)])
        arrived(Kind.g_sib, k, grad_out.at[:, columns(other, k)])

    loop(CUTS, landed)
    sent(Kind.opp_yp, d_opp.at[:, 0])
    sent(Kind.opp_ym, d_opp.at[:, 0])
    sent(Kind.sum_yp, xb.at[:, y])
    sent(Kind.sum_ym, xb.at[:, y])
    sent(Kind.opp_zp, g_opp.at[:, 0])
    sent(Kind.opp_zm, g_opp.at[:, 0])
    sent(Kind.sum_zp, g_opp)
    sent(Kind.sum_zm, g_opp)
    sent(Kind.late_opp_zp, late.at[:, 0, TOP])
    sent(Kind.late_opp_zm, late.at[:, 0, TOP])
    sent(Kind.late_sum_zp, late.at[:, 0])
    sent(Kind.late_sum_zm, late.at[:, 0])
    sent(Kind.g_x, g_send.at[:EARLY])
    sent(Kind.gb_x, late_out)
    local(Local.d, xb.at[:, y, 0], xb.at[:, y, 0]).wait()
    sent(Kind.d_sib, xb.at[:, y, 0])
    half = grad_out.at[:, pl.ds(pl.multiple_of(c * HALF, HALF), HALF)]
    local(Local.g, half, half).wait()
    sent(Kind.g_sib, half)
    sent(Kind.cot, cot)
    sent(Kind.pg, pg.at[:, 0])
    sent(Kind.tow, hid)
    sent(Kind.hid, hid.at[:3])
    sent(Kind.v_z, vec_z.at[:3])
    sent(Kind.v_y, vec_y.at[:3])
    sent(Kind.v_c, vec_c)
    sent(Kind.v_x, vec_x)
    sent(Kind.v_t, vec_c)
    sent(Kind.v_b, vec_t.at[c])
    sent(Kind.keep, grouped.at[c])


def towers(*operands):
    low, wide = jnp.bfloat16, jnp.float32
    scratch = [
        ((CUTS, 4, 2, OWN, CUT), low),
        ((CUTS + 1, 2, 4, OWN, CUT), low),
        ((4, 2, OWN, SPAN), wide),
        ((4, 2, OWN, SPAN), low),
        ((2, 4, OWN, SPAN), low),
        ((4, OWN, SPAN), low),
        ((4, OWN, SPAN), low),
        ((4, OWN, SPAN), low),
        ((4, OWN, SPAN), low),
        ((4, OWN, SPAN), low),
        ((CUTS, 2, OWN, CUT), low),
        ((EARLY, 2, OWN, CUT), low),
        ((LATE, 4, OWN, CUT), low),
        ((CUTS, OWN, CUT), low),
        ((CUTS, OWN, CUT), low),
        ((CUTS, 2, OWN, CUT), low),
        ((CUTS, 2, OWN, CUT), low),
        ((CUTS, OWN, CUT), low),
        ((CUTS, OWN, CUT), low),
        ((CUTS, 2, OWN, CUT), low),
        ((CUTS, 2, OWN, CUT), low),
        ((CUTS, OWN, CUT), low),
        ((CUTS, OWN, CUT), low),
        ((1, OWN), jnp.int32),
        ((1, FEAT), jnp.int32),
        ((2, 2, OUT), wide),
        ((1, OUT), wide),
        ((2, OWN, OWN), low),
        ((1, FEAT), low),
        ((4, 8, SPAN), wide),
        ((8, SPAN), wide),
        ((2, 16, SPAN // 2), wide),
        ((16, SPAN // 2), wide),
        ((16, SPAN // 2), wide),
        ((16, SPAN // 2), wide),
        ((4, 16, SPAN // 2), wide),
        ((4, 16, SPAN // 2), wide),
    ]
    anywhere, near = pl.BlockSpec(memory_space=pl.ANY), pl.BlockSpec(memory_space=pltpu.VMEM)
    return pl.pallas_call(
        body,
        out_shape=[
            pltpu.VMEM((OWN, OUT), low),
            pltpu.VMEM((OWN, FEAT), low),
            pltpu.VMEM((ROWS, FEAT), wide),
            pltpu.VMEM((2, 2, 16, SPAN // 2), wide),
        ],
        in_specs=[anywhere] * 7,
        out_specs=[near] * 4,
        scratch_shapes=[pltpu.VMEM(shape, kind) for shape, kind in scratch]
        + [
            pltpu.SemaphoreType.DMA((len(Kind),)),
            pltpu.SemaphoreType.DMA((len(ROWED), CUTS)),
            pltpu.SemaphoreType.DMA((sum(FEW.values()),)),
            pltpu.SemaphoreType.DMA((CUTS,)),
            pltpu.SemaphoreType.DMA((len(Local),)),
            pltpu.SemaphoreType.REGULAR,
        ],
        compiler_params=pltpu.CompilerParams(
            collective_id=0, has_side_effects=True, vmem_limit_bytes=GRANT
        ),
    )(*operands)


def closing(
    mixed_in, feat_in, grad_in, vec_in, momentum, weights,
    mixed, feat, grad, stitch, bias, new_momentum, new_weights,
    stitch_here, bias_here, weights_here, moved, result, sem,
):
    t = lax.axis_index("tower")
    started = []

    def start(count, src, dst):
        size = src.shape[0] // count
        for i in range(count):
            first = len(started)
            part = pl.ds(i * size, size)
            started.append(pltpu.make_async_copy(src.at[part], dst.at[part], sem.at[first]))
            started[-1].start()
        return started[-count:]

    loads = start(PARTS, weights, weights_here)
    start(PARTS, grad_in, grad)
    start(2, feat_in, feat)
    start(2, mixed_in, mixed)
    size = ROWS // PARTS
    for i in range(PARTS):
        rows = pl.ds(i * size, size)
        moved[rows] = momentum_rate * momentum[rows] + grad_in[rows]
        start(1, moved.at[rows], new_momentum.at[rows])
        loads[i].wait()
        result[rows] = weights_here[rows].astype(jnp.float32) - learn_rate * moved[rows]
        start(1, result.at[rows], new_weights.at[rows])
    for j in range(4):
        for h in range(2):
            part = slice((2 * j + h) * SPAN // 2, (2 * j + h + 1) * SPAN // 2)
            for s in range(2):
                for u in range(2):
                    stitch_here[s, u : u + 1, part] = vec_in[h, s, 4 * u + j : 4 * u + j + 1, :]
            bias_here[0:1, part] = vec_in[h, t, 8 + j : 9 + j, :]
    start(1, stitch_here, stitch)
    start(1, bias_here, bias)
    for copy in started[PARTS:]:
        copy.wait()


def close(mixed, feat, grad, vec, momentum, weights):
    anywhere, near = pl.BlockSpec(memory_space=pl.ANY), pl.BlockSpec(memory_space=pltpu.VMEM)
    small = [jax.ShapeDtypeStruct((2, 2, OUT), jnp.float32), jax.ShapeDtypeStruct((1, OUT), jnp.float32)]
    shapes = [*(jax.ShapeDtypeStruct(v.shape, v.dtype) for v in (mixed, feat, grad)), *small]
    shapes += [jax.ShapeDtypeStruct(grad.shape, grad.dtype)] * 2
    kept_near = [pltpu.with_memory_space_constraint(v, pltpu.VMEM) for v in (mixed, feat, grad, vec, momentum)]
    return pl.pallas_call(
        closing,
        out_shape=shapes,
        in_specs=[near] * 5 + [anywhere],
        out_specs=[anywhere] * 7,
        scratch_shapes=[pltpu.VMEM(v.shape, v.dtype) for v in (*small, weights, grad, grad)]
        + [pltpu.SemaphoreType.DMA((4 * PARTS + 6,))],
        compiler_params=pltpu.CompilerParams(vmem_limit_bytes=GRANT),
        cost_estimate=pl.CostEstimate(flops=0, bytes_accessed=14_000_000, transcendentals=0),
    )(*kept_near, weights)


def shards(features, group, pad_mask, weights, bias, stitch, momentum, cotangent):
    sums = towers(features[0], weights[0], cotangent[0], group[None], pad_mask[None], stitch, bias)
    mixed, feat_grad, weight_grad, stitch_grad, bias_grad, new_momentum, new_weights = close(
        *sums, momentum[0], weights[0]
    )
    return (
        mixed[None], feat_grad[None], weight_grad[None], bias_grad, stitch_grad, new_momentum[None], new_weights[None]
    )


def solution(mesh):
    placed = (
        P("tower", "blk", None),
        P("blk"),
        P(),
        P("tower", "blk", None),
        P("tower", None),
        P(),
        P("tower", "blk", None),
        P("tower", "blk", None),
    )
    return jax.shard_map(
        shards,
        mesh=mesh,
        in_specs=placed,
        out_specs=(
            P("tower", "blk", None),
            P("tower", "blk", None),
            P("tower", "blk", None),
            P("tower", None),
            P(),
            P("tower", "blk", None),
            P("tower", "blk", None),
        ),
        check_vma=False,
    )
```

```python
import enum

import jax
import jax.numpy as jnp
from jax import lax
from jax.experimental import pallas as pl
from jax.experimental.pallas import tpu as pltpu
from jax.sharding import PartitionSpec as P

momentum_rate = 0.9
learn_rate = 0.0001

FEAT = 9216
OUT = 4096
HALF = FEAT // 2
OWN = 128
ROWS = 64
SPAN = 1024
CUT = 512
CUTS = HALF // CUT
LATE = 1
EARLY = CUTS - LATE
PARTS = 4
GRANT = 56 << 20
STRIP = 32
ORDER = (2, 1, 3, 0)


class Kind(enum.IntEnum):
    (
        x_sib, w_sib, w_x, own_yp, own_ym, own_zp, own_zm, pair_zp, pair_zm, sib_yp, sib_ym, fwd_yp, fwd_ym, fwd_zp, fwd_zm,
        opp_yp, opp_ym, opp_zp, opp_zm, sum_yp, sum_ym, sum_zp, sum_zm, g_x, d_sib, g_sib, late_opp_zp, late_opp_zm,
        late_sum_zp, late_sum_zm, keep, cot, hg, pre, pg, hid, tow, gb_x, v_c, v_x, v_z, v_y, v_t, v_b,
    ) = range(44)


class Local(enum.IntEnum):
    w, cot, small, small_1, small_2, small_3 = range(6)


ROWED = (
    (Kind.x_sib, Kind.w_sib, Kind.g_x),
    (Kind.w_x, Kind.sum_zp, Kind.sum_zm, Kind.late_sum_zp, Kind.late_sum_zm),
    (Kind.own_yp, Kind.sib_yp, Kind.opp_yp),
    (Kind.own_ym, Kind.sib_ym, Kind.opp_ym),
    (Kind.own_zp, Kind.pair_zp, Kind.opp_zp, Kind.late_opp_zp),
    (Kind.own_zm, Kind.pair_zm, Kind.opp_zm, Kind.late_opp_zm),
    (Kind.fwd_yp, Kind.fwd_ym, Kind.fwd_zp, Kind.fwd_zm, Kind.sum_yp, Kind.sum_ym),
)
ROW = {kind: row for row, kinds in enumerate(ROWED) for kind in kinds}
FEW = {
    Kind.keep: 1, Kind.cot: 1, Kind.hg: 4, Kind.pre: 4, Kind.pg: 4, Kind.hid: 1, Kind.tow: 1, Kind.gb_x: LATE, Kind.v_c: 1,
    Kind.v_x: 1, Kind.v_z: 1, Kind.v_y: 1, Kind.v_t: 1, Kind.v_b: 1, Kind.d_sib: 1, Kind.g_sib: 1,
}
FIRST = {kind: sum(list(FEW.values())[:place]) for place, kind in enumerate(FEW)}
TOGETHER = (
    (Kind.own_yp, Kind.own_ym, Kind.sib_yp, Kind.sib_ym, Kind.fwd_yp, Kind.fwd_ym),
    (
        Kind.own_zp, Kind.own_zm, Kind.pair_zp, Kind.pair_zm, Kind.fwd_zp, Kind.fwd_zm, Kind.w_x, Kind.x_sib,
    ),
    (Kind.opp_yp, Kind.opp_ym),
    (Kind.sum_yp, Kind.sum_ym),
    (Kind.opp_zp, Kind.opp_zm),
    (Kind.sum_zp, Kind.sum_zm),
    (Kind.late_opp_zp, Kind.late_opp_zm),
    (Kind.late_sum_zp, Kind.late_sum_zm),
)
LEAVES = {kind: group for group, kinds in enumerate(TOGETHER) for kind in kinds}
for _kind in Kind:
    LEAVES.setdefault(_kind, len(set(LEAVES.values())))


def body(
    features, weights, cotangent, group_in, pad_in, stitch_in, bias_in,
    mixed_out, feat_out, grad_out, vec_t,
    xb, wb, pre, pg, pgt, cot, cot_in, hg_send, hg, hid, d_opp, g_opp, late,
    relay_yp, relay_ym, part_yp, part_ym, relay_zp, relay_zm, part_zp, part_zm,
    g_send, g_in, group, pad, stitch, bias, grouped, absent, coef, bias_sum, vec, vec_c, vec_x, vec_xin, vec_z, vec_y,
    send_sem, row_sem, few_sem, load_sem, local_sem, room_sem,
):
    blk, t = lax.axis_index("blk"), lax.axis_index("tower")
    y, x, z, c = blk // 16, (blk // 8) % 2, (blk // 2) % 4, blk % 2
    other = 1 - c

    def place(y, x, z, c):
        return ((y * 2 + x) * 4 + z) * 2 + c

    yp, yo, ym = (y + 1) % 4, (y + 2) % 4, (y + 3) % 4
    zp, zo, zm = (z + 1) % 4, (z + 2) % 4, (z + 3) % 4
    to_yp, to_yo, to_ym = ((place(v, x, z, c), t) for v in (yp, yo, ym))
    to_zp, to_zo, to_zm = ((place(y, x, v, c), t) for v in (zp, zo, zm))
    to_x = (place(y, 1 - x, z, c), t)
    to_sib = (place(y, x, z, other), t)
    to_tower = (blk, 1 - t)
    to_y = (None, to_yp, to_yo, to_ym)
    to_z = (None, to_zp, to_zo, to_zm)

    def remote(kind, k, src, dst, device):
        if kind in ROW:
            landed = row_sem.at[ROW[kind], k]
        else:
            landed = few_sem.at[FIRST[kind] + (k if FEW[kind] > 1 else 0)]
        return pltpu.make_async_remote_copy(
            src_ref=src, dst_ref=dst, send_sem=send_sem.at[LEAVES[kind]], recv_sem=landed,
            device_id=device, device_id_type=pl.DeviceIdType.MESH,
        )

    def arrived(kind, k, dst):
        remote(kind, k, dst, dst, to_sib).wait_recv()

    def sent(kind, src):
        remote(kind, 0, src, src, to_sib).wait_send()

    def local(kind, src, dst):
        return pltpu.make_async_copy(src, dst, local_sem.at[kind])

    def columns(side, k):
        return pl.ds(pl.multiple_of(side * HALF + k * CUT, CUT), CUT)

    def loop(count, step):
        lax.fori_loop(0, count, lambda k, carry: (step(k), carry)[1], 0)

    hid_other = hg
    late_out = hg_send.at[:, :, :CUT]
    hid_send = cot_in
    staged = g_send
    TOP, LOW = pl.ds(0, OWN // 2), pl.ds(OWN // 2, OWN // 2)
    own_rows = pl.ds(pl.multiple_of(c * ROWS, ROWS), ROWS)
    sib_rows = pl.ds(pl.multiple_of(other * ROWS, ROWS), ROWS)

    def load_x(k):
        return pltpu.make_async_copy(features.at[:, columns(c, k)], xb.at[k, y, c], load_sem.at[k])

    def load_other(k):
        return pltpu.make_async_copy(features.at[:, columns(other, k)], staged.at[k], load_sem.at[k])

    def load_w(k):
        return local(Local.w, weights.at[:, columns(c, k)], wb.at[k, x, z, own_rows])

    def start_loads(k):
        load_x(k).start()
        load_other(k).start()
        load_w(k).start()

    barrier = pltpu.get_barrier_semaphore()
    partners = (to_yp, to_yo, to_ym, to_zp, to_zo, to_zm, to_x, to_sib, to_tower)
    for device in partners:
        pl.semaphore_signal(barrier, inc=1, device_id=device, device_id_type=pl.DeviceIdType.MESH)

    small = [
        local(Local.small + i, src, dst)
        for i, (src, dst) in enumerate(((group_in, group), (pad_in, pad), (stitch_in, stitch), (bias_in, bias)))
    ]
    for copy in small[:2]:
        copy.start()
    loop(CUTS, start_loads)
    for copy in small[2:]:
        copy.start()
    for j in range(4):
        local(Local.cot, cotangent.at[:, pl.ds(j * SPAN, SPAN)], cot.at[j]).start()

    for copy in small[:2]:
        copy.wait()
    grouped[c] = jnp.broadcast_to(group[...].astype(jnp.float32), (OWN, OWN)).T.astype(jnp.bfloat16)
    absent[...] = 1.0 - pad[...].astype(jnp.float32).astype(jnp.bfloat16)

    def kept(value, core, side, k):
        rows = jnp.concatenate([grouped[core]] * (CUT // OWN), 1)
        return value * (1.0 - rows * absent[0:1, columns(side, k)])

    def masked(k):
        pltpu.make_async_copy(xb.at[k, y], xb.at[k, y], load_sem.at[k]).wait()
        staged[k] = kept(staged[k], c, other, k)
        xb[k, y, c] = kept(xb[k, y, c], c, c, k)

    masked(0)
    pl.semaphore_wait(barrier, len(partners))

    def x_sib(k):
        return remote(Kind.x_sib, k, staged.at[k], xb.at[k, y, c], to_sib)

    def w_sib(k):
        return remote(Kind.w_sib, k, weights.at[:, columns(other, k)], wb.at[k, x, z, own_rows], to_sib)

    def to_sibling(k):
        pl.when(k > 0)(lambda: masked(k))
        remote(Kind.own_yp, k, xb.at[k, y, c], xb.at[k, y, c], to_yp).start()
        remote(Kind.own_ym, k, xb.at[k, y, c], xb.at[k, y, c], to_ym).start()
        x_sib(k).start()
        w_sib(k).start()

    def own_out(k):
        arrived(Kind.x_sib, k, xb.at[k, y, :, : (OWN + ROWS) // 2])
        remote(Kind.sib_yp, k, xb.at[k, y, other], xb.at[k, y, other], to_yp).start()
        remote(Kind.sib_ym, k, xb.at[k, y, other], xb.at[k, y, other], to_ym).start()
        remote(Kind.w_x, k, wb.at[k, x, z], wb.at[k, x, z], to_x).start()
        remote(Kind.own_zp, k, wb.at[k, x, z], wb.at[k, x, z], to_zp).start()
        remote(Kind.own_zm, k, wb.at[k, x, z], wb.at[k, x, z], to_zm).start()

    every_w = wb.at[:CUTS, x, z]

    def first(k):
        pl.when(k < CUTS)(lambda: to_sibling(k))

        @pl.when(k == 0)
        def _():
            every = wb.at[:CUTS, x, z, own_rows]
            local(Local.w, every, every).wait()

        pl.when(k >= 1)(lambda: own_out(k - 1))

    loop(CUTS + 1, first)
    remote(Kind.keep, 0, grouped.at[c], grouped.at[c], to_sib).start()
    for j in range(4):
        remote(Kind.cot, j, cotangent.at[:, pl.ds(j * SPAN, SPAN)], cot_in.at[j], to_tower).start()

    def pair_out(k):
        arrived(Kind.w_x, k, wb.at[k, 1 - x, z])
        remote(Kind.pair_zp, k, wb.at[k, 1 - x, z], wb.at[k, 1 - x, z], to_zp).start()
        remote(Kind.pair_zm, k, wb.at[k, 1 - x, z], wb.at[k, 1 - x, z], to_zm).start()

    loop(CUTS, pair_out)

    def forward(k):
        arrived(Kind.own_yp, k, xb.at[k, ym])
        arrived(Kind.own_ym, k, xb.at[k, yp])
        remote(Kind.fwd_yp, k, xb.at[k, ym, 0], xb.at[k, ym, 0], to_yp).start()
        remote(Kind.fwd_ym, k, xb.at[k, yp, 1], xb.at[k, yp, 1], to_ym).start()
        arrived(Kind.own_zp, k, wb.at[k, :, zm])
        arrived(Kind.own_zm, k, wb.at[k, :, zp])
        remote(Kind.fwd_zp, k, wb.at[k, x, zm], wb.at[k, x, zm], to_zp).start()
        remote(Kind.fwd_zm, k, wb.at[k, 1 - x, zp], wb.at[k, 1 - x, zp], to_zm).start()

    loop(CUTS, forward)

    for copy in small[2:]:
        copy.wait()
    for j in range(4):
        part = slice(j * SPAN, (j + 1) * SPAN)
        coef[j, 0:1, :] = jnp.where(t == 0, stitch[0, 0:1, part], stitch[1, 1:2, part])
        coef[j, 1:2, :] = jnp.where(t == 0, stitch[1, 0:1, part], stitch[0, 1:2, part])
        coef[j, 2:3, :] = jnp.where(t == 0, stitch[0, 1:2, part], stitch[1, 0:1, part])
        coef[j, 3:4, :] = bias[0:1, part]
    local(Local.cot, cot, cot).wait()
    arrived(Kind.cot, 0, cot_in)
    for d in ORDER:
        j = (y + d) % 4

        def combine(i, d=d, j=j):
            rows = pl.ds(pl.multiple_of(i * STRIP, STRIP), STRIP)
            value = (
                coef[j, 0:1, :] * cot[j, rows, :].astype(jnp.float32)
                + coef[j, 1:2, :] * cot_in[j, rows, :].astype(jnp.float32)
            ).astype(jnp.bfloat16)
            if d == 0:
                hg[y, rows, :] = value
            else:
                hg_send[j, rows, :] = value

        loop(OWN // STRIP, combine)
        if d:
            remote(Kind.hg, d, hg_send.at[j], hg.at[y], to_y[d]).start()

    def pre_in(i):
        return grad_out.at[:, pl.ds(pl.multiple_of(i * SPAN, SPAN), SPAN)]

    def gathered(k):
        arrived(Kind.fwd_yp, k, xb.at[k, 0:2])

    def add_block(k, b):
        pre[b] += lax.dot_general(
            xb[k, b].reshape(2 * OWN, CUT), wb[k].reshape(SPAN, CUT),
            (((1,), (1,)), ((), ())), preferred_element_type=jnp.float32,
        ).reshape(2, OWN, SPAN)

    def add_product(k):
        gathered(k)
        loop(4, lambda b: add_block(k, b))

    def clear(b):
        pre[b] = jnp.zeros((2, OWN, SPAN), jnp.float32)

    loop(4, clear)
    loop(CUTS - 1, add_product)
    gathered(CUTS - 1)

    for d in ORDER:
        b = (y + d) % 4
        add_block(CUTS - 1, b)
        for h in range(2):
            part = pl.ds(h * ROWS, ROWS)
            remote(Kind.pre, d, pre.at[b, other, part], pre_in(2 * d + h), to_sib).start()
    bias_sum[...] = jnp.zeros_like(bias_sum)

    def activate(d):
        b = (y + d) % 4
        arrived(Kind.pre, d, pre.at[b, other])
        if d:
            arrived(Kind.hg, 4 - d, hg.at[b])

        def act(i):
            rows = pl.ds(pl.multiple_of(i * STRIP, STRIP), STRIP)
            per = ROWS // STRIP
            rows_in = pl.ds(pl.multiple_of((i % per) * STRIP, STRIP), STRIP)
            value = pre[b, c, rows, :] + pre_in(2 * d + i // per)[rows_in, :] + coef[y, 3:4, :]
            gate = jax.nn.sigmoid(value)
            hidden = (value * gate).astype(jnp.bfloat16)
            grad = (hg[b, rows, :].astype(jnp.float32) * gate * (1.0 + value * (1.0 - gate))).astype(jnp.bfloat16)
            pg[b, c, rows, :] = grad
            if d == 0:
                hid[y, rows, :] = hidden
            else:
                hid_send[b, rows, :] = hidden
            bias_sum[...] += jnp.sum(grad.astype(jnp.float32).reshape(STRIP // 8, 8, SPAN), 0)

        loop(OWN // STRIP, act)
        remote(Kind.pg, d, pg.at[b, c], pg.at[b, c], to_sib).start()
        if d:
            remote(Kind.hid, d, hid_send.at[b], hid.at[y], to_y[d]).start()

    def product_d(k, b):
        product = jnp.dot(
            pg[b].reshape(2 * OWN, SPAN), wb[k].reshape(SPAN, CUT), preferred_element_type=jnp.float32
        )
        return product.astype(jnp.bfloat16).reshape(2, OWN, CUT)

    def product_late(k, side):
        return jnp.dot(
            pgt[side].reshape(4 * OWN, SPAN), xb[k].reshape(SPAN, CUT), preferred_element_type=jnp.float32
        ).reshape(4, OWN, CUT)

    def product_g(k, v):
        product = jnp.dot(
            pgt[:, v].reshape(2 * OWN, SPAN), xb[k].reshape(SPAN, CUT), preferred_element_type=jnp.float32
        )
        return product.astype(jnp.bfloat16).reshape(2, OWN, CUT)

    def late_away(i):
        late_out[...] = product_late(EARLY + i, 1 - x).astype(jnp.bfloat16)
        remote(Kind.gb_x, i, late_out, late.at[i], to_x).start()

    def opposite_d(k):
        d_opp[k] = product_d(k, yo)
        remote(Kind.opp_yp, k, d_opp.at[k, 0], relay_yp.at[k], to_yp).start()
        remote(Kind.opp_ym, k, d_opp.at[k, 1], relay_ym.at[k], to_ym).start()

    def opposite_g(k):
        g_opp[k] = product_g(k, zo)
        remote(Kind.opp_zp, k, g_opp.at[k, 0], relay_zp.at[k], to_zp).start()
        remote(Kind.opp_zm, k, g_opp.at[k, 1], relay_zm.at[k], to_zm).start()

    for d in ORDER:
        activate(d)
    pl.semaphore_signal(room_sem, inc=1, device_id=to_tower, device_id_type=pl.DeviceIdType.MESH)
    for d in ORDER:
        arrived(Kind.pg, d, pg.at[(y + d) % 4, other])
        if d == 2:
            loop(CUTS, opposite_d)

    wide = 256
    eye = (
        lax.broadcasted_iota(jnp.int32, (wide, wide), 0) == lax.broadcasted_iota(jnp.int32, (wide, wide), 1)
    ).astype(jnp.bfloat16)
    for o in range(SPAN // wide):
        flipped = lax.dot_general(
            eye, pg[:, :, :, o * wide : (o + 1) * wide].reshape(SPAN, wide),
            (((1,), (1,)), ((), ())), preferred_element_type=jnp.float32,
        )
        pgt[o // 2, (o % 2) * 2 : (o % 2) * 2 + 2] = flipped.astype(jnp.bfloat16).reshape(2, OWN, SPAN)
    loop(EARLY, opposite_g)
    arrived(Kind.hid, 0, hid.at[:3])
    pl.semaphore_wait(room_sem, 1)
    for j in range(4):
        remote(Kind.tow, j, hid.at[j], hid_other.at[j], to_tower).start()
    sent(Kind.hg, hg_send.at[:3])
    loop(LATE, late_away)

    sent(Kind.w_sib, wb.at[:CUTS, x, z, own_rows])
    sent(Kind.own_yp, xb.at[:, 0:3])
    sent(Kind.own_zp, xb)
    sent(Kind.pre, pre.at[:, other])
    arrived(Kind.keep, 0, grouped.at[other])

    def slot(k):
        return (k + CUTS) % (CUTS + 1)

    def g_keep(k):
        part = pl.ds(pl.multiple_of((k % (SPAN // CUT)) * CUT, CUT), CUT)
        block = k // (SPAN // CUT)
        return pre.at[block // 2, block % 2, :, part]

    def products(k):
        s = slot(k)

        def block_g(i):
            v = (zo + 1 + i) % 4
            wb[s, :, v] = product_g(k, v)

        def block_d(i):
            b = (yo + 1 + i) % 4
            xb[k, b] = product_d(k, b)

        pl.when(k < EARLY)(lambda: loop(3, block_g))
        loop(3, block_d)

    def late_in(i):
        k = EARLY + i
        arrived(Kind.gb_x, i, late.at[i])

        late[i] = (product_late(k, x) + late[i].astype(jnp.float32)).astype(jnp.bfloat16)
        remote(Kind.late_opp_zp, k, late.at[i, zo, TOP], relay_zp.at[k, TOP], to_zp).start()
        remote(Kind.late_opp_zm, k, late.at[i, zo, LOW], relay_zm.at[k, TOP], to_zm).start()

    def wide_sum(*terms):
        total = terms[0].astype(jnp.float32)
        for term in terms[1:]:
            total += term.astype(jnp.float32)
        return total

    def relays(k):
        arrived(Kind.opp_yp, k, relay_yp.at[k])
        xb[k, yp, 0] = wide_sum(xb[k, yp, 0], relay_yp[k]).astype(jnp.bfloat16)
        remote(Kind.sum_yp, k, xb.at[k, yp], part_yp.at[k], to_yp).start()
        arrived(Kind.opp_ym, k, relay_ym.at[k])
        xb[k, ym, 1] = wide_sum(xb[k, ym, 1], relay_ym[k]).astype(jnp.bfloat16)
        remote(Kind.sum_ym, k, xb.at[k, ym], part_ym.at[k], to_ym).start()
        pl.when(k < EARLY)(lambda: relays_z(k))
        pl.when(k >= EARLY)(lambda: relays_late(k))

    def relays_z(k):
        s = slot(k)
        arrived(Kind.opp_zp, k, relay_zp.at[k])
        wb[s, 0, zp] = wide_sum(wb[s, 0, zp], relay_zp[k]).astype(jnp.bfloat16)
        remote(Kind.sum_zp, k, wb.at[s, :, zp], part_zp.at[k], to_zp).start()
        arrived(Kind.opp_zm, k, relay_zm.at[k])
        wb[s, 1, zm] = wide_sum(wb[s, 1, zm], relay_zm[k]).astype(jnp.bfloat16)
        remote(Kind.sum_zm, k, wb.at[s, :, zm], part_zm.at[k], to_zm).start()

    def relays_late(k):
        i = k - EARLY
        arrived(Kind.late_opp_zp, k, relay_zp.at[k, TOP])
        late[i, zp, TOP] = wide_sum(late[i, zp, TOP], relay_zp[k, TOP]).astype(jnp.bfloat16)
        remote(Kind.late_sum_zp, k, late.at[i, zp], part_zp.at[k, 0], to_zp).start()
        arrived(Kind.late_opp_zm, k, relay_zm.at[k, TOP])
        late[i, zm, LOW] = wide_sum(late[i, zm, LOW], relay_zm[k, TOP]).astype(jnp.bfloat16)
        remote(Kind.late_sum_zm, k, late.at[i, zm], part_zm.at[k, 0], to_zm).start()

    def grad_done(k):
        remote(Kind.g_sib, 0, g_keep(k).at[sib_rows], grad_out.at[:, columns(c, k)], to_sib).start()
        grad_out[:, columns(c, k)] = g_keep(k)[own_rows, :]

    def sums_z(k):
        s = slot(k)
        arrived(Kind.sum_zp, k, xb.at[k, 0:2])
        g_send[k] = wide_sum(wb[s, 1 - x, z], part_zp[k, 1 - x], part_zm[k, 1 - x]).astype(jnp.bfloat16)
        remote(Kind.g_x, k, g_send.at[k], g_in.at[k], to_x).start()
        g_keep(k)[...] = wide_sum(wb[s, x, z], part_zp[k, x], part_zm[k, x])

    def sums_late(k):
        arrived(Kind.late_sum_zp, k, xb.at[k, 0])
        g_keep(k)[...] = wide_sum(late[k - EARLY, z], part_zp[k, 0], part_zm[k, 0])
        grad_done(k)

    def sums(k):
        pl.when(k < EARLY)(lambda: sums_z(k))
        pl.when(k >= EARLY)(lambda: sums_late(k))
        arrived(Kind.sum_yp, k, xb.at[k, 0:2])
        theirs = wide_sum(xb[k, y, other], part_yp[k, other], part_ym[k, other])
        xb[k, y, other] = kept(theirs.astype(jnp.bfloat16), other, c, k)
        remote(Kind.d_sib, 0, xb.at[k, y, other], feat_out.at[:, columns(c, k)], to_sib).start()
        ours = wide_sum(xb[k, y, c], part_yp[k, c], part_ym[k, c])
        feat_out[:, columns(c, k)] = kept(ours.astype(jnp.bfloat16), c, c, k)

    def ends(k):
        arrived(Kind.g_x, k, g_in.at[k])
        g_keep(k)[...] += g_in[k].astype(jnp.float32)
        grad_done(k)

    def mixing():
        arrived(Kind.tow, 0, hid_other)
        for j in range(4):

            def strip(i, sums, j=j):
                rows = pl.ds(pl.multiple_of(i * STRIP, STRIP), STRIP)
                here = hid[j, rows, :].astype(jnp.float32)
                there = hid_other[j, rows, :].astype(jnp.float32)
                mixed_out[rows, j * SPAN : (j + 1) * SPAN] = (coef[j, 0:1, :] * here + coef[j, 2:3, :] * there).astype(jnp.bfloat16)
                up = cot[j, rows, :].astype(jnp.float32)
                return (
                    sums[0] + jnp.sum((up * here).reshape(STRIP // 8, 8, SPAN), 0),
                    sums[1] + jnp.sum((up * there).reshape(STRIP // 8, 8, SPAN), 0),
                )

            zero = jnp.zeros((8, SPAN), jnp.float32)
            here, there = lax.fori_loop(0, OWN // STRIP, strip, (zero, zero))
            here, there = jnp.sum(here, 0, keepdims=True), jnp.sum(there, 0, keepdims=True)
            for h in range(2):
                part = slice(h * SPAN // 2, (h + 1) * SPAN // 2)
                vec[h, j : j + 1, :] = jnp.where(t == 0, here[:, part], there[:, part])
                vec[h, 4 + j : 5 + j, :] = jnp.where(t == 0, there[:, part], here[:, part])
        bias = jnp.sum(bias_sum[...], 0, keepdims=True)
        bias = jnp.where(lax.broadcasted_iota(jnp.int32, (8, SPAN), 0) == y, bias, 0.0)
        for h in range(2):
            vec[h, 8:16, :] = bias[:, h * SPAN // 2 : (h + 1) * SPAN // 2]
        remote(Kind.v_c, 0, vec.at[other], vec_c, to_sib).start()

    def over_cores():
        arrived(Kind.v_c, 0, vec_c)
        vec_x[...] = vec[c] + vec_c[...]
        remote(Kind.v_x, 0, vec_x, vec_xin, to_x).start()

    def over_x():
        arrived(Kind.v_x, 0, vec_xin)
        vec_z[z] = vec_x[...] + vec_xin[...]
        for d in range(1, 4):
            remote(Kind.v_z, d, vec_z.at[z], vec_z.at[z], to_z[d]).start()

    def over_z():
        arrived(Kind.v_z, 0, vec_z.at[:3])
        vec_y[y] = (vec_z[0] + vec_z[1]) + (vec_z[2] + vec_z[3])
        for d in range(1, 4):
            remote(Kind.v_y, d, vec_y.at[y], vec_y.at[y], to_y[d]).start()

    def over_y():
        arrived(Kind.v_y, 0, vec_y.at[:3])
        vec_t[c, t] = (vec_y[0] + vec_y[1]) + (vec_y[2] + vec_y[3])
        remote(Kind.v_t, 0, vec_t.at[c, t], vec_t.at[c, t], to_tower).start()

    def over_towers():
        arrived(Kind.v_t, 0, vec_t.at[c, 1 - t])
        remote(Kind.v_b, 0, vec_t.at[c], vec_t.at[c], to_sib).start()

    between = {
        3: (mixing, over_cores), 4: (lambda: late_in(0), over_x,), 6: (over_z,), 8: (over_y,), 9: (over_towers,),
    }

    def step(s):
        pl.when(s < CUTS)(lambda: products(s))
        pl.when(s < CUTS)(lambda: relays(s))
        pl.when((s >= 2) & (s < CUTS + 2))(lambda: sums(s - 2))
        pl.when((s >= 3) & (s < EARLY + 3))(lambda: ends(s - 3))
        for at, tasks in between.items():

            @pl.when(s == at)
            def _(tasks=tasks):
                for task in tasks:
                    task()

    loop(CUTS + 2, step)

    arrived(Kind.v_b, 0, vec_t.at[other])

    def half(ref, side):
        return ref.at[:, pl.ds(pl.multiple_of(side * HALF, HALF), HALF)]

    arrived(Kind.d_sib, 0, half(feat_out, other))
    arrived(Kind.g_sib, 0, half(grad_out, other))
    sent(Kind.opp_yp, d_opp)
    sent(Kind.sum_yp, xb.at[:, 0:2])
    sent(Kind.opp_zp, g_opp)
    sent(Kind.sum_zp, xb.at[:EARLY, 0:2])
    sent(Kind.late_opp_zp, late.at[:, 0])
    sent(Kind.late_sum_zp, late.at[:, 0:2])
    sent(Kind.g_x, g_send.at[:EARLY])
    sent(Kind.gb_x, late)
    sent(Kind.d_sib, xb.at[:, y, 0])
    sent(Kind.g_sib, half(grad_out, other))
    sent(Kind.cot, cot)
    sent(Kind.pg, pg.at[:, 0])
    sent(Kind.tow, hid)
    sent(Kind.hid, hid.at[:3])
    sent(Kind.v_z, vec_z.at[:3])
    sent(Kind.v_y, vec_y.at[:3])
    sent(Kind.v_c, vec_c)
    sent(Kind.v_x, vec_x)
    sent(Kind.v_t, vec_c)
    sent(Kind.v_b, vec_t.at[c])
    sent(Kind.keep, grouped.at[c])


def towers(*operands):
    low, wide = jnp.bfloat16, jnp.float32
    scratch = [
        ((CUTS, 4, 2, OWN, CUT), low),
        ((CUTS + 1, 2, 4, OWN, CUT), low),
        ((4, 2, OWN, SPAN), wide),
        ((4, 2, OWN, SPAN), low),
        ((2, 4, OWN, SPAN), low),
        ((4, OWN, SPAN), low),
        ((4, OWN, SPAN), low),
        ((4, OWN, SPAN), low),
        ((4, OWN, SPAN), low),
        ((4, OWN, SPAN), low),
        ((CUTS, 2, OWN, CUT), low),
        ((EARLY, 2, OWN, CUT), low),
        ((LATE, 4, OWN, CUT), low),
        ((CUTS, OWN, CUT), low),
        ((CUTS, OWN, CUT), low),
        ((CUTS, 2, OWN, CUT), low),
        ((CUTS, 2, OWN, CUT), low),
        ((CUTS, OWN, CUT), low),
        ((CUTS, OWN, CUT), low),
        ((CUTS, 2, OWN, CUT), low),
        ((CUTS, 2, OWN, CUT), low),
        ((CUTS, OWN, CUT), low),
        ((CUTS, OWN, CUT), low),
        ((1, OWN), jnp.int32),
        ((1, FEAT), jnp.int32),
        ((2, 2, OUT), wide),
        ((1, OUT), wide),
        ((2, OWN, OWN), low),
        ((1, FEAT), low),
        ((4, 8, SPAN), wide),
        ((8, SPAN), wide),
        ((2, 16, SPAN // 2), wide),
        ((16, SPAN // 2), wide),
        ((16, SPAN // 2), wide),
        ((16, SPAN // 2), wide),
        ((4, 16, SPAN // 2), wide),
        ((4, 16, SPAN // 2), wide),
    ]
    anywhere, near = pl.BlockSpec(memory_space=pl.ANY), pl.BlockSpec(memory_space=pltpu.VMEM)
    return pl.pallas_call(
        body,
        out_shape=[
            pltpu.VMEM((OWN, OUT), low),
            pltpu.VMEM((OWN, FEAT), low),
            pltpu.VMEM((ROWS, FEAT), wide),
            pltpu.VMEM((2, 2, 16, SPAN // 2), wide),
        ],
        in_specs=[anywhere] * 7,
        out_specs=[near] * 4,
        scratch_shapes=[pltpu.VMEM(shape, kind) for shape, kind in scratch]
        + [
            pltpu.SemaphoreType.DMA((len(set(LEAVES.values())),)),
            pltpu.SemaphoreType.DMA((len(ROWED), CUTS)),
            pltpu.SemaphoreType.DMA((sum(FEW.values()),)),
            pltpu.SemaphoreType.DMA((CUTS,)),
            pltpu.SemaphoreType.DMA((len(Local),)),
            pltpu.SemaphoreType.REGULAR,
        ],
        compiler_params=pltpu.CompilerParams(
            collective_id=0, has_side_effects=True, vmem_limit_bytes=GRANT
        ),
    )(*operands)


def closing(
    mixed_in, feat_in, grad_in, vec_in, momentum, weights,
    mixed, feat, grad, stitch, bias, new_momentum, new_weights,
    stitch_here, bias_here, weights_here, moved, result, sem,
):
    t = lax.axis_index("tower")
    started = []

    def start(count, src, dst):
        size = src.shape[0] // count
        for i in range(count):
            first = len(started)
            part = pl.ds(i * size, size)
            started.append(pltpu.make_async_copy(src.at[part], dst.at[part], sem.at[first]))
            started[-1].start()
        return started[-count:]

    loads = start(PARTS, weights, weights_here)
    start(PARTS, grad_in, grad)
    start(2, feat_in, feat)
    start(2, mixed_in, mixed)
    size = ROWS // PARTS
    for i in range(PARTS):
        rows = pl.ds(i * size, size)
        moved[rows] = momentum_rate * momentum[rows] + grad_in[rows]
        start(1, moved.at[rows], new_momentum.at[rows])
        loads[i].wait()
        result[rows] = weights_here[rows].astype(jnp.float32) - learn_rate * moved[rows]
        start(1, result.at[rows], new_weights.at[rows])
    for j in range(4):
        for h in range(2):
            part = slice((2 * j + h) * SPAN // 2, (2 * j + h + 1) * SPAN // 2)
            for s in range(2):
                for u in range(2):
                    stitch_here[s, u : u + 1, part] = vec_in[h, s, 4 * u + j : 4 * u + j + 1, :]
            bias_here[0:1, part] = vec_in[h, t, 8 + j : 9 + j, :]
    start(1, stitch_here, stitch)
    start(1, bias_here, bias)
    for copy in started[PARTS:]:
        copy.wait()


def close(mixed, feat, grad, vec, momentum, weights):
    anywhere, near = pl.BlockSpec(memory_space=pl.ANY), pl.BlockSpec(memory_space=pltpu.VMEM)
    small = [jax.ShapeDtypeStruct((2, 2, OUT), jnp.float32), jax.ShapeDtypeStruct((1, OUT), jnp.float32)]
    shapes = [*(jax.ShapeDtypeStruct(v.shape, v.dtype) for v in (mixed, feat, grad)), *small]
    shapes += [jax.ShapeDtypeStruct(grad.shape, grad.dtype)] * 2
    kept_near = [pltpu.with_memory_space_constraint(v, pltpu.VMEM) for v in (mixed, feat, grad, vec, momentum)]
    return pl.pallas_call(
        closing,
        out_shape=shapes,
        in_specs=[near] * 5 + [anywhere],
        out_specs=[anywhere] * 7,
        scratch_shapes=[pltpu.VMEM(v.shape, v.dtype) for v in (*small, weights, grad, grad)]
        + [pltpu.SemaphoreType.DMA((4 * PARTS + 6,))],
        compiler_params=pltpu.CompilerParams(vmem_limit_bytes=GRANT),
        cost_estimate=pl.CostEstimate(flops=0, bytes_accessed=14_000_000, transcendentals=0),
    )(*kept_near, weights)


def shards(features, group, pad_mask, weights, bias, stitch, momentum, cotangent):
    sums = towers(features[0], weights[0], cotangent[0], group[None], pad_mask[None], stitch, bias)
    mixed, feat_grad, weight_grad, stitch_grad, bias_grad, new_momentum, new_weights = close(
        *sums, momentum[0], weights[0]
    )
    return (
        mixed[None], feat_grad[None], weight_grad[None], bias_grad, stitch_grad, new_momentum[None], new_weights[None]
    )


def solution(mesh):
    placed = (
        P("tower", "blk", None),
        P("blk"),
        P(),
        P("tower", "blk", None),
        P("tower", None),
        P(),
        P("tower", "blk", None),
        P("tower", "blk", None),
    )
    return jax.shard_map(
        shards,
        mesh=mesh,
        in_specs=placed,
        out_specs=(
            P("tower", "blk", None),
            P("tower", "blk", None),
            P("tower", "blk", None),
            P("tower", None),
            P(),
            P("tower", "blk", None),
            P("tower", "blk", None),
        ),
        check_vma=False,
    )
```

```python
import enum

import jax
import jax.numpy as jnp
from jax import lax
from jax.experimental import pallas as pl
from jax.experimental.pallas import tpu as pltpu
from jax.sharding import PartitionSpec as P

momentum_rate = 0.9
learn_rate = 0.0001

FEAT = 9216
OUT = 4096
HALF = FEAT // 2
OWN = 128
ROWS = 64
SPAN = 1024
CUT = 512
CUTS = HALF // CUT
LATE = 1
EARLY = CUTS - LATE
AHEAD = 4
PARTS = 4
GRANT = 56 << 20
STRIP = 32
ORDER = (2, 1, 3, 0)


class Kind(enum.IntEnum):
    (
        x_sib, w_sib, w_x, own_yp, own_ym, own_zp, own_zm, pair_zp, pair_zm, sib_yp, sib_ym, fwd_yp, fwd_ym, fwd_zp, fwd_zm,
        opp_yp, opp_ym, opp_zp, opp_zm, sum_yp, sum_ym, sum_zp, sum_zm, g_x, d_sib, g_sib, late_opp_zp, late_opp_zm,
        late_sum_zp, late_sum_zm, keep, cot, hg, pre, pg, hid, tow, gb_x, v_c, v_x, v_z, v_y, b_y, v_t, v_b,
    ) = range(45)


class Local(enum.IntEnum):
    w, cot, small, small_1, small_2, small_3 = range(6)


ROWED = (
    (Kind.x_sib, Kind.w_sib, Kind.g_x),
    (Kind.w_x, Kind.sum_zp, Kind.sum_zm, Kind.late_sum_zp, Kind.late_sum_zm),
    (Kind.own_yp, Kind.sib_yp, Kind.opp_yp),
    (Kind.own_ym, Kind.sib_ym, Kind.opp_ym),
    (Kind.own_zp, Kind.pair_zp, Kind.opp_zp, Kind.late_opp_zp),
    (Kind.own_zm, Kind.pair_zm, Kind.opp_zm, Kind.late_opp_zm),
    (Kind.fwd_yp, Kind.fwd_ym, Kind.fwd_zp, Kind.fwd_zm, Kind.sum_yp, Kind.sum_ym),
)
ROW = {kind: row for row, kinds in enumerate(ROWED) for kind in kinds}
FEW = {
    Kind.keep: 1, Kind.cot: 1, Kind.hg: 4, Kind.pre: 4, Kind.pg: 4, Kind.hid: 1, Kind.tow: 1, Kind.gb_x: LATE, Kind.v_c: 1,
    Kind.v_x: 1, Kind.v_z: 1, Kind.v_y: 1, Kind.b_y: 1, Kind.v_t: 1, Kind.v_b: 1, Kind.d_sib: 1, Kind.g_sib: 1,
}
FIRST = {kind: sum(list(FEW.values())[:place]) for place, kind in enumerate(FEW)}
TOGETHER = (
    (Kind.own_yp, Kind.own_ym, Kind.sib_yp, Kind.sib_ym, Kind.fwd_yp, Kind.fwd_ym),
    (
        Kind.own_zp, Kind.own_zm, Kind.pair_zp, Kind.pair_zm, Kind.fwd_zp, Kind.fwd_zm, Kind.w_x, Kind.x_sib,
    ),
    (Kind.opp_yp, Kind.opp_ym),
    (Kind.sum_yp, Kind.sum_ym),
    (Kind.opp_zp, Kind.opp_zm),
    (Kind.sum_zp, Kind.sum_zm),
    (Kind.late_opp_zp, Kind.late_opp_zm),
    (Kind.late_sum_zp, Kind.late_sum_zm),
)
LEAVES = {kind: group for group, kinds in enumerate(TOGETHER) for kind in kinds}
for _kind in Kind:
    LEAVES.setdefault(_kind, len(set(LEAVES.values())))


def body(
    features, weights, cotangent, group_in, pad_in, stitch_in, bias_in,
    mixed_out, feat_out, grad_out, vec_t,
    xb, wb, pre, pg, pgt, cot, cot_in, hg_send, hg, hid, d_opp, g_opp, late,
    relay_yp, relay_ym, part_yp, part_ym, relay_zp, relay_zm, part_zp, part_zm,
    g_send, g_in, group, pad, stitch, bias, grouped, absent, coef, bias_sum, vec, vec_c, vec_x, vec_xin, vec_z, vec_y, bias_y,
    send_sem, row_sem, few_sem, load_sem, local_sem, room_sem, chips_sem, all_sem,
):
    blk, t = lax.axis_index("blk"), lax.axis_index("tower")
    y, x, z, c = blk // 16, (blk // 8) % 2, (blk // 2) % 4, blk % 2
    other = 1 - c

    def place(y, x, z, c):
        return ((y * 2 + x) * 4 + z) * 2 + c

    yp, yo, ym = (y + 1) % 4, (y + 2) % 4, (y + 3) % 4
    zp, zo, zm = (z + 1) % 4, (z + 2) % 4, (z + 3) % 4
    to_yp, to_yo, to_ym = ((place(v, x, z, c), t) for v in (yp, yo, ym))
    to_zp, to_zo, to_zm = ((place(y, x, v, c), t) for v in (zp, zo, zm))
    to_x = (place(y, 1 - x, z, c), t)
    to_sib = (place(y, x, z, other), t)
    to_tower = (blk, 1 - t)
    to_y = (None, to_yp, to_yo, to_ym)
    to_z = (None, to_zp, to_zo, to_zm)

    def remote(kind, k, src, dst, device):
        if kind in ROW:
            landed = row_sem.at[ROW[kind], k]
        else:
            landed = few_sem.at[FIRST[kind] + (k if FEW[kind] > 1 else 0)]
        return pltpu.make_async_remote_copy(
            src_ref=src, dst_ref=dst, send_sem=send_sem.at[LEAVES[kind]], recv_sem=landed,
            device_id=device, device_id_type=pl.DeviceIdType.MESH,
        )

    def arrived(kind, k, dst):
        remote(kind, k, dst, dst, to_sib).wait_recv()

    def sent(kind, src):
        remote(kind, 0, src, src, to_sib).wait_send()

    def local(kind, src, dst):
        return pltpu.make_async_copy(src, dst, local_sem.at[kind])

    def columns(side, k):
        return pl.ds(pl.multiple_of(side * HALF + k * CUT, CUT), CUT)

    def loop(count, step):
        lax.fori_loop(0, count, lambda k, carry: (step(k), carry)[1], 0)

    hid_other = hg
    late_out = hg_send.at[:, :, :CUT]
    hid_send = cot_in
    staged = g_send
    TOP, LOW = pl.ds(0, OWN // 2), pl.ds(OWN // 2, OWN // 2)
    own_rows = pl.ds(pl.multiple_of(c * ROWS, ROWS), ROWS)
    sib_rows = pl.ds(pl.multiple_of(other * ROWS, ROWS), ROWS)

    def load_x(k):
        return pltpu.make_async_copy(features.at[:, columns(c, k)], xb.at[k, y, c], load_sem.at[k])

    def load_other(k):
        return pltpu.make_async_copy(features.at[:, columns(other, k)], staged.at[k], load_sem.at[k])

    def load_w(k):
        return local(Local.w, weights.at[:, columns(c, k)], wb.at[k, x, z, own_rows])

    def start_loads(k):
        load_x(k).start()
        load_other(k).start()
        load_w(k).start()

    barrier = pltpu.get_barrier_semaphore()
    along_y, across = (to_yp, to_yo, to_ym), (to_zp, to_zo, to_zm, to_x, to_tower)

    def signal(sem, device):
        pl.semaphore_signal(sem, inc=1, device_id=device, device_id_type=pl.DeviceIdType.MESH)

    def greet(sem):
        for core, devices in enumerate((along_y, across)):

            @pl.when(c == core)
            def _(devices=devices):
                for device in devices:
                    signal(sem, device)

    greeted = len(along_y) + c * (len(across) - len(along_y))
    signal(barrier, to_sib)
    greet(barrier)

    small = [
        local(Local.small + i, src, dst)
        for i, (src, dst) in enumerate(((group_in, group), (pad_in, pad), (stitch_in, stitch), (bias_in, bias)))
    ]
    for copy in small[:2]:
        copy.start()
    loop(CUTS, start_loads)
    for copy in small[2:]:
        copy.start()
    for j in range(4):
        local(Local.cot, cotangent.at[:, pl.ds(j * SPAN, SPAN)], cot.at[j]).start()

    for copy in small[:2]:
        copy.wait()
    grouped[c] = jnp.broadcast_to(group[...].astype(jnp.float32), (OWN, OWN)).T.astype(jnp.bfloat16)
    absent[...] = 1.0 - pad[...].astype(jnp.float32).astype(jnp.bfloat16)

    def kept(value, core, side, k):
        rows = jnp.concatenate([grouped[core]] * (CUT // OWN), 1)
        return value * (1.0 - rows * absent[0:1, columns(side, k)])

    def masked(k):
        pltpu.make_async_copy(xb.at[k, y], xb.at[k, y], load_sem.at[k]).wait()
        staged[k] = kept(staged[k], c, other, k)
        xb[k, y, c] = kept(xb[k, y, c], c, c, k)

    masked(0)
    pl.semaphore_wait(barrier, greeted + 1)
    greet(chips_sem)

    def x_sib(k):
        return remote(Kind.x_sib, k, staged.at[k], xb.at[k, y, c], to_sib)

    def w_sib(k):
        return remote(Kind.w_sib, k, weights.at[:, columns(other, k)], wb.at[k, x, z, own_rows], to_sib)

    def own_y(k):
        remote(Kind.own_yp, k, xb.at[k, y, c], xb.at[k, y, c], to_yp).start()
        remote(Kind.own_ym, k, xb.at[k, y, c], xb.at[k, y, c], to_ym).start()

    def to_sibling(k):
        x_sib(k).start()
        w_sib(k).start()

    def own_out(k):
        arrived(Kind.x_sib, k, xb.at[k, y, :, : (OWN + ROWS) // 2])
        remote(Kind.sib_yp, k, xb.at[k, y, other], xb.at[k, y, other], to_yp).start()
        remote(Kind.sib_ym, k, xb.at[k, y, other], xb.at[k, y, other], to_ym).start()
        remote(Kind.w_x, k, wb.at[k, x, z], wb.at[k, x, z], to_x).start()
        remote(Kind.own_zp, k, wb.at[k, x, z], wb.at[k, x, z], to_zp).start()
        remote(Kind.own_zm, k, wb.at[k, x, z], wb.at[k, x, z], to_zm).start()

    every_w = wb.at[:CUTS, x, z]

    def ahead(k):
        pl.when(k > 0)(lambda: masked(k))
        pl.when(c == 0)(lambda: own_y(k))
        to_sibling(k)

    def first(k):
        @pl.when(k < CUTS)
        def _():
            masked(k)
            own_y(k)
            to_sibling(k)

        own_out(k - AHEAD)

    loop(AHEAD, ahead)
    pl.semaphore_wait(chips_sem, greeted)
    signal(all_sem, to_sib)
    pl.semaphore_wait(all_sem, 1)
    pl.when(c == 1)(lambda: loop(AHEAD, own_y))
    every = wb.at[:CUTS, x, z, own_rows]
    local(Local.w, every, every).wait()
    loop(CUTS, lambda k: first(k + AHEAD))
    remote(Kind.keep, 0, grouped.at[c], grouped.at[c], to_sib).start()
    for j in range(4):
        remote(Kind.cot, j, cotangent.at[:, pl.ds(j * SPAN, SPAN)], cot_in.at[j], to_tower).start()

    def pair_out(k):
        arrived(Kind.w_x, k, wb.at[k, 1 - x, z])
        remote(Kind.pair_zp, k, wb.at[k, 1 - x, z], wb.at[k, 1 - x, z], to_zp).start()
        remote(Kind.pair_zm, k, wb.at[k, 1 - x, z], wb.at[k, 1 - x, z], to_zm).start()

    loop(CUTS, pair_out)

    def forward(k):
        arrived(Kind.own_yp, k, xb.at[k, ym])
        arrived(Kind.own_ym, k, xb.at[k, yp])
        remote(Kind.fwd_yp, k, xb.at[k, ym, 0], xb.at[k, ym, 0], to_yp).start()
        remote(Kind.fwd_ym, k, xb.at[k, yp, 1], xb.at[k, yp, 1], to_ym).start()
        arrived(Kind.own_zp, k, wb.at[k, :, zm])
        arrived(Kind.own_zm, k, wb.at[k, :, zp])
        remote(Kind.fwd_zp, k, wb.at[k, x, zm], wb.at[k, x, zm], to_zp).start()
        remote(Kind.fwd_zm, k, wb.at[k, 1 - x, zp], wb.at[k, 1 - x, zp], to_zm).start()

    loop(CUTS, forward)

    for copy in small[2:]:
        copy.wait()
    for j in range(4):
        part = slice(j * SPAN, (j + 1) * SPAN)
        coef[j, 0:1, :] = jnp.where(t == 0, stitch[0, 0:1, part], stitch[1, 1:2, part])
        coef[j, 1:2, :] = jnp.where(t == 0, stitch[1, 0:1, part], stitch[0, 1:2, part])
        coef[j, 2:3, :] = jnp.where(t == 0, stitch[0, 1:2, part], stitch[1, 0:1, part])
        coef[j, 3:4, :] = bias[0:1, part]
    local(Local.cot, cot, cot).wait()
    arrived(Kind.cot, 0, cot_in)
    for d in ORDER:
        j = (y + d) % 4

        def combine(i, d=d, j=j):
            rows = pl.ds(pl.multiple_of(i * STRIP, STRIP), STRIP)
            value = (
                coef[j, 0:1, :] * cot[j, rows, :].astype(jnp.float32)
                + coef[j, 1:2, :] * cot_in[j, rows, :].astype(jnp.float32)
            ).astype(jnp.bfloat16)
            if d == 0:
                hg[y, rows, :] = value
            else:
                hg_send[j, rows, :] = value

        loop(OWN // STRIP, combine)
        if d:
            remote(Kind.hg, d, hg_send.at[j], hg.at[y], to_y[d]).start()

    def pre_in(i):
        return grad_out.at[:, pl.ds(pl.multiple_of(i * SPAN, SPAN), SPAN)]

    def gathered(k):
        arrived(Kind.fwd_yp, k, xb.at[k, 0:2])

    def add_block(k, b):
        pre[b] += lax.dot_general(
            xb[k, b].reshape(2 * OWN, CUT), wb[k].reshape(SPAN, CUT),
            (((1,), (1,)), ((), ())), preferred_element_type=jnp.float32,
        ).reshape(2, OWN, SPAN)

    def add_product(k):
        gathered(k)
        loop(4, lambda b: add_block(k, b))

    def clear(b):
        pre[b] = jnp.zeros((2, OWN, SPAN), jnp.float32)

    loop(4, clear)
    loop(CUTS - 1, add_product)
    gathered(CUTS - 1)

    for d in ORDER:
        b = (y + d) % 4
        add_block(CUTS - 1, b)
        for h in range(2):
            part = pl.ds(h * ROWS, ROWS)
            remote(Kind.pre, d, pre.at[b, other, part], pre_in(2 * d + h), to_sib).start()
    bias_sum[...] = jnp.zeros_like(bias_sum)

    def activate(d):
        b = (y + d) % 4
        arrived(Kind.pre, d, pre.at[b, other])
        if d:
            arrived(Kind.hg, 4 - d, hg.at[b])

        def act(i):
            rows = pl.ds(pl.multiple_of(i * STRIP, STRIP), STRIP)
            per = ROWS // STRIP
            rows_in = pl.ds(pl.multiple_of((i % per) * STRIP, STRIP), STRIP)
            value = pre[b, c, rows, :] + pre_in(2 * d + i // per)[rows_in, :] + coef[y, 3:4, :]
            gate = jax.nn.sigmoid(value)
            hidden = (value * gate).astype(jnp.bfloat16)
            grad = (hg[b, rows, :].astype(jnp.float32) * gate * (1.0 + value * (1.0 - gate))).astype(jnp.bfloat16)
            pg[b, c, rows, :] = grad
            if d == 0:
                hid[y, rows, :] = hidden
            else:
                hid_send[b, rows, :] = hidden
            bias_sum[...] += jnp.sum(grad.astype(jnp.float32).reshape(STRIP // 8, 8, SPAN), 0)

        loop(OWN // STRIP, act)
        remote(Kind.pg, d, pg.at[b, c], pg.at[b, c], to_sib).start()
        if d:
            remote(Kind.hid, d, hid_send.at[b], hid.at[y], to_y[d]).start()

    def product_d(k, b):
        product = jnp.dot(
            pg[b].reshape(2 * OWN, SPAN), wb[k].reshape(SPAN, CUT), preferred_element_type=jnp.float32
        )
        return product.astype(jnp.bfloat16).reshape(2, OWN, CUT)

    def product_late(k, side):
        return jnp.dot(
            pgt[side].reshape(4 * OWN, SPAN), xb[k].reshape(SPAN, CUT), preferred_element_type=jnp.float32
        ).reshape(4, OWN, CUT)

    def product_g(k, v):
        product = jnp.dot(
            pgt[:, v].reshape(2 * OWN, SPAN), xb[k].reshape(SPAN, CUT), preferred_element_type=jnp.float32
        )
        return product.astype(jnp.bfloat16).reshape(2, OWN, CUT)

    def late_away(i):
        late_out[...] = product_late(EARLY + i, 1 - x).astype(jnp.bfloat16)
        remote(Kind.gb_x, i, late_out, late.at[i], to_x).start()

    def opposite_d(k):
        d_opp[k] = product_d(k, yo)
        remote(Kind.opp_yp, k, d_opp.at[k, 0], relay_yp.at[k], to_yp).start()
        remote(Kind.opp_ym, k, d_opp.at[k, 1], relay_ym.at[k], to_ym).start()

    def opposite_g(k):
        g_opp[k] = product_g(k, zo)
        remote(Kind.opp_zp, k, g_opp.at[k, 0], relay_zp.at[k], to_zp).start()
        remote(Kind.opp_zm, k, g_opp.at[k, 1], relay_zm.at[k], to_zm).start()

    for d in ORDER:
        activate(d)
    pl.semaphore_signal(room_sem, inc=1, device_id=to_tower, device_id_type=pl.DeviceIdType.MESH)
    for d in ORDER:
        arrived(Kind.pg, d, pg.at[(y + d) % 4, other])
        if d == 2:
            loop(CUTS, opposite_d)

    wide = 256
    eye = (
        lax.broadcasted_iota(jnp.int32, (wide, wide), 0) == lax.broadcasted_iota(jnp.int32, (wide, wide), 1)
    ).astype(jnp.bfloat16)
    for o in range(SPAN // wide):
        flipped = lax.dot_general(
            eye, pg[:, :, :, o * wide : (o + 1) * wide].reshape(SPAN, wide),
            (((1,), (1,)), ((), ())), preferred_element_type=jnp.float32,
        )
        pgt[o // 2, (o % 2) * 2 : (o % 2) * 2 + 2] = flipped.astype(jnp.bfloat16).reshape(2, OWN, SPAN)
    loop(EARLY, opposite_g)
    arrived(Kind.hid, 0, hid.at[:3])
    pl.semaphore_wait(room_sem, 1)
    for j in range(4):
        remote(Kind.tow, j, hid.at[j], hid_other.at[j], to_tower).start()
    sent(Kind.hg, hg_send.at[:3])
    loop(LATE, late_away)

    sent(Kind.w_sib, wb.at[:CUTS, x, z, own_rows])
    sent(Kind.own_yp, xb.at[:, 0:3])
    sent(Kind.own_zp, xb)
    sent(Kind.pre, pre.at[:, other])
    arrived(Kind.keep, 0, grouped.at[other])

    def slot(k):
        return (k + CUTS) % (CUTS + 1)

    def g_keep(k):
        part = pl.ds(pl.multiple_of((k % (SPAN // CUT)) * CUT, CUT), CUT)
        block = k // (SPAN // CUT)
        return pre.at[block // 2, block % 2, :, part]

    def products(k):
        s = slot(k)

        def block_g(i):
            v = (zo + 1 + i) % 4
            wb[s, :, v] = product_g(k, v)

        def block_d(i):
            b = (yo + 1 + i) % 4
            xb[k, b] = product_d(k, b)

        pl.when(k < EARLY)(lambda: loop(3, block_g))
        loop(3, block_d)

    def late_in(i):
        k = EARLY + i
        arrived(Kind.gb_x, i, late.at[i])

        late[i] = (product_late(k, x) + late[i].astype(jnp.float32)).astype(jnp.bfloat16)
        remote(Kind.late_opp_zp, k, late.at[i, zo, TOP], relay_zp.at[k, TOP], to_zp).start()
        remote(Kind.late_opp_zm, k, late.at[i, zo, LOW], relay_zm.at[k, TOP], to_zm).start()

    def wide_sum(*terms):
        total = terms[0].astype(jnp.float32)
        for term in terms[1:]:
            total += term.astype(jnp.float32)
        return total

    def relays(k):
        arrived(Kind.opp_yp, k, relay_yp.at[k])
        xb[k, yp, 0] = wide_sum(xb[k, yp, 0], relay_yp[k]).astype(jnp.bfloat16)
        remote(Kind.sum_yp, k, xb.at[k, yp], part_yp.at[k], to_yp).start()
        arrived(Kind.opp_ym, k, relay_ym.at[k])
        xb[k, ym, 1] = wide_sum(xb[k, ym, 1], relay_ym[k]).astype(jnp.bfloat16)
        remote(Kind.sum_ym, k, xb.at[k, ym], part_ym.at[k], to_ym).start()
        pl.when(k < EARLY)(lambda: relays_z(k))
        pl.when(k >= EARLY)(lambda: relays_late(k))

    def relays_z(k):
        s = slot(k)
        arrived(Kind.opp_zp, k, relay_zp.at[k])
        wb[s, 0, zp] = wide_sum(wb[s, 0, zp], relay_zp[k]).astype(jnp.bfloat16)
        remote(Kind.sum_zp, k, wb.at[s, :, zp], part_zp.at[k], to_zp).start()
        arrived(Kind.opp_zm, k, relay_zm.at[k])
        wb[s, 1, zm] = wide_sum(wb[s, 1, zm], relay_zm[k]).astype(jnp.bfloat16)
        remote(Kind.sum_zm, k, wb.at[s, :, zm], part_zm.at[k], to_zm).start()

    def relays_late(k):
        i = k - EARLY
        arrived(Kind.late_opp_zp, k, relay_zp.at[k, TOP])
        late[i, zp, TOP] = wide_sum(late[i, zp, TOP], relay_zp[k, TOP]).astype(jnp.bfloat16)
        remote(Kind.late_sum_zp, k, late.at[i, zp], part_zp.at[k, 0], to_zp).start()
        arrived(Kind.late_opp_zm, k, relay_zm.at[k, TOP])
        late[i, zm, LOW] = wide_sum(late[i, zm, LOW], relay_zm[k, TOP]).astype(jnp.bfloat16)
        remote(Kind.late_sum_zm, k, late.at[i, zm], part_zm.at[k, 0], to_zm).start()

    def grad_done(k):
        remote(Kind.g_sib, 0, g_keep(k).at[sib_rows], grad_out.at[:, columns(c, k)], to_sib).start()
        grad_out[:, columns(c, k)] = g_keep(k)[own_rows, :]

    def sums_z(k):
        s = slot(k)
        arrived(Kind.sum_zp, k, xb.at[k, 0:2])
        g_send[k] = wide_sum(wb[s, 1 - x, z], part_zp[k, 1 - x], part_zm[k, 1 - x]).astype(jnp.bfloat16)
        remote(Kind.g_x, k, g_send.at[k], g_in.at[k], to_x).start()
        g_keep(k)[...] = wide_sum(wb[s, x, z], part_zp[k, x], part_zm[k, x])

    def sums_late(k):
        arrived(Kind.late_sum_zp, k, xb.at[k, 0])
        g_keep(k)[...] = wide_sum(late[k - EARLY, z], part_zp[k, 0], part_zm[k, 0])
        grad_done(k)

    def sums(k):
        pl.when(k < EARLY)(lambda: sums_z(k))
        pl.when(k >= EARLY)(lambda: sums_late(k))
        arrived(Kind.sum_yp, k, xb.at[k, 0:2])
        theirs = wide_sum(xb[k, y, other], part_yp[k, other], part_ym[k, other])
        xb[k, y, other] = kept(theirs.astype(jnp.bfloat16), other, c, k)
        remote(Kind.d_sib, 0, xb.at[k, y, other], feat_out.at[:, columns(c, k)], to_sib).start()
        ours = wide_sum(xb[k, y, c], part_yp[k, c], part_ym[k, c])
        feat_out[:, columns(c, k)] = kept(ours.astype(jnp.bfloat16), c, c, k)

    def ends(k):
        arrived(Kind.g_x, k, g_in.at[k])
        g_keep(k)[...] += g_in[k].astype(jnp.float32)
        grad_done(k)

    def mixing():
        arrived(Kind.tow, 0, hid_other)
        for j in range(4):

            def strip(i, sums, j=j):
                rows = pl.ds(pl.multiple_of(i * STRIP, STRIP), STRIP)
                here = hid[j, rows, :].astype(jnp.float32)
                there = hid_other[j, rows, :].astype(jnp.float32)
                mixed_out[rows, j * SPAN : (j + 1) * SPAN] = (coef[j, 0:1, :] * here + coef[j, 2:3, :] * there).astype(jnp.bfloat16)
                up = cot[j, rows, :].astype(jnp.float32)
                return (
                    sums[0] + jnp.sum((up * here).reshape(STRIP // 8, 8, SPAN), 0),
                    sums[1] + jnp.sum((up * there).reshape(STRIP // 8, 8, SPAN), 0),
                )

            zero = jnp.zeros((8, SPAN), jnp.float32)
            here, there = lax.fori_loop(0, OWN // STRIP, strip, (zero, zero))
            here, there = jnp.sum(here, 0, keepdims=True), jnp.sum(there, 0, keepdims=True)
            for h in range(2):
                part = slice(h * SPAN // 2, (h + 1) * SPAN // 2)
                vec[h, j : j + 1, :] = jnp.where(t == 0, here[:, part], there[:, part])
                vec[h, 4 + j : 5 + j, :] = jnp.where(t == 0, there[:, part], here[:, part])
        bias = jnp.sum(bias_sum[...], 0, keepdims=True)
        bias = jnp.where(lax.broadcasted_iota(jnp.int32, (8, SPAN), 0) == y, bias, 0.0)
        for h in range(2):
            vec[h, 8:16, :] = bias[:, h * SPAN // 2 : (h + 1) * SPAN // 2]
        remote(Kind.v_c, 0, vec.at[other], vec_c, to_sib).start()

    def over_cores():
        arrived(Kind.v_c, 0, vec_c)
        vec_x[...] = vec[c] + vec_c[...]
        remote(Kind.v_x, 0, vec_x, vec_xin, to_x).start()

    def over_x():
        arrived(Kind.v_x, 0, vec_xin)
        vec_z[z] = vec_x[...] + vec_xin[...]
        for d in range(1, 4):
            remote(Kind.v_z, d, vec_z.at[z], vec_z.at[z], to_z[d]).start()

    def over_z():
        arrived(Kind.v_z, 0, vec_z.at[:3])
        total = (vec_z[0] + vec_z[1]) + (vec_z[2] + vec_z[3])
        vec_y[y] = total[:8]
        bias_y[y] = jnp.sum(total[8:], 0, keepdims=True)
        for d in range(1, 4):
            remote(Kind.v_y, d, vec_y.at[y], vec_y.at[y], to_y[d]).start()
            remote(Kind.b_y, d, bias_y.at[y], bias_y.at[y], to_y[d]).start()

    def over_y():
        arrived(Kind.v_y, 0, vec_y.at[:3])
        arrived(Kind.b_y, 0, bias_y.at[:3])
        vec_t[c, t, 0:8] = (vec_y[0] + vec_y[1]) + (vec_y[2] + vec_y[3])
        for j in range(4):
            vec_t[c, t, 8 + j : 9 + j] = bias_y[j]
        remote(Kind.v_t, 0, vec_t.at[c, t], vec_t.at[c, t], to_tower).start()

    def over_towers():
        arrived(Kind.v_t, 0, vec_t.at[c, 1 - t])
        remote(Kind.v_b, 0, vec_t.at[c], vec_t.at[c], to_sib).start()

    between = {
        3: (mixing, over_cores), 4: (lambda: late_in(0), over_x,), 6: (over_z,), 8: (over_y,), 9: (over_towers,),
    }

    def step(s):
        pl.when(s < CUTS)(lambda: products(s))
        pl.when(s < CUTS)(lambda: relays(s))
        pl.when((s >= 2) & (s < CUTS + 2))(lambda: sums(s - 2))
        pl.when((s >= 3) & (s < EARLY + 3))(lambda: ends(s - 3))
        for at, tasks in between.items():

            @pl.when(s == at)
            def _(tasks=tasks):
                for task in tasks:
                    task()

    loop(CUTS + 2, step)

    arrived(Kind.v_b, 0, vec_t.at[other])

    def half(ref, side):
        return ref.at[:, pl.ds(pl.multiple_of(side * HALF, HALF), HALF)]

    arrived(Kind.d_sib, 0, half(feat_out, other))
    arrived(Kind.g_sib, 0, half(grad_out, other))
    sent(Kind.opp_yp, d_opp)
    sent(Kind.sum_yp, xb.at[:, 0:2])
    sent(Kind.opp_zp, g_opp)
    sent(Kind.sum_zp, xb.at[:EARLY, 0:2])
    sent(Kind.late_opp_zp, late.at[:, 0])
    sent(Kind.late_sum_zp, late.at[:, 0:2])
    sent(Kind.g_x, g_send.at[:EARLY])
    sent(Kind.gb_x, late)
    sent(Kind.d_sib, xb.at[:, y, 0])
    sent(Kind.g_sib, half(grad_out, other))
    sent(Kind.cot, cot)
    sent(Kind.pg, pg.at[:, 0])
    sent(Kind.tow, hid)
    sent(Kind.hid, hid.at[:3])
    sent(Kind.v_z, vec_z.at[:3])
    sent(Kind.v_y, vec_y.at[:3])
    sent(Kind.b_y, bias_y.at[:3])
    sent(Kind.v_c, vec_c)
    sent(Kind.v_x, vec_x)
    sent(Kind.v_t, vec_c)
    sent(Kind.v_b, vec_t.at[c])
    sent(Kind.keep, grouped.at[c])


def towers(*operands):
    low, wide = jnp.bfloat16, jnp.float32
    scratch = [
        ((CUTS, 4, 2, OWN, CUT), low),
        ((CUTS + 1, 2, 4, OWN, CUT), low),
        ((4, 2, OWN, SPAN), wide),
        ((4, 2, OWN, SPAN), low),
        ((2, 4, OWN, SPAN), low),
        ((4, OWN, SPAN), low),
        ((4, OWN, SPAN), low),
        ((4, OWN, SPAN), low),
        ((4, OWN, SPAN), low),
        ((4, OWN, SPAN), low),
        ((CUTS, 2, OWN, CUT), low),
        ((EARLY, 2, OWN, CUT), low),
        ((LATE, 4, OWN, CUT), low),
        ((CUTS, OWN, CUT), low),
        ((CUTS, OWN, CUT), low),
        ((CUTS, 2, OWN, CUT), low),
        ((CUTS, 2, OWN, CUT), low),
        ((CUTS, OWN, CUT), low),
        ((CUTS, OWN, CUT), low),
        ((CUTS, 2, OWN, CUT), low),
        ((CUTS, 2, OWN, CUT), low),
        ((CUTS, OWN, CUT), low),
        ((CUTS, OWN, CUT), low),
        ((1, OWN), jnp.int32),
        ((1, FEAT), jnp.int32),
        ((2, 2, OUT), wide),
        ((1, OUT), wide),
        ((2, OWN, OWN), low),
        ((1, FEAT), low),
        ((4, 8, SPAN), wide),
        ((8, SPAN), wide),
        ((2, 16, SPAN // 2), wide),
        ((16, SPAN // 2), wide),
        ((16, SPAN // 2), wide),
        ((16, SPAN // 2), wide),
        ((4, 16, SPAN // 2), wide),
        ((4, 8, SPAN // 2), wide),
        ((4, 1, SPAN // 2), wide),
    ]
    anywhere, near = pl.BlockSpec(memory_space=pl.ANY), pl.BlockSpec(memory_space=pltpu.VMEM)
    return pl.pallas_call(
        body,
        out_shape=[
            pltpu.VMEM((OWN, OUT), low),
            pltpu.VMEM((OWN, FEAT), low),
            pltpu.VMEM((ROWS, FEAT), wide),
            pltpu.VMEM((2, 2, 16, SPAN // 2), wide),
        ],
        in_specs=[anywhere] * 7,
        out_specs=[near] * 4,
        scratch_shapes=[pltpu.VMEM(shape, kind) for shape, kind in scratch]
        + [
            pltpu.SemaphoreType.DMA((len(set(LEAVES.values())),)),
            pltpu.SemaphoreType.DMA((len(ROWED), CUTS)),
            pltpu.SemaphoreType.DMA((sum(FEW.values()),)),
            pltpu.SemaphoreType.DMA((CUTS,)),
            pltpu.SemaphoreType.DMA((len(Local),)),
            pltpu.SemaphoreType.REGULAR,
            pltpu.SemaphoreType.REGULAR,
            pltpu.SemaphoreType.REGULAR,
        ],
        compiler_params=pltpu.CompilerParams(
            collective_id=0, has_side_effects=True, vmem_limit_bytes=GRANT
        ),
    )(*operands)


def closing(
    mixed_in, feat_in, grad_in, vec_in, momentum, weights,
    mixed, feat, grad, stitch, bias, new_momentum, new_weights,
    stitch_here, bias_here, weights_here, moved, result, sem,
):
    t = lax.axis_index("tower")
    started = []

    def start(count, src, dst):
        size = src.shape[0] // count
        for i in range(count):
            first = len(started)
            part = pl.ds(i * size, size)
            started.append(pltpu.make_async_copy(src.at[part], dst.at[part], sem.at[first]))
            started[-1].start()
        return started[-count:]

    loads = start(PARTS, weights, weights_here)
    start(PARTS, grad_in, grad)
    start(2, feat_in, feat)
    start(2, mixed_in, mixed)
    size = ROWS // PARTS
    for i in range(PARTS):
        rows = pl.ds(i * size, size)
        moved[rows] = momentum_rate * momentum[rows] + grad_in[rows]
        start(1, moved.at[rows], new_momentum.at[rows])
        loads[i].wait()
        result[rows] = weights_here[rows].astype(jnp.float32) - learn_rate * moved[rows]
        start(1, result.at[rows], new_weights.at[rows])
    for j in range(4):
        for h in range(2):
            part = slice((2 * j + h) * SPAN // 2, (2 * j + h + 1) * SPAN // 2)
            for s in range(2):
                for u in range(2):
                    stitch_here[s, u : u + 1, part] = vec_in[h, s, 4 * u + j : 4 * u + j + 1, :]
            bias_here[0:1, part] = vec_in[h, t, 8 + j : 9 + j, :]
    start(1, stitch_here, stitch)
    start(1, bias_here, bias)
    for copy in started[PARTS:]:
        copy.wait()


def close(mixed, feat, grad, vec, momentum, weights):
    anywhere, near = pl.BlockSpec(memory_space=pl.ANY), pl.BlockSpec(memory_space=pltpu.VMEM)
    small = [jax.ShapeDtypeStruct((2, 2, OUT), jnp.float32), jax.ShapeDtypeStruct((1, OUT), jnp.float32)]
    shapes = [*(jax.ShapeDtypeStruct(v.shape, v.dtype) for v in (mixed, feat, grad)), *small]
    shapes += [jax.ShapeDtypeStruct(grad.shape, grad.dtype)] * 2
    kept_near = [pltpu.with_memory_space_constraint(v, pltpu.VMEM) for v in (mixed, feat, grad, vec, momentum)]
    return pl.pallas_call(
        closing,
        out_shape=shapes,
        in_specs=[near] * 5 + [anywhere],
        out_specs=[anywhere] * 7,
        scratch_shapes=[pltpu.VMEM(v.shape, v.dtype) for v in (*small, weights, grad, grad)]
        + [pltpu.SemaphoreType.DMA((4 * PARTS + 6,))],
        compiler_params=pltpu.CompilerParams(vmem_limit_bytes=GRANT),
        cost_estimate=pl.CostEstimate(flops=0, bytes_accessed=14_000_000, transcendentals=0),
    )(*kept_near, weights)


def shards(features, group, pad_mask, weights, bias, stitch, momentum, cotangent):
    sums = towers(features[0], weights[0], cotangent[0], group[None], pad_mask[None], stitch, bias)
    mixed, feat_grad, weight_grad, stitch_grad, bias_grad, new_momentum, new_weights = close(
        *sums, momentum[0], weights[0]
    )
    return (
        mixed[None], feat_grad[None], weight_grad[None], bias_grad, stitch_grad, new_momentum[None], new_weights[None]
    )


def solution(mesh):
    placed = (
        P("tower", "blk", None),
        P("blk"),
        P(),
        P("tower", "blk", None),
        P("tower", None),
        P(),
        P("tower", "blk", None),
        P("tower", "blk", None),
    )
    return jax.shard_map(
        shards,
        mesh=mesh,
        in_specs=placed,
        out_specs=(
            P("tower", "blk", None),
            P("tower", "blk", None),
            P("tower", "blk", None),
            P("tower", None),
            P(),
            P("tower", "blk", None),
            P("tower", "blk", None),
        ),
        check_vma=False,
    )
```

```python
import enum

import jax
import jax.numpy as jnp
from jax import lax
from jax.experimental import pallas as pl
from jax.experimental.pallas import tpu as pltpu
from jax.sharding import PartitionSpec as P

momentum_rate = 0.9
learn_rate = 0.0001

FEAT = 9216
OUT = 4096
HALF = FEAT // 2
OWN = 128
ROWS = 64
SPAN = 1024
CUT = 512
CUTS = HALF // CUT
LATE = 2
EARLY = CUTS - LATE
AHEAD = 4
PARTS = 4
GRANT = 56 << 20
STRIP = 32
ORDER = (2, 1, 3, 0)


class Kind(enum.IntEnum):
    (
        x_sib, w_sib, w_x, own_yp, own_ym, own_zp, own_zm, pair_zp, pair_zm, sib_yp, sib_ym, fwd_yp, fwd_ym, fwd_zp, fwd_zm,
        opp_yp, opp_ym, opp_zp, opp_zm, sum_yp, sum_ym, sum_zp, sum_zm, g_x, d_sib, g_sib, late_opp_zp, late_opp_zm,
        late_sum_zp, late_sum_zm, keep, cot, hg, pre, pg, hid, tow, gb_x, v_c, v_x, v_z, v_y, b_y, v_t, v_b,
    ) = range(45)


class Local(enum.IntEnum):
    w, cot, small, small_1, small_2, small_3 = range(6)


ROWED = (
    (Kind.x_sib, Kind.w_sib, Kind.g_x),
    (Kind.w_x, Kind.sum_zp, Kind.sum_zm, Kind.late_sum_zp, Kind.late_sum_zm),
    (Kind.own_yp, Kind.sib_yp, Kind.opp_yp),
    (Kind.own_ym, Kind.sib_ym, Kind.opp_ym),
    (Kind.own_zp, Kind.pair_zp, Kind.opp_zp, Kind.late_opp_zp),
    (Kind.own_zm, Kind.pair_zm, Kind.opp_zm, Kind.late_opp_zm),
    (Kind.fwd_yp, Kind.fwd_ym, Kind.fwd_zp, Kind.fwd_zm, Kind.sum_yp, Kind.sum_ym),
)
ROW = {kind: row for row, kinds in enumerate(ROWED) for kind in kinds}
FEW = {
    Kind.keep: 1, Kind.cot: 1, Kind.hg: 4, Kind.pre: 4, Kind.pg: 4, Kind.hid: 1, Kind.tow: 1, Kind.gb_x: LATE, Kind.v_c: 1,
    Kind.v_x: 1, Kind.v_z: 1, Kind.v_y: 1, Kind.b_y: 1, Kind.v_t: 1, Kind.v_b: 1, Kind.d_sib: 1, Kind.g_sib: 1,
}
FIRST = {kind: sum(list(FEW.values())[:place]) for place, kind in enumerate(FEW)}
TOGETHER = (
    (Kind.own_yp, Kind.own_ym, Kind.sib_yp, Kind.sib_ym, Kind.fwd_yp, Kind.fwd_ym),
    (
        Kind.own_zp, Kind.own_zm, Kind.pair_zp, Kind.pair_zm, Kind.fwd_zp, Kind.fwd_zm, Kind.w_x, Kind.x_sib,
    ),
    (Kind.opp_yp, Kind.opp_ym),
    (Kind.sum_yp, Kind.sum_ym),
    (Kind.opp_zp, Kind.opp_zm),
    (Kind.sum_zp, Kind.sum_zm),
    (Kind.late_opp_zp, Kind.late_opp_zm),
    (Kind.late_sum_zp, Kind.late_sum_zm),
)
LEAVES = {kind: group for group, kinds in enumerate(TOGETHER) for kind in kinds}
for _kind in Kind:
    LEAVES.setdefault(_kind, len(set(LEAVES.values())))


def body(
    features, weights, cotangent, group_in, pad_in, stitch_in, bias_in,
    mixed_out, feat_out, grad_out, vec_t,
    xb, wb, pre, pg, pgt, cot, cot_in, hg_send, hg, hid, d_opp, g_opp, late,
    relay_yp, relay_ym, part_yp, part_ym, relay_zp, relay_zm, part_zp, part_zm,
    g_send, g_in, group, pad, stitch, bias, grouped, absent, coef, bias_sum, vec, vec_c, vec_x, vec_xin, vec_z, vec_y, bias_y,
    send_sem, row_sem, few_sem, load_sem, local_sem, room_sem, chips_sem, all_sem,
):
    blk, t = lax.axis_index("blk"), lax.axis_index("tower")
    y, x, z, c = blk // 16, (blk // 8) % 2, (blk // 2) % 4, blk % 2
    other = 1 - c

    def place(y, x, z, c):
        return ((y * 2 + x) * 4 + z) * 2 + c

    yp, yo, ym = (y + 1) % 4, (y + 2) % 4, (y + 3) % 4
    zp, zo, zm = (z + 1) % 4, (z + 2) % 4, (z + 3) % 4
    to_yp, to_yo, to_ym = ((place(v, x, z, c), t) for v in (yp, yo, ym))
    to_zp, to_zo, to_zm = ((place(y, x, v, c), t) for v in (zp, zo, zm))
    to_x = (place(y, 1 - x, z, c), t)
    to_sib = (place(y, x, z, other), t)
    to_tower = (blk, 1 - t)
    to_y = (None, to_yp, to_yo, to_ym)
    to_z = (None, to_zp, to_zo, to_zm)

    def remote(kind, k, src, dst, device):
        if kind in ROW:
            landed = row_sem.at[ROW[kind], k]
        else:
            landed = few_sem.at[FIRST[kind] + (k if FEW[kind] > 1 else 0)]
        return pltpu.make_async_remote_copy(
            src_ref=src, dst_ref=dst, send_sem=send_sem.at[LEAVES[kind]], recv_sem=landed,
            device_id=device, device_id_type=pl.DeviceIdType.MESH,
        )

    def arrived(kind, k, dst):
        remote(kind, k, dst, dst, to_sib).wait_recv()

    def sent(kind, src):
        remote(kind, 0, src, src, to_sib).wait_send()

    def local(kind, src, dst):
        return pltpu.make_async_copy(src, dst, local_sem.at[kind])

    def columns(side, k):
        return pl.ds(pl.multiple_of(side * HALF + k * CUT, CUT), CUT)

    def loop(count, step):
        lax.fori_loop(0, count, lambda k, carry: (step(k), carry)[1], 0)

    hid_other = hg
    hid_send = cot_in
    staged = g_send
    TOP, LOW = pl.ds(0, OWN // 2), pl.ds(OWN // 2, OWN // 2)
    own_rows = pl.ds(pl.multiple_of(c * ROWS, ROWS), ROWS)
    sib_rows = pl.ds(pl.multiple_of(other * ROWS, ROWS), ROWS)

    def load_x(k):
        return pltpu.make_async_copy(features.at[:, columns(c, k)], xb.at[k, y, c], load_sem.at[k])

    def load_other(k):
        return pltpu.make_async_copy(features.at[:, columns(other, k)], staged.at[k], load_sem.at[k])

    def load_w(k):
        return local(Local.w, weights.at[:, columns(c, k)], wb.at[k, x, z, own_rows])

    def start_loads(k):
        load_x(k).start()
        load_other(k).start()
        load_w(k).start()

    barrier = pltpu.get_barrier_semaphore()
    along_y, across = (to_yp, to_yo, to_ym), (to_zp, to_zo, to_zm, to_x, to_tower)

    def signal(sem, device):
        pl.semaphore_signal(sem, inc=1, device_id=device, device_id_type=pl.DeviceIdType.MESH)

    def greet(sem):
        for core, devices in enumerate((along_y, across)):

            @pl.when(c == core)
            def _(devices=devices):
                for device in devices:
                    signal(sem, device)

    greeted = len(along_y) + c * (len(across) - len(along_y))
    signal(barrier, to_sib)
    greet(barrier)

    small = [
        local(Local.small + i, src, dst)
        for i, (src, dst) in enumerate(((group_in, group), (pad_in, pad), (stitch_in, stitch), (bias_in, bias)))
    ]
    for copy in small[:2]:
        copy.start()
    loop(CUTS, start_loads)
    for copy in small[2:]:
        copy.start()
    for j in range(4):
        local(Local.cot, cotangent.at[:, pl.ds(j * SPAN, SPAN)], cot.at[j]).start()

    for copy in small[:2]:
        copy.wait()
    grouped[c] = jnp.broadcast_to(group[...].astype(jnp.float32), (OWN, OWN)).T.astype(jnp.bfloat16)
    absent[...] = 1.0 - pad[...].astype(jnp.float32).astype(jnp.bfloat16)

    def kept(value, core, side, k):
        rows = jnp.concatenate([grouped[core]] * (CUT // OWN), 1)
        return value * (1.0 - rows * absent[0:1, columns(side, k)])

    def masked(k):
        pltpu.make_async_copy(xb.at[k, y], xb.at[k, y], load_sem.at[k]).wait()
        staged[k] = kept(staged[k], c, other, k)
        xb[k, y, c] = kept(xb[k, y, c], c, c, k)

    masked(0)
    pl.semaphore_wait(barrier, greeted + 1)
    greet(chips_sem)

    def x_sib(k):
        return remote(Kind.x_sib, k, staged.at[k], xb.at[k, y, c], to_sib)

    def w_sib(k):
        return remote(Kind.w_sib, k, weights.at[:, columns(other, k)], wb.at[k, x, z, own_rows], to_sib)

    def own_y(k):
        remote(Kind.own_yp, k, xb.at[k, y, c], xb.at[k, y, c], to_yp).start()
        remote(Kind.own_ym, k, xb.at[k, y, c], xb.at[k, y, c], to_ym).start()

    def to_sibling(k):
        x_sib(k).start()
        w_sib(k).start()

    def own_out(k):
        arrived(Kind.x_sib, k, xb.at[k, y, :, : (OWN + ROWS) // 2])
        remote(Kind.sib_yp, k, xb.at[k, y, other], xb.at[k, y, other], to_yp).start()
        remote(Kind.sib_ym, k, xb.at[k, y, other], xb.at[k, y, other], to_ym).start()
        remote(Kind.w_x, k, wb.at[k, x, z], wb.at[k, x, z], to_x).start()
        remote(Kind.own_zp, k, wb.at[k, x, z], wb.at[k, x, z], to_zp).start()
        remote(Kind.own_zm, k, wb.at[k, x, z], wb.at[k, x, z], to_zm).start()

    every_w = wb.at[:CUTS, x, z]

    def ahead(k):
        pl.when(k > 0)(lambda: masked(k))
        pl.when(c == 0)(lambda: own_y(k))
        to_sibling(k)

    def first(k):
        @pl.when(k < CUTS)
        def _():
            masked(k)
            own_y(k)
            to_sibling(k)

        own_out(k - AHEAD)

    loop(AHEAD, ahead)
    pl.semaphore_wait(chips_sem, greeted)
    signal(all_sem, to_sib)
    pl.semaphore_wait(all_sem, 1)
    pl.when(c == 1)(lambda: loop(AHEAD, own_y))
    every = wb.at[:CUTS, x, z, own_rows]
    local(Local.w, every, every).wait()
    loop(CUTS, lambda k: first(k + AHEAD))
    remote(Kind.keep, 0, grouped.at[c], grouped.at[c], to_sib).start()
    for j in range(4):
        remote(Kind.cot, j, cotangent.at[:, pl.ds(j * SPAN, SPAN)], cot_in.at[j], to_tower).start()

    def pair_out(k):
        arrived(Kind.w_x, k, wb.at[k, 1 - x, z])
        remote(Kind.pair_zp, k, wb.at[k, 1 - x, z], wb.at[k, 1 - x, z], to_zp).start()
        remote(Kind.pair_zm, k, wb.at[k, 1 - x, z], wb.at[k, 1 - x, z], to_zm).start()

    loop(CUTS, pair_out)

    def forward(k):
        arrived(Kind.own_yp, k, xb.at[k, ym])
        arrived(Kind.own_ym, k, xb.at[k, yp])
        remote(Kind.fwd_yp, k, xb.at[k, ym, 0], xb.at[k, ym, 0], to_yp).start()
        remote(Kind.fwd_ym, k, xb.at[k, yp, 1], xb.at[k, yp, 1], to_ym).start()
        arrived(Kind.own_zp, k, wb.at[k, :, zm])
        arrived(Kind.own_zm, k, wb.at[k, :, zp])
        remote(Kind.fwd_zp, k, wb.at[k, x, zm], wb.at[k, x, zm], to_zp).start()
        remote(Kind.fwd_zm, k, wb.at[k, 1 - x, zp], wb.at[k, 1 - x, zp], to_zm).start()

    loop(CUTS, forward)

    for copy in small[2:]:
        copy.wait()
    for j in range(4):
        part = slice(j * SPAN, (j + 1) * SPAN)
        coef[j, 0:1, :] = jnp.where(t == 0, stitch[0, 0:1, part], stitch[1, 1:2, part])
        coef[j, 1:2, :] = jnp.where(t == 0, stitch[1, 0:1, part], stitch[0, 1:2, part])
        coef[j, 2:3, :] = jnp.where(t == 0, stitch[0, 1:2, part], stitch[1, 0:1, part])
        coef[j, 3:4, :] = bias[0:1, part]
    local(Local.cot, cot, cot).wait()
    arrived(Kind.cot, 0, cot_in)
    for d in ORDER:
        j = (y + d) % 4

        def combine(i, d=d, j=j):
            rows = pl.ds(pl.multiple_of(i * STRIP, STRIP), STRIP)
            value = (
                coef[j, 0:1, :] * cot[j, rows, :].astype(jnp.float32)
                + coef[j, 1:2, :] * cot_in[j, rows, :].astype(jnp.float32)
            ).astype(jnp.bfloat16)
            if d == 0:
                hg[y, rows, :] = value
            else:
                hg_send[j, rows, :] = value

        loop(OWN // STRIP, combine)
        if d:
            remote(Kind.hg, d, hg_send.at[j], hg.at[y], to_y[d]).start()

    def pre_in(i):
        return grad_out.at[:, pl.ds(pl.multiple_of(i * SPAN, SPAN), SPAN)]

    def gathered(k):
        arrived(Kind.fwd_yp, k, xb.at[k, 0:2])

    def add_block(k, b):
        pre[b] += lax.dot_general(
            xb[k, b].reshape(2 * OWN, CUT), wb[k].reshape(SPAN, CUT),
            (((1,), (1,)), ((), ())), preferred_element_type=jnp.float32,
        ).reshape(2, OWN, SPAN)

    def add_product(k):
        gathered(k)
        loop(4, lambda b: add_block(k, b))

    def clear(b):
        pre[b] = jnp.zeros((2, OWN, SPAN), jnp.float32)

    loop(4, clear)
    loop(CUTS - 1, add_product)
    gathered(CUTS - 1)

    for d in ORDER:
        b = (y + d) % 4
        add_block(CUTS - 1, b)
        for h in range(2):
            part = pl.ds(h * ROWS, ROWS)
            remote(Kind.pre, d, pre.at[b, other, part], pre_in(2 * d + h), to_sib).start()
    bias_sum[...] = jnp.zeros_like(bias_sum)

    def activate(d):
        b = (y + d) % 4
        arrived(Kind.pre, d, pre.at[b, other])
        if d:
            arrived(Kind.hg, 4 - d, hg.at[b])

        def act(i):
            rows = pl.ds(pl.multiple_of(i * STRIP, STRIP), STRIP)
            per = ROWS // STRIP
            rows_in = pl.ds(pl.multiple_of((i % per) * STRIP, STRIP), STRIP)
            value = pre[b, c, rows, :] + pre_in(2 * d + i // per)[rows_in, :] + coef[y, 3:4, :]
            gate = jax.nn.sigmoid(value)
            hidden = (value * gate).astype(jnp.bfloat16)
            grad = (hg[b, rows, :].astype(jnp.float32) * gate * (1.0 + value * (1.0 - gate))).astype(jnp.bfloat16)
            pg[b, c, rows, :] = grad
            if d == 0:
                hid[y, rows, :] = hidden
            else:
                hid_send[b, rows, :] = hidden
            bias_sum[...] += jnp.sum(grad.astype(jnp.float32).reshape(STRIP // 8, 8, SPAN), 0)

        loop(OWN // STRIP, act)
        remote(Kind.pg, d, pg.at[b, c], pg.at[b, c], to_sib).start()
        if d:
            remote(Kind.hid, d, hid_send.at[b], hid.at[y], to_y[d]).start()

    def product_d(k, b):
        product = jnp.dot(
            pg[b].reshape(2 * OWN, SPAN), wb[k].reshape(SPAN, CUT), preferred_element_type=jnp.float32
        )
        return product.astype(jnp.bfloat16).reshape(2, OWN, CUT)

    def product_late(k, side):
        return jnp.dot(
            pgt[side].reshape(4 * OWN, SPAN), xb[k].reshape(SPAN, CUT), preferred_element_type=jnp.float32
        ).reshape(4, OWN, CUT)

    def product_g(k, v):
        product = jnp.dot(
            pgt[:, v].reshape(2 * OWN, SPAN), xb[k].reshape(SPAN, CUT), preferred_element_type=jnp.float32
        )
        return product.astype(jnp.bfloat16).reshape(2, OWN, CUT)

    def late_away(i):
        away = hg_send.at[:, :, i * CUT : (i + 1) * CUT]
        away[...] = product_late(EARLY + i, 1 - x).astype(jnp.bfloat16)
        remote(Kind.gb_x, i, away, late.at[i], to_x).start()

    def opposite_d(k):
        d_opp[k] = product_d(k, yo)
        remote(Kind.opp_yp, k, d_opp.at[k, 0], relay_yp.at[k], to_yp).start()
        remote(Kind.opp_ym, k, d_opp.at[k, 1], relay_ym.at[k], to_ym).start()

    def opposite_g(k):
        g_opp[k] = product_g(k, zo)
        remote(Kind.opp_zp, k, g_opp.at[k, 0], relay_zp.at[k], to_zp).start()
        remote(Kind.opp_zm, k, g_opp.at[k, 1], relay_zm.at[k], to_zm).start()

    for d in ORDER:
        activate(d)
    pl.semaphore_signal(room_sem, inc=1, device_id=to_tower, device_id_type=pl.DeviceIdType.MESH)
    for d in ORDER:
        arrived(Kind.pg, d, pg.at[(y + d) % 4, other])
        if d == 2:
            loop(CUTS, opposite_d)

    wide = 256
    eye = (
        lax.broadcasted_iota(jnp.int32, (wide, wide), 0) == lax.broadcasted_iota(jnp.int32, (wide, wide), 1)
    ).astype(jnp.bfloat16)
    for o in range(SPAN // wide):
        flipped = lax.dot_general(
            eye, pg[:, :, :, o * wide : (o + 1) * wide].reshape(SPAN, wide),
            (((1,), (1,)), ((), ())), preferred_element_type=jnp.float32,
        )
        pgt[o // 2, (o % 2) * 2 : (o % 2) * 2 + 2] = flipped.astype(jnp.bfloat16).reshape(2, OWN, SPAN)
    loop(EARLY, opposite_g)
    arrived(Kind.hid, 0, hid.at[:3])
    pl.semaphore_wait(room_sem, 1)
    for j in range(4):
        remote(Kind.tow, j, hid.at[j], hid_other.at[j], to_tower).start()
    sent(Kind.hg, hg_send.at[:3])
    late_away(0)

    sent(Kind.w_sib, wb.at[:CUTS, x, z, own_rows])
    sent(Kind.own_yp, xb.at[:, 0:3])
    sent(Kind.own_zp, xb)
    sent(Kind.pre, pre.at[:, other])
    arrived(Kind.keep, 0, grouped.at[other])

    def slot(k):
        return (k + CUTS) % (CUTS + 1)

    def g_keep(k):
        part = pl.ds(pl.multiple_of((k % (SPAN // CUT)) * CUT, CUT), CUT)
        block = k // (SPAN // CUT)
        return pre.at[block // 2, block % 2, :, part]

    def products(k):
        s = slot(k)

        def block_g(i):
            v = (zo + 1 + i) % 4
            wb[s, :, v] = product_g(k, v)

        def block_d(i):
            b = (yo + 1 + i) % 4
            xb[k, b] = product_d(k, b)

        pl.when(k < EARLY)(lambda: loop(3, block_g))
        loop(3, block_d)

    def late_in(i):
        k = EARLY + i
        arrived(Kind.gb_x, i, late.at[i])

        late[i] = (product_late(k, x) + late[i].astype(jnp.float32)).astype(jnp.bfloat16)
        remote(Kind.late_opp_zp, k, late.at[i, zo, TOP], relay_zp.at[k, TOP], to_zp).start()
        remote(Kind.late_opp_zm, k, late.at[i, zo, LOW], relay_zm.at[k, TOP], to_zm).start()

    def wide_sum(*terms):
        total = terms[0].astype(jnp.float32)
        for term in terms[1:]:
            total += term.astype(jnp.float32)
        return total

    def relays(k):
        arrived(Kind.opp_yp, k, relay_yp.at[k])
        xb[k, yp, 0] = wide_sum(xb[k, yp, 0], relay_yp[k]).astype(jnp.bfloat16)
        remote(Kind.sum_yp, k, xb.at[k, yp], part_yp.at[k], to_yp).start()
        arrived(Kind.opp_ym, k, relay_ym.at[k])
        xb[k, ym, 1] = wide_sum(xb[k, ym, 1], relay_ym[k]).astype(jnp.bfloat16)
        remote(Kind.sum_ym, k, xb.at[k, ym], part_ym.at[k], to_ym).start()
        pl.when(k < EARLY)(lambda: relays_z(k))
        pl.when(k >= EARLY)(lambda: relays_late(k))

    def relays_z(k):
        s = slot(k)
        arrived(Kind.opp_zp, k, relay_zp.at[k])
        wb[s, 0, zp] = wide_sum(wb[s, 0, zp], relay_zp[k]).astype(jnp.bfloat16)
        remote(Kind.sum_zp, k, wb.at[s, :, zp], part_zp.at[k], to_zp).start()
        arrived(Kind.opp_zm, k, relay_zm.at[k])
        wb[s, 1, zm] = wide_sum(wb[s, 1, zm], relay_zm[k]).astype(jnp.bfloat16)
        remote(Kind.sum_zm, k, wb.at[s, :, zm], part_zm.at[k], to_zm).start()

    def relays_late(k):
        i = k - EARLY
        arrived(Kind.late_opp_zp, k, relay_zp.at[k, TOP])
        late[i, zp, TOP] = wide_sum(late[i, zp, TOP], relay_zp[k, TOP]).astype(jnp.bfloat16)
        remote(Kind.late_sum_zp, k, late.at[i, zp], part_zp.at[k, 0], to_zp).start()
        arrived(Kind.late_opp_zm, k, relay_zm.at[k, TOP])
        late[i, zm, LOW] = wide_sum(late[i, zm, LOW], relay_zm[k, TOP]).astype(jnp.bfloat16)
        remote(Kind.late_sum_zm, k, late.at[i, zm], part_zm.at[k, 0], to_zm).start()

    def grad_done(k):
        remote(Kind.g_sib, 0, g_keep(k).at[sib_rows], grad_out.at[:, columns(c, k)], to_sib).start()
        grad_out[:, columns(c, k)] = g_keep(k)[own_rows, :]

    def sums_z(k):
        s = slot(k)
        arrived(Kind.sum_zp, k, xb.at[k, 0:2])
        g_send[k] = wide_sum(wb[s, 1 - x, z], part_zp[k, 1 - x], part_zm[k, 1 - x]).astype(jnp.bfloat16)
        remote(Kind.g_x, k, g_send.at[k], g_in.at[k], to_x).start()
        g_keep(k)[...] = wide_sum(wb[s, x, z], part_zp[k, x], part_zm[k, x])

    def sums_late(k):
        arrived(Kind.late_sum_zp, k, xb.at[k, 0])
        g_keep(k)[...] = wide_sum(late[k - EARLY, z], part_zp[k, 0], part_zm[k, 0])
        grad_done(k)

    def sums(k):
        pl.when(k < EARLY)(lambda: sums_z(k))
        pl.when(k >= EARLY)(lambda: sums_late(k))
        arrived(Kind.sum_yp, k, xb.at[k, 0:2])
        theirs = wide_sum(xb[k, y, other], part_yp[k, other], part_ym[k, other])
        xb[k, y, other] = kept(theirs.astype(jnp.bfloat16), other, c, k)
        remote(Kind.d_sib, 0, xb.at[k, y, other], feat_out.at[:, columns(c, k)], to_sib).start()
        ours = wide_sum(xb[k, y, c], part_yp[k, c], part_ym[k, c])
        feat_out[:, columns(c, k)] = kept(ours.astype(jnp.bfloat16), c, c, k)

    def ends(k):
        arrived(Kind.g_x, k, g_in.at[k])
        g_keep(k)[...] += g_in[k].astype(jnp.float32)
        grad_done(k)

    def mixing():
        arrived(Kind.tow, 0, hid_other)
        for j in range(4):

            def strip(i, sums, j=j):
                rows = pl.ds(pl.multiple_of(i * STRIP, STRIP), STRIP)
                here = hid[j, rows, :].astype(jnp.float32)
                there = hid_other[j, rows, :].astype(jnp.float32)
                mixed_out[rows, j * SPAN : (j + 1) * SPAN] = (coef[j, 0:1, :] * here + coef[j, 2:3, :] * there).astype(jnp.bfloat16)
                up = cot[j, rows, :].astype(jnp.float32)
                return (
                    sums[0] + jnp.sum((up * here).reshape(STRIP // 8, 8, SPAN), 0),
                    sums[1] + jnp.sum((up * there).reshape(STRIP // 8, 8, SPAN), 0),
                )

            zero = jnp.zeros((8, SPAN), jnp.float32)
            here, there = lax.fori_loop(0, OWN // STRIP, strip, (zero, zero))
            here, there = jnp.sum(here, 0, keepdims=True), jnp.sum(there, 0, keepdims=True)
            for h in range(2):
                part = slice(h * SPAN // 2, (h + 1) * SPAN // 2)
                vec[h, j : j + 1, :] = jnp.where(t == 0, here[:, part], there[:, part])
                vec[h, 4 + j : 5 + j, :] = jnp.where(t == 0, there[:, part], here[:, part])
        bias = jnp.sum(bias_sum[...], 0, keepdims=True)
        bias = jnp.where(lax.broadcasted_iota(jnp.int32, (8, SPAN), 0) == y, bias, 0.0)
        for h in range(2):
            vec[h, 8:16, :] = bias[:, h * SPAN // 2 : (h + 1) * SPAN // 2]
        remote(Kind.v_c, 0, vec.at[other], vec_c, to_sib).start()

    def over_cores():
        arrived(Kind.v_c, 0, vec_c)
        vec_x[...] = vec[c] + vec_c[...]
        remote(Kind.v_x, 0, vec_x, vec_xin, to_x).start()

    def over_x():
        arrived(Kind.v_x, 0, vec_xin)
        vec_z[z] = vec_x[...] + vec_xin[...]
        for d in range(1, 4):
            remote(Kind.v_z, d, vec_z.at[z], vec_z.at[z], to_z[d]).start()

    def over_z():
        arrived(Kind.v_z, 0, vec_z.at[:3])
        total = (vec_z[0] + vec_z[1]) + (vec_z[2] + vec_z[3])
        vec_y[y] = total[:8]
        bias_y[y] = jnp.sum(total[8:], 0, keepdims=True)
        for d in range(1, 4):
            remote(Kind.v_y, d, vec_y.at[y], vec_y.at[y], to_y[d]).start()
            remote(Kind.b_y, d, bias_y.at[y], bias_y.at[y], to_y[d]).start()

    def over_y():
        arrived(Kind.v_y, 0, vec_y.at[:3])
        arrived(Kind.b_y, 0, bias_y.at[:3])
        vec_t[c, t, 0:8] = (vec_y[0] + vec_y[1]) + (vec_y[2] + vec_y[3])
        for j in range(4):
            vec_t[c, t, 8 + j : 9 + j] = bias_y[j]
        remote(Kind.v_t, 0, vec_t.at[c, t], vec_t.at[c, t], to_tower).start()

    def over_towers():
        arrived(Kind.v_t, 0, vec_t.at[c, 1 - t])
        remote(Kind.v_b, 0, vec_t.at[c], vec_t.at[c], to_sib).start()

    between = {
        3: (mixing, over_cores), 4: (over_x, lambda: late_away(1), lambda: late_in(0)), 6: (over_z, lambda: late_in(1)),
        8: (over_y,), 9: (over_towers,),
    }

    def step(s):
        pl.when(s < CUTS)(lambda: products(s))
        pl.when(s < CUTS)(lambda: relays(s))
        pl.when((s >= 2) & (s < CUTS + 2))(lambda: sums(s - 2))
        pl.when((s >= 4) & (s < EARLY + 4))(lambda: ends(s - 4))
        for at, tasks in between.items():

            @pl.when(s == at)
            def _(tasks=tasks):
                for task in tasks:
                    task()

    loop(CUTS + 2, step)

    arrived(Kind.v_b, 0, vec_t.at[other])

    def half(ref, side):
        return ref.at[:, pl.ds(pl.multiple_of(side * HALF, HALF), HALF)]

    arrived(Kind.d_sib, 0, half(feat_out, other))
    arrived(Kind.g_sib, 0, half(grad_out, other))
    sent(Kind.opp_yp, d_opp)
    sent(Kind.sum_yp, xb.at[:, 0:2])
    sent(Kind.opp_zp, g_opp)
    sent(Kind.sum_zp, xb.at[:EARLY, 0:2])
    sent(Kind.late_opp_zp, late.at[:, 0])
    sent(Kind.late_sum_zp, late.at[:, 0:2])
    sent(Kind.g_x, g_send.at[:EARLY])
    sent(Kind.gb_x, late)
    sent(Kind.d_sib, xb.at[:, y, 0])
    sent(Kind.g_sib, half(grad_out, other))
    sent(Kind.cot, cot)
    sent(Kind.pg, pg.at[:, 0])
    sent(Kind.tow, hid)
    sent(Kind.hid, hid.at[:3])
    sent(Kind.v_z, vec_z.at[:3])
    sent(Kind.v_y, vec_y.at[:3])
    sent(Kind.b_y, bias_y.at[:3])
    sent(Kind.v_c, vec_c)
    sent(Kind.v_x, vec_x)
    sent(Kind.v_t, vec_c)
    sent(Kind.v_b, vec_t.at[c])
    sent(Kind.keep, grouped.at[c])


def towers(*operands):
    low, wide = jnp.bfloat16, jnp.float32
    scratch = [
        ((CUTS, 4, 2, OWN, CUT), low),
        ((CUTS + 1, 2, 4, OWN, CUT), low),
        ((4, 2, OWN, SPAN), wide),
        ((4, 2, OWN, SPAN), low),
        ((2, 4, OWN, SPAN), low),
        ((4, OWN, SPAN), low),
        ((4, OWN, SPAN), low),
        ((4, OWN, SPAN), low),
        ((4, OWN, SPAN), low),
        ((4, OWN, SPAN), low),
        ((CUTS, 2, OWN, CUT), low),
        ((EARLY, 2, OWN, CUT), low),
        ((LATE, 4, OWN, CUT), low),
        ((CUTS, OWN, CUT), low),
        ((CUTS, OWN, CUT), low),
        ((CUTS, 2, OWN, CUT), low),
        ((CUTS, 2, OWN, CUT), low),
        ((CUTS, OWN, CUT), low),
        ((CUTS, OWN, CUT), low),
        ((CUTS, 2, OWN, CUT), low),
        ((CUTS, 2, OWN, CUT), low),
        ((CUTS, OWN, CUT), low),
        ((EARLY, OWN, CUT), low),
        ((1, OWN), jnp.int32),
        ((1, FEAT), jnp.int32),
        ((2, 2, OUT), wide),
        ((1, OUT), wide),
        ((2, OWN, OWN), low),
        ((1, FEAT), low),
        ((4, 8, SPAN), wide),
        ((8, SPAN), wide),
        ((2, 16, SPAN // 2), wide),
        ((16, SPAN // 2), wide),
        ((16, SPAN // 2), wide),
        ((16, SPAN // 2), wide),
        ((4, 16, SPAN // 2), wide),
        ((4, 8, SPAN // 2), wide),
        ((4, 1, SPAN // 2), wide),
    ]
    anywhere, near = pl.BlockSpec(memory_space=pl.ANY), pl.BlockSpec(memory_space=pltpu.VMEM)
    return pl.pallas_call(
        body,
        out_shape=[
            pltpu.VMEM((OWN, OUT), low),
            pltpu.VMEM((OWN, FEAT), low),
            pltpu.VMEM((ROWS, FEAT), wide),
            pltpu.VMEM((2, 2, 16, SPAN // 2), wide),
        ],
        in_specs=[anywhere] * 7,
        out_specs=[near] * 4,
        scratch_shapes=[pltpu.VMEM(shape, kind) for shape, kind in scratch]
        + [
            pltpu.SemaphoreType.DMA((len(set(LEAVES.values())),)),
            pltpu.SemaphoreType.DMA((len(ROWED), CUTS)),
            pltpu.SemaphoreType.DMA((sum(FEW.values()),)),
            pltpu.SemaphoreType.DMA((CUTS,)),
            pltpu.SemaphoreType.DMA((len(Local),)),
            pltpu.SemaphoreType.REGULAR,
            pltpu.SemaphoreType.REGULAR,
            pltpu.SemaphoreType.REGULAR,
        ],
        compiler_params=pltpu.CompilerParams(
            collective_id=0, has_side_effects=True, vmem_limit_bytes=GRANT
        ),
    )(*operands)


def closing(
    mixed_in, feat_in, grad_in, vec_in, momentum, weights,
    mixed, feat, grad, stitch, bias, new_momentum, new_weights,
    stitch_here, bias_here, weights_here, moved, result, sem,
):
    t = lax.axis_index("tower")
    started = []

    def start(count, src, dst):
        size = src.shape[0] // count
        for i in range(count):
            first = len(started)
            part = pl.ds(i * size, size)
            started.append(pltpu.make_async_copy(src.at[part], dst.at[part], sem.at[first]))
            started[-1].start()
        return started[-count:]

    loads = start(PARTS, weights, weights_here)
    start(PARTS, grad_in, grad)
    start(2, feat_in, feat)
    start(2, mixed_in, mixed)
    size = ROWS // PARTS
    for i in range(PARTS):
        rows = pl.ds(i * size, size)
        moved[rows] = momentum_rate * momentum[rows] + grad_in[rows]
        start(1, moved.at[rows], new_momentum.at[rows])
        loads[i].wait()
        result[rows] = weights_here[rows].astype(jnp.float32) - learn_rate * moved[rows]
        start(1, result.at[rows], new_weights.at[rows])
    for j in range(4):
        for h in range(2):
            part = slice((2 * j + h) * SPAN // 2, (2 * j + h + 1) * SPAN // 2)
            for s in range(2):
                for u in range(2):
                    stitch_here[s, u : u + 1, part] = vec_in[h, s, 4 * u + j : 4 * u + j + 1, :]
            bias_here[0:1, part] = vec_in[h, t, 8 + j : 9 + j, :]
    start(1, stitch_here, stitch)
    start(1, bias_here, bias)
    for copy in started[PARTS:]:
        copy.wait()


def close(mixed, feat, grad, vec, momentum, weights):
    anywhere, near = pl.BlockSpec(memory_space=pl.ANY), pl.BlockSpec(memory_space=pltpu.VMEM)
    small = [jax.ShapeDtypeStruct((2, 2, OUT), jnp.float32), jax.ShapeDtypeStruct((1, OUT), jnp.float32)]
    shapes = [*(jax.ShapeDtypeStruct(v.shape, v.dtype) for v in (mixed, feat, grad)), *small]
    shapes += [jax.ShapeDtypeStruct(grad.shape, grad.dtype)] * 2
    kept_near = [pltpu.with_memory_space_constraint(v, pltpu.VMEM) for v in (mixed, feat, grad, vec, momentum)]
    return pl.pallas_call(
        closing,
        out_shape=shapes,
        in_specs=[near] * 5 + [anywhere],
        out_specs=[anywhere] * 7,
        scratch_shapes=[pltpu.VMEM(v.shape, v.dtype) for v in (*small, weights, grad, grad)]
        + [pltpu.SemaphoreType.DMA((4 * PARTS + 6,))],
        compiler_params=pltpu.CompilerParams(vmem_limit_bytes=GRANT),
        cost_estimate=pl.CostEstimate(flops=0, bytes_accessed=14_000_000, transcendentals=0),
    )(*kept_near, weights)


def shards(features, group, pad_mask, weights, bias, stitch, momentum, cotangent):
    sums = towers(features[0], weights[0], cotangent[0], group[None], pad_mask[None], stitch, bias)
    mixed, feat_grad, weight_grad, stitch_grad, bias_grad, new_momentum, new_weights = close(
        *sums, momentum[0], weights[0]
    )
    return (
        mixed[None], feat_grad[None], weight_grad[None], bias_grad, stitch_grad, new_momentum[None], new_weights[None]
    )


def solution(mesh):
    placed = (
        P("tower", "blk", None),
        P("blk"),
        P(),
        P("tower", "blk", None),
        P("tower", None),
        P(),
        P("tower", "blk", None),
        P("tower", "blk", None),
    )
    return jax.shard_map(
        shards,
        mesh=mesh,
        in_specs=placed,
        out_specs=(
            P("tower", "blk", None),
            P("tower", "blk", None),
            P("tower", "blk", None),
            P("tower", None),
            P(),
            P("tower", "blk", None),
            P("tower", "blk", None),
        ),
        check_vma=False,
    )
```

```python
import enum

import jax
import jax.numpy as jnp
from jax import lax
from jax.experimental import pallas as pl
from jax.experimental.pallas import tpu as pltpu
from jax.sharding import PartitionSpec as P

momentum_rate = 0.9
learn_rate = 0.0001

FEAT = 9216
OUT = 4096
HALF = FEAT // 2
OWN = 128
ROWS = 64
SPAN = 1024
CUT = 512
CUTS = HALF // CUT
LATE = 1
EARLY = CUTS - LATE
AHEAD = 4
PARTS = 4
GRANT = 56 << 20
STRIP = 32
ORDER = (2, 1, 3, 0)


class Kind(enum.IntEnum):
    (
        x_sib, w_sib, w_x, own_yp, own_ym, own_zp, own_zm, pair_zp, pair_zm, sib_yp, sib_ym, fwd_yp, fwd_ym, fwd_zp, fwd_zm,
        opp_yp, opp_ym, opp_zp, opp_zm, sum_yp, sum_ym, sum_zp, sum_zm, g_x, d_sib, g_sib, late_opp_zp, late_opp_zm,
        late_sum_zp, late_sum_zm, keep, cot, hg, pre, pg, hid, tow, gb_x, v_c, v_x, v_z, v_y, b_y, v_t, v_b,
    ) = range(45)


class Local(enum.IntEnum):
    w, cot, small, small_1, small_2, small_3 = range(6)


ROWED = (
    (Kind.x_sib, Kind.w_sib, Kind.g_x),
    (Kind.w_x, Kind.sum_zp, Kind.sum_zm, Kind.late_sum_zp, Kind.late_sum_zm),
    (Kind.own_yp, Kind.sib_yp, Kind.opp_yp),
    (Kind.own_ym, Kind.sib_ym, Kind.opp_ym),
    (Kind.own_zp, Kind.pair_zp, Kind.opp_zp, Kind.late_opp_zp),
    (Kind.own_zm, Kind.pair_zm, Kind.opp_zm, Kind.late_opp_zm),
    (Kind.fwd_yp, Kind.fwd_ym, Kind.fwd_zp, Kind.fwd_zm, Kind.sum_yp, Kind.sum_ym),
)
ROW = {kind: row for row, kinds in enumerate(ROWED) for kind in kinds}
FEW = {
    Kind.keep: 1, Kind.cot: 1, Kind.hg: 4, Kind.pre: 4, Kind.pg: 4, Kind.hid: 1, Kind.tow: 1, Kind.gb_x: LATE, Kind.v_c: 1,
    Kind.v_x: 1, Kind.v_z: 1, Kind.v_y: 1, Kind.b_y: 1, Kind.v_t: 1, Kind.v_b: 1, Kind.d_sib: 1, Kind.g_sib: 1,
}
FIRST = {kind: sum(list(FEW.values())[:place]) for place, kind in enumerate(FEW)}
TOGETHER = (
    (Kind.own_yp, Kind.own_ym, Kind.sib_yp, Kind.sib_ym, Kind.fwd_yp, Kind.fwd_ym),
    (
        Kind.own_zp, Kind.own_zm, Kind.pair_zp, Kind.pair_zm, Kind.fwd_zp, Kind.fwd_zm, Kind.w_x, Kind.x_sib,
    ),
    (Kind.opp_yp, Kind.opp_ym),
    (Kind.sum_yp, Kind.sum_ym),
    (Kind.opp_zp, Kind.opp_zm),
    (Kind.sum_zp, Kind.sum_zm),
    (Kind.late_opp_zp, Kind.late_opp_zm),
    (Kind.late_sum_zp, Kind.late_sum_zm),
)
LEAVES = {kind: group for group, kinds in enumerate(TOGETHER) for kind in kinds}
for _kind in Kind:
    LEAVES.setdefault(_kind, len(set(LEAVES.values())))


def body(
    features, weights, cotangent, group_in, pad_in, stitch_in, bias_in,
    mixed_out, feat_out, grad_out, vec_t,
    xb, wb, pre, pg, pgt, cot, cot_in, hg_send, hg, hid, d_opp, g_opp, late,
    relay_yp, relay_ym, part_yp, part_ym, relay_zp, relay_zm, part_zp, part_zm,
    g_send, g_in, group, pad, stitch, bias, grouped, absent, coef, bias_sum, vec, vec_c, vec_x, vec_xin, vec_z, vec_y, bias_y,
    send_sem, row_sem, few_sem, load_sem, local_sem, room_sem, chips_sem, all_sem,
):
    blk, t = lax.axis_index("blk"), lax.axis_index("tower")
    y, x, z, c = blk // 16, (blk // 8) % 2, (blk // 2) % 4, blk % 2
    other = 1 - c

    def place(y, x, z, c):
        return ((y * 2 + x) * 4 + z) * 2 + c

    yp, yo, ym = (y + 1) % 4, (y + 2) % 4, (y + 3) % 4
    zp, zo, zm = (z + 1) % 4, (z + 2) % 4, (z + 3) % 4
    to_yp, to_yo, to_ym = ((place(v, x, z, c), t) for v in (yp, yo, ym))
    to_zp, to_zo, to_zm = ((place(y, x, v, c), t) for v in (zp, zo, zm))
    to_x = (place(y, 1 - x, z, c), t)
    to_sib = (place(y, x, z, other), t)
    to_tower = (blk, 1 - t)
    to_y = (None, to_yp, to_yo, to_ym)
    to_z = (None, to_zp, to_zo, to_zm)

    def remote(kind, k, src, dst, device):
        if kind in ROW:
            landed = row_sem.at[ROW[kind], k]
        else:
            landed = few_sem.at[FIRST[kind] + (k if FEW[kind] > 1 else 0)]
        return pltpu.make_async_remote_copy(
            src_ref=src, dst_ref=dst, send_sem=send_sem.at[LEAVES[kind]], recv_sem=landed,
            device_id=device, device_id_type=pl.DeviceIdType.MESH,
        )

    def arrived(kind, k, dst):
        remote(kind, k, dst, dst, to_sib).wait_recv()

    def sent(kind, src):
        remote(kind, 0, src, src, to_sib).wait_send()

    def local(kind, src, dst):
        return pltpu.make_async_copy(src, dst, local_sem.at[kind])

    def columns(side, k):
        return pl.ds(pl.multiple_of(side * HALF + k * CUT, CUT), CUT)

    def loop(count, step):
        lax.fori_loop(0, count, lambda k, carry: (step(k), carry)[1], 0)

    hid_other = hg
    late_out = hg_send.at[:, :, :CUT]
    hid_send = cot_in
    staged = g_send
    TOP, LOW = pl.ds(0, OWN // 2), pl.ds(OWN // 2, OWN // 2)
    own_rows = pl.ds(pl.multiple_of(c * ROWS, ROWS), ROWS)
    sib_rows = pl.ds(pl.multiple_of(other * ROWS, ROWS), ROWS)

    def load_x(k):
        return pltpu.make_async_copy(features.at[:, columns(c, k)], xb.at[k, y, c], load_sem.at[k])

    def load_other(k):
        return pltpu.make_async_copy(features.at[:, columns(other, k)], staged.at[k], load_sem.at[k])

    def load_w(k):
        return local(Local.w, weights.at[:, columns(c, k)], wb.at[k, x, z, own_rows])

    def start_loads(k):
        load_x(k).start()
        load_other(k).start()
        load_w(k).start()

    barrier = pltpu.get_barrier_semaphore()
    along_y, across = (to_yp, to_yo, to_ym), (to_zp, to_zo, to_zm, to_x, to_tower)

    def signal(sem, device):
        pl.semaphore_signal(sem, inc=1, device_id=device, device_id_type=pl.DeviceIdType.MESH)

    def greet(sem):
        for core, devices in enumerate((along_y, across)):

            @pl.when(c == core)
            def _(devices=devices):
                for device in devices:
                    signal(sem, device)

    greeted = len(along_y) + c * (len(across) - len(along_y))
    signal(barrier, to_sib)
    greet(barrier)

    small = [
        local(Local.small + i, src, dst)
        for i, (src, dst) in enumerate(((group_in, group), (pad_in, pad), (stitch_in, stitch), (bias_in, bias)))
    ]
    for copy in small[:2]:
        copy.start()
    loop(CUTS, start_loads)
    for copy in small[2:]:
        copy.start()
    for j in range(4):
        local(Local.cot, cotangent.at[:, pl.ds(j * SPAN, SPAN)], cot.at[j]).start()

    for copy in small[:2]:
        copy.wait()
    grouped[c] = jnp.broadcast_to(group[...].astype(jnp.float32), (OWN, OWN)).T.astype(jnp.bfloat16)
    absent[...] = 1.0 - pad[...].astype(jnp.float32).astype(jnp.bfloat16)

    def kept(value, core, side, k):
        rows = jnp.concatenate([grouped[core]] * (CUT // OWN), 1)
        return value * (1.0 - rows * absent[0:1, columns(side, k)])

    def masked(k):
        pltpu.make_async_copy(xb.at[k, y], xb.at[k, y], load_sem.at[k]).wait()
        staged[k] = kept(staged[k], c, other, k)
        xb[k, y, c] = kept(xb[k, y, c], c, c, k)

    masked(0)
    pl.semaphore_wait(barrier, greeted + 1)
    greet(chips_sem)

    def x_sib(k):
        return remote(Kind.x_sib, k, staged.at[k], xb.at[k, y, c], to_sib)

    def w_sib(k):
        return remote(Kind.w_sib, k, weights.at[:, columns(other, k)], wb.at[k, x, z, own_rows], to_sib)

    def own_y(k):
        remote(Kind.own_yp, k, xb.at[k, y, c], xb.at[k, y, c], to_yp).start()
        remote(Kind.own_ym, k, xb.at[k, y, c], xb.at[k, y, c], to_ym).start()

    def to_sibling(k):
        x_sib(k).start()
        w_sib(k).start()

    def own_out(k):
        arrived(Kind.x_sib, k, xb.at[k, y, :, : (OWN + ROWS) // 2])
        remote(Kind.sib_yp, k, xb.at[k, y, other], xb.at[k, y, other], to_yp).start()
        remote(Kind.sib_ym, k, xb.at[k, y, other], xb.at[k, y, other], to_ym).start()
        remote(Kind.w_x, k, wb.at[k, x, z], wb.at[k, x, z], to_x).start()
        remote(Kind.own_zp, k, wb.at[k, x, z], wb.at[k, x, z], to_zp).start()
        remote(Kind.own_zm, k, wb.at[k, x, z], wb.at[k, x, z], to_zm).start()

    every_w = wb.at[:CUTS, x, z]

    def ahead(k):
        pl.when(k > 0)(lambda: masked(k))
        pl.when(c == 0)(lambda: own_y(k))
        to_sibling(k)

    def first(k):
        @pl.when(k < CUTS)
        def _():
            masked(k)
            own_y(k)
            to_sibling(k)

        own_out(k - AHEAD)

    loop(AHEAD, ahead)
    pl.semaphore_wait(chips_sem, greeted)
    signal(all_sem, to_sib)
    pl.semaphore_wait(all_sem, 1)
    pl.when(c == 1)(lambda: loop(AHEAD, own_y))
    every = wb.at[:CUTS, x, z, own_rows]
    local(Local.w, every, every).wait()
    loop(CUTS, lambda k: first(k + AHEAD))
    remote(Kind.keep, 0, grouped.at[c], grouped.at[c], to_sib).start()
    for j in range(4):
        remote(Kind.cot, j, cotangent.at[:, pl.ds(j * SPAN, SPAN)], cot_in.at[j], to_tower).start()

    def pair_out(k):
        arrived(Kind.w_x, k, wb.at[k, 1 - x, z])
        remote(Kind.pair_zp, k, wb.at[k, 1 - x, z], wb.at[k, 1 - x, z], to_zp).start()
        remote(Kind.pair_zm, k, wb.at[k, 1 - x, z], wb.at[k, 1 - x, z], to_zm).start()

    loop(CUTS, pair_out)

    def forward(k):
        arrived(Kind.own_yp, k, xb.at[k, ym])
        arrived(Kind.own_ym, k, xb.at[k, yp])
        remote(Kind.fwd_yp, k, xb.at[k, ym, 0], xb.at[k, ym, 0], to_yp).start()
        remote(Kind.fwd_ym, k, xb.at[k, yp, 1], xb.at[k, yp, 1], to_ym).start()
        arrived(Kind.own_zp, k, wb.at[k, :, zm])
        arrived(Kind.own_zm, k, wb.at[k, :, zp])
        remote(Kind.fwd_zp, k, wb.at[k, x, zm], wb.at[k, x, zm], to_zp).start()
        remote(Kind.fwd_zm, k, wb.at[k, 1 - x, zp], wb.at[k, 1 - x, zp], to_zm).start()

    loop(CUTS, forward)

    for copy in small[2:]:
        copy.wait()
    for j in range(4):
        part = slice(j * SPAN, (j + 1) * SPAN)
        coef[j, 0:1, :] = jnp.where(t == 0, stitch[0, 0:1, part], stitch[1, 1:2, part])
        coef[j, 1:2, :] = jnp.where(t == 0, stitch[1, 0:1, part], stitch[0, 1:2, part])
        coef[j, 2:3, :] = jnp.where(t == 0, stitch[0, 1:2, part], stitch[1, 0:1, part])
        coef[j, 3:4, :] = bias[0:1, part]
    local(Local.cot, cot, cot).wait()
    arrived(Kind.cot, 0, cot_in)
    for d in ORDER:
        j = (y + d) % 4

        def combine(i, d=d, j=j):
            rows = pl.ds(pl.multiple_of(i * STRIP, STRIP), STRIP)
            value = (
                coef[j, 0:1, :] * cot[j, rows, :].astype(jnp.float32)
                + coef[j, 1:2, :] * cot_in[j, rows, :].astype(jnp.float32)
            ).astype(jnp.bfloat16)
            if d == 0:
                hg[y, rows, :] = value
            else:
                hg_send[j, rows, :] = value

        loop(OWN // STRIP, combine)
        if d:
            remote(Kind.hg, d, hg_send.at[j], hg.at[y], to_y[d]).start()

    def pre_in(i):
        return grad_out.at[:, pl.ds(pl.multiple_of(i * SPAN, SPAN), SPAN)]

    def gathered(k):
        arrived(Kind.fwd_yp, k, xb.at[k, 0:2])

    def add_block(k, b):
        pre[b] += lax.dot_general(
            xb[k, b].reshape(2 * OWN, CUT), wb[k].reshape(SPAN, CUT),
            (((1,), (1,)), ((), ())), preferred_element_type=jnp.float32,
        ).reshape(2, OWN, SPAN)

    def add_product(k):
        gathered(k)
        loop(4, lambda b: add_block(k, b))

    def clear(b):
        pre[b] = jnp.zeros((2, OWN, SPAN), jnp.float32)

    loop(4, clear)
    loop(CUTS - 1, add_product)
    gathered(CUTS - 1)

    for d in ORDER:
        b = (y + d) % 4
        add_block(CUTS - 1, b)
        for h in range(2):
            part = pl.ds(h * ROWS, ROWS)
            remote(Kind.pre, d, pre.at[b, other, part], pre_in(2 * d + h), to_sib).start()
    bias_sum[...] = jnp.zeros_like(bias_sum)

    def activate(d):
        b = (y + d) % 4
        arrived(Kind.pre, d, pre.at[b, other])
        if d:
            arrived(Kind.hg, 4 - d, hg.at[b])

        def act(i):
            rows = pl.ds(pl.multiple_of(i * STRIP, STRIP), STRIP)
            per = ROWS // STRIP
            rows_in = pl.ds(pl.multiple_of((i % per) * STRIP, STRIP), STRIP)
            value = pre[b, c, rows, :] + pre_in(2 * d + i // per)[rows_in, :] + coef[y, 3:4, :]
            gate = jax.nn.sigmoid(value)
            hidden = (value * gate).astype(jnp.bfloat16)
            grad = (hg[b, rows, :].astype(jnp.float32) * gate * (1.0 + value * (1.0 - gate))).astype(jnp.bfloat16)
            pg[b, c, rows, :] = grad
            if d == 0:
                hid[y, rows, :] = hidden
            else:
                hid_send[b, rows, :] = hidden
            bias_sum[...] += jnp.sum(grad.astype(jnp.float32).reshape(STRIP // 8, 8, SPAN), 0)

        loop(OWN // STRIP, act)
        remote(Kind.pg, d, pg.at[b, c], pg.at[b, c], to_sib).start()
        if d:
            remote(Kind.hid, d, hid_send.at[b], hid.at[y], to_y[d]).start()

    def product_d(k, b):
        product = jnp.dot(
            pg[b].reshape(2 * OWN, SPAN), wb[k].reshape(SPAN, CUT), preferred_element_type=jnp.float32
        )
        return product.astype(jnp.bfloat16).reshape(2, OWN, CUT)

    def product_late(k, side):
        return jnp.dot(
            pgt[side].reshape(4 * OWN, SPAN), xb[k].reshape(SPAN, CUT), preferred_element_type=jnp.float32
        ).reshape(4, OWN, CUT)

    def product_g(k, v):
        product = jnp.dot(
            pgt[:, v].reshape(2 * OWN, SPAN), xb[k].reshape(SPAN, CUT), preferred_element_type=jnp.float32
        )
        return product.astype(jnp.bfloat16).reshape(2, OWN, CUT)

    def late_away(i):
        late_out[...] = product_late(EARLY + i, 1 - x).astype(jnp.bfloat16)
        remote(Kind.gb_x, i, late_out, late.at[i], to_x).start()

    def opposite_d(k):
        d_opp[k] = product_d(k, yo)
        remote(Kind.opp_yp, k, d_opp.at[k, 0], relay_yp.at[k], to_yp).start()
        remote(Kind.opp_ym, k, d_opp.at[k, 1], relay_ym.at[k], to_ym).start()

    def opposite_g(k):
        g_opp[k] = product_g(k, zo)
        remote(Kind.opp_zp, k, g_opp.at[k, 0], relay_zp.at[k], to_zp).start()
        remote(Kind.opp_zm, k, g_opp.at[k, 1], relay_zm.at[k], to_zm).start()

    for d in ORDER:
        activate(d)
    pl.semaphore_signal(room_sem, inc=1, device_id=to_tower, device_id_type=pl.DeviceIdType.MESH)
    for d in ORDER:
        arrived(Kind.pg, d, pg.at[(y + d) % 4, other])
        if d == 2:
            loop(CUTS, opposite_d)

    wide = 256
    eye = (
        lax.broadcasted_iota(jnp.int32, (wide, wide), 0) == lax.broadcasted_iota(jnp.int32, (wide, wide), 1)
    ).astype(jnp.bfloat16)
    for o in range(SPAN // wide):
        flipped = lax.dot_general(
            eye, pg[:, :, :, o * wide : (o + 1) * wide].reshape(SPAN, wide),
            (((1,), (1,)), ((), ())), preferred_element_type=jnp.float32,
        )
        pgt[o // 2, (o % 2) * 2 : (o % 2) * 2 + 2] = flipped.astype(jnp.bfloat16).reshape(2, OWN, SPAN)
    loop(EARLY, opposite_g)
    arrived(Kind.hid, 0, hid.at[:3])
    pl.semaphore_wait(room_sem, 1)
    for j in range(4):
        remote(Kind.tow, j, hid.at[j], hid_other.at[j], to_tower).start()
    sent(Kind.hg, hg_send.at[:3])
    loop(LATE, late_away)

    sent(Kind.w_sib, wb.at[:CUTS, x, z, own_rows])
    sent(Kind.own_yp, xb.at[:, 0:3])
    sent(Kind.own_zp, xb)
    sent(Kind.pre, pre.at[:, other])
    arrived(Kind.keep, 0, grouped.at[other])

    def slot(k):
        return (k + CUTS) % (CUTS + 1)

    def g_keep(k):
        part = pl.ds(pl.multiple_of((k % (SPAN // CUT)) * CUT, CUT), CUT)
        block = k // (SPAN // CUT)
        return pre.at[block // 2, block % 2, :, part]

    def products(k):
        s = slot(k)

        def block_g(i):
            v = (zo + 1 + i) % 4
            wb[s, :, v] = product_g(k, v)

        def block_d(i):
            b = (yo + 1 + i) % 4
            xb[k, b] = product_d(k, b)

        pl.when(k < EARLY)(lambda: loop(3, block_g))
        loop(3, block_d)

    def late_in(i):
        k = EARLY + i
        arrived(Kind.gb_x, i, late.at[i])

        late[i] = (product_late(k, x) + late[i].astype(jnp.float32)).astype(jnp.bfloat16)
        remote(Kind.late_opp_zp, k, late.at[i, zo, TOP], relay_zp.at[k, TOP], to_zp).start()
        remote(Kind.late_opp_zm, k, late.at[i, zo, LOW], relay_zm.at[k, TOP], to_zm).start()

    def wide_sum(*terms):
        total = terms[0].astype(jnp.float32)
        for term in terms[1:]:
            total += term.astype(jnp.float32)
        return total

    def relays(k):
        arrived(Kind.opp_yp, k, relay_yp.at[k])
        xb[k, yp, 0] = wide_sum(xb[k, yp, 0], relay_yp[k]).astype(jnp.bfloat16)
        remote(Kind.sum_yp, k, xb.at[k, yp], part_yp.at[k], to_yp).start()
        arrived(Kind.opp_ym, k, relay_ym.at[k])
        xb[k, ym, 1] = wide_sum(xb[k, ym, 1], relay_ym[k]).astype(jnp.bfloat16)
        remote(Kind.sum_ym, k, xb.at[k, ym], part_ym.at[k], to_ym).start()
        pl.when(k < EARLY)(lambda: relays_z(k))
        pl.when(k >= EARLY)(lambda: relays_late(k))

    def relays_z(k):
        s = slot(k)
        arrived(Kind.opp_zp, k, relay_zp.at[k])
        wb[s, 0, zp] = wide_sum(wb[s, 0, zp], relay_zp[k]).astype(jnp.bfloat16)
        remote(Kind.sum_zp, k, wb.at[s, :, zp], part_zp.at[k], to_zp).start()
        arrived(Kind.opp_zm, k, relay_zm.at[k])
        wb[s, 1, zm] = wide_sum(wb[s, 1, zm], relay_zm[k]).astype(jnp.bfloat16)
        remote(Kind.sum_zm, k, wb.at[s, :, zm], part_zm.at[k], to_zm).start()

    def relays_late(k):
        i = k - EARLY
        arrived(Kind.late_opp_zp, k, relay_zp.at[k, TOP])
        late[i, zp, TOP] = wide_sum(late[i, zp, TOP], relay_zp[k, TOP]).astype(jnp.bfloat16)
        remote(Kind.late_sum_zp, k, late.at[i, zp], part_zp.at[k, 0], to_zp).start()
        arrived(Kind.late_opp_zm, k, relay_zm.at[k, TOP])
        late[i, zm, LOW] = wide_sum(late[i, zm, LOW], relay_zm[k, TOP]).astype(jnp.bfloat16)
        remote(Kind.late_sum_zm, k, late.at[i, zm], part_zm.at[k, 0], to_zm).start()

    def grad_done(k):
        remote(Kind.g_sib, 0, g_keep(k).at[sib_rows], grad_out.at[:, columns(c, k)], to_sib).start()
        grad_out[:, columns(c, k)] = g_keep(k)[own_rows, :]

    def sums_z(k):
        s = slot(k)
        arrived(Kind.sum_zp, k, xb.at[k, 0:2])
        g_send[k] = wide_sum(wb[s, 1 - x, z], part_zp[k, 1 - x], part_zm[k, 1 - x]).astype(jnp.bfloat16)
        remote(Kind.g_x, k, g_send.at[k], g_in.at[k], to_x).start()
        g_keep(k)[...] = wide_sum(wb[s, x, z], part_zp[k, x], part_zm[k, x])

    def sums_late(k):
        arrived(Kind.late_sum_zp, k, xb.at[k, 0])
        g_keep(k)[...] = wide_sum(late[k - EARLY, z], part_zp[k, 0], part_zm[k, 0])
        grad_done(k)

    def sums(k):
        pl.when(k < EARLY)(lambda: sums_z(k))
        pl.when(k >= EARLY)(lambda: sums_late(k))
        arrived(Kind.sum_yp, k, xb.at[k, 0:2])
        theirs = wide_sum(xb[k, y, other], part_yp[k, other], part_ym[k, other])
        xb[k, y, other] = kept(theirs.astype(jnp.bfloat16), other, c, k)
        remote(Kind.d_sib, 0, xb.at[k, y, other], feat_out.at[:, columns(c, k)], to_sib).start()
        ours = wide_sum(xb[k, y, c], part_yp[k, c], part_ym[k, c])
        feat_out[:, columns(c, k)] = kept(ours.astype(jnp.bfloat16), c, c, k)

    def ends(k):
        arrived(Kind.g_x, k, g_in.at[k])
        g_keep(k)[...] += g_in[k].astype(jnp.float32)
        grad_done(k)

    def mixing():
        arrived(Kind.tow, 0, hid_other)
        for j in range(4):

            def strip(i, sums, j=j):
                rows = pl.ds(pl.multiple_of(i * STRIP, STRIP), STRIP)
                here = hid[j, rows, :].astype(jnp.float32)
                there = hid_other[j, rows, :].astype(jnp.float32)
                mixed_out[rows, j * SPAN : (j + 1) * SPAN] = (coef[j, 0:1, :] * here + coef[j, 2:3, :] * there).astype(jnp.bfloat16)
                up = cot[j, rows, :].astype(jnp.float32)
                return (
                    sums[0] + jnp.sum((up * here).reshape(STRIP // 8, 8, SPAN), 0),
                    sums[1] + jnp.sum((up * there).reshape(STRIP // 8, 8, SPAN), 0),
                )

            zero = jnp.zeros((8, SPAN), jnp.float32)
            here, there = lax.fori_loop(0, OWN // STRIP, strip, (zero, zero))
            here, there = jnp.sum(here, 0, keepdims=True), jnp.sum(there, 0, keepdims=True)
            for h in range(2):
                part = slice(h * SPAN // 2, (h + 1) * SPAN // 2)
                vec[h, j : j + 1, :] = jnp.where(t == 0, here[:, part], there[:, part])
                vec[h, 4 + j : 5 + j, :] = jnp.where(t == 0, there[:, part], here[:, part])
        bias = jnp.sum(bias_sum[...], 0, keepdims=True)
        bias = jnp.where(lax.broadcasted_iota(jnp.int32, (8, SPAN), 0) == y, bias, 0.0)
        for h in range(2):
            vec[h, 8:16, :] = bias[:, h * SPAN // 2 : (h + 1) * SPAN // 2]
        remote(Kind.v_c, 0, vec.at[other], vec_c, to_sib).start()

    def over_cores():
        arrived(Kind.v_c, 0, vec_c)
        vec_x[...] = vec[c] + vec_c[...]
        remote(Kind.v_x, 0, vec_x, vec_xin, to_x).start()

    def over_x():
        arrived(Kind.v_x, 0, vec_xin)
        vec_z[z] = vec_x[...] + vec_xin[...]
        for d in range(1, 4):
            remote(Kind.v_z, d, vec_z.at[z], vec_z.at[z], to_z[d]).start()

    def over_z():
        arrived(Kind.v_z, 0, vec_z.at[:3])
        total = (vec_z[0] + vec_z[1]) + (vec_z[2] + vec_z[3])
        vec_y[y] = total[:8]
        bias_y[y] = jnp.sum(total[8:], 0, keepdims=True)
        for d in range(1, 4):
            remote(Kind.v_y, d, vec_y.at[y], vec_y.at[y], to_y[d]).start()
            remote(Kind.b_y, d, bias_y.at[y], bias_y.at[y], to_y[d]).start()

    def over_y():
        arrived(Kind.v_y, 0, vec_y.at[:3])
        arrived(Kind.b_y, 0, bias_y.at[:3])
        vec_t[c, t, 0:8] = (vec_y[0] + vec_y[1]) + (vec_y[2] + vec_y[3])
        for j in range(4):
            vec_t[c, t, 8 + j : 9 + j] = bias_y[j]
        remote(Kind.v_t, 0, vec_t.at[c, t], vec_t.at[c, t], to_tower).start()

    def over_towers():
        arrived(Kind.v_t, 0, vec_t.at[c, 1 - t])
        remote(Kind.v_b, 0, vec_t.at[c], vec_t.at[c], to_sib).start()

    between = {
        2: (mixing, over_cores), 3: (over_x,), 4: (lambda: late_in(0),), 5: (over_z,), 7: (over_y,), 9: (over_towers,),
    }

    def step(s):
        pl.when(s < CUTS)(lambda: products(s))
        pl.when(s < CUTS)(lambda: relays(s))
        pl.when((s >= 2) & (s < CUTS + 2))(lambda: sums(s - 2))
        pl.when((s >= 3) & (s < EARLY + 3))(lambda: ends(s - 3))
        for at, tasks in between.items():

            @pl.when(s == at)
            def _(tasks=tasks):
                for task in tasks:
                    task()

    loop(CUTS + 2, step)

    arrived(Kind.v_b, 0, vec_t.at[other])

    def half(ref, side):
        return ref.at[:, pl.ds(pl.multiple_of(side * HALF, HALF), HALF)]

    arrived(Kind.d_sib, 0, half(feat_out, other))
    arrived(Kind.g_sib, 0, half(grad_out, other))
    sent(Kind.opp_yp, d_opp)
    sent(Kind.sum_yp, xb.at[:, 0:2])
    sent(Kind.opp_zp, g_opp)
    sent(Kind.sum_zp, xb.at[:EARLY, 0:2])
    sent(Kind.late_opp_zp, late.at[:, 0])
    sent(Kind.late_sum_zp, late.at[:, 0:2])
    sent(Kind.g_x, g_send.at[:EARLY])
    sent(Kind.gb_x, late)
    sent(Kind.d_sib, xb.at[:, y, 0])
    sent(Kind.g_sib, half(grad_out, other))
    sent(Kind.cot, cot)
    sent(Kind.pg, pg.at[:, 0])
    sent(Kind.tow, hid)
    sent(Kind.hid, hid.at[:3])
    sent(Kind.v_z, vec_z.at[:3])
    sent(Kind.v_y, vec_y.at[:3])
    sent(Kind.b_y, bias_y.at[:3])
    sent(Kind.v_c, vec_c)
    sent(Kind.v_x, vec_x)
    sent(Kind.v_t, vec_c)
    sent(Kind.v_b, vec_t.at[c])
    sent(Kind.keep, grouped.at[c])


def towers(*operands):
    low, wide = jnp.bfloat16, jnp.float32
    scratch = [
        ((CUTS, 4, 2, OWN, CUT), low),
        ((CUTS + 1, 2, 4, OWN, CUT), low),
        ((4, 2, OWN, SPAN), wide),
        ((4, 2, OWN, SPAN), low),
        ((2, 4, OWN, SPAN), low),
        ((4, OWN, SPAN), low),
        ((4, OWN, SPAN), low),
        ((4, OWN, SPAN), low),
        ((4, OWN, SPAN), low),
        ((4, OWN, SPAN), low),
        ((CUTS, 2, OWN, CUT), low),
        ((EARLY, 2, OWN, CUT), low),
        ((LATE, 4, OWN, CUT), low),
        ((CUTS, OWN, CUT), low),
        ((CUTS, OWN, CUT), low),
        ((CUTS, 2, OWN, CUT), low),
        ((CUTS, 2, OWN, CUT), low),
        ((CUTS, OWN, CUT), low),
        ((CUTS, OWN, CUT), low),
        ((CUTS, 2, OWN, CUT), low),
        ((CUTS, 2, OWN, CUT), low),
        ((CUTS, OWN, CUT), low),
        ((CUTS, OWN, CUT), low),
        ((1, OWN), jnp.int32),
        ((1, FEAT), jnp.int32),
        ((2, 2, OUT), wide),
        ((1, OUT), wide),
        ((2, OWN, OWN), low),
        ((1, FEAT), low),
        ((4, 8, SPAN), wide),
        ((8, SPAN), wide),
        ((2, 16, SPAN // 2), wide),
        ((16, SPAN // 2), wide),
        ((16, SPAN // 2), wide),
        ((16, SPAN // 2), wide),
        ((4, 16, SPAN // 2), wide),
        ((4, 8, SPAN // 2), wide),
        ((4, 1, SPAN // 2), wide),
    ]
    anywhere, near = pl.BlockSpec(memory_space=pl.ANY), pl.BlockSpec(memory_space=pltpu.VMEM)
    return pl.pallas_call(
        body,
        out_shape=[
            pltpu.VMEM((OWN, OUT), low),
            pltpu.VMEM((OWN, FEAT), low),
            pltpu.VMEM((ROWS, FEAT), wide),
            pltpu.VMEM((2, 2, 16, SPAN // 2), wide),
        ],
        in_specs=[anywhere] * 7,
        out_specs=[near] * 4,
        scratch_shapes=[pltpu.VMEM(shape, kind) for shape, kind in scratch]
        + [
            pltpu.SemaphoreType.DMA((len(set(LEAVES.values())),)),
            pltpu.SemaphoreType.DMA((len(ROWED), CUTS)),
            pltpu.SemaphoreType.DMA((sum(FEW.values()),)),
            pltpu.SemaphoreType.DMA((CUTS,)),
            pltpu.SemaphoreType.DMA((len(Local),)),
            pltpu.SemaphoreType.REGULAR,
            pltpu.SemaphoreType.REGULAR,
            pltpu.SemaphoreType.REGULAR,
        ],
        compiler_params=pltpu.CompilerParams(
            collective_id=0, has_side_effects=True, vmem_limit_bytes=GRANT
        ),
    )(*operands)


def closing(
    mixed_in, feat_in, grad_in, vec_in, momentum, weights,
    mixed, feat, grad, stitch, bias, new_momentum, new_weights,
    stitch_here, bias_here, weights_here, moved, result, sem,
):
    t = lax.axis_index("tower")
    started = []

    def start(count, src, dst):
        size = src.shape[0] // count
        for i in range(count):
            first = len(started)
            part = pl.ds(i * size, size)
            started.append(pltpu.make_async_copy(src.at[part], dst.at[part], sem.at[first]))
            started[-1].start()
        return started[-count:]

    loads = start(PARTS, weights, weights_here)
    start(PARTS, grad_in, grad)
    start(2, feat_in, feat)
    start(2, mixed_in, mixed)
    size = ROWS // PARTS
    for i in range(PARTS):
        rows = pl.ds(i * size, size)
        moved[rows] = momentum_rate * momentum[rows] + grad_in[rows]
        start(1, moved.at[rows], new_momentum.at[rows])
        loads[i].wait()
        result[rows] = weights_here[rows].astype(jnp.float32) - learn_rate * moved[rows]
        start(1, result.at[rows], new_weights.at[rows])
    for j in range(4):
        for h in range(2):
            part = slice((2 * j + h) * SPAN // 2, (2 * j + h + 1) * SPAN // 2)
            for s in range(2):
                for u in range(2):
                    stitch_here[s, u : u + 1, part] = vec_in[h, s, 4 * u + j : 4 * u + j + 1, :]
            bias_here[0:1, part] = vec_in[h, t, 8 + j : 9 + j, :]
    start(1, stitch_here, stitch)
    start(1, bias_here, bias)
    for copy in started[PARTS:]:
        copy.wait()


def close(mixed, feat, grad, vec, momentum, weights):
    anywhere, near = pl.BlockSpec(memory_space=pl.ANY), pl.BlockSpec(memory_space=pltpu.VMEM)
    small = [jax.ShapeDtypeStruct((2, 2, OUT), jnp.float32), jax.ShapeDtypeStruct((1, OUT), jnp.float32)]
    shapes = [*(jax.ShapeDtypeStruct(v.shape, v.dtype) for v in (mixed, feat, grad)), *small]
    shapes += [jax.ShapeDtypeStruct(grad.shape, grad.dtype)] * 2
    kept_near = [pltpu.with_memory_space_constraint(v, pltpu.VMEM) for v in (mixed, feat, grad, vec, momentum)]
    return pl.pallas_call(
        closing,
        out_shape=shapes,
        in_specs=[near] * 5 + [anywhere],
        out_specs=[anywhere] * 7,
        scratch_shapes=[pltpu.VMEM(v.shape, v.dtype) for v in (*small, weights, grad, grad)]
        + [pltpu.SemaphoreType.DMA((4 * PARTS + 6,))],
        compiler_params=pltpu.CompilerParams(vmem_limit_bytes=GRANT),
        cost_estimate=pl.CostEstimate(flops=0, bytes_accessed=14_000_000, transcendentals=0),
    )(*kept_near, weights)


def shards(features, group, pad_mask, weights, bias, stitch, momentum, cotangent):
    sums = towers(features[0], weights[0], cotangent[0], group[None], pad_mask[None], stitch, bias)
    mixed, feat_grad, weight_grad, stitch_grad, bias_grad, new_momentum, new_weights = close(
        *sums, momentum[0], weights[0]
    )
    return (
        mixed[None], feat_grad[None], weight_grad[None], bias_grad, stitch_grad, new_momentum[None], new_weights[None]
    )


def solution(mesh):
    placed = (
        P("tower", "blk", None),
        P("blk"),
        P(),
        P("tower", "blk", None),
        P("tower", None),
        P(),
        P("tower", "blk", None),
        P("tower", "blk", None),
    )
    return jax.shard_map(
        shards,
        mesh=mesh,
        in_specs=placed,
        out_specs=(
            P("tower", "blk", None),
            P("tower", "blk", None),
            P("tower", "blk", None),
            P("tower", None),
            P(),
            P("tower", "blk", None),
            P("tower", "blk", None),
        ),
        check_vma=False,
    )
```
